32 devices in a mesh: gx: 2 (over x), gy: 8 (over z, y), vert: 2 (over core).
Axes of the slice: x: 2, y: 2, z: 4, core: 2. Of those that a mesh axis runs over, the one named last changes fastest.
Arguments:
- distribution: float32 [32, 128, 4096], P('gx', 'gy', 'vert'), may hold values from -6 to 6
- density: float32 [32, 128], P('gx', 'gy'), may hold values from 0.3 to 3
- cell_type: int32 [32, 128], P('gx', 'gy'), may hold values from 0 to 2, as said below
- inflow: float32 [4096], P('vert'), may hold values from -6 to 6
Outputs:
- evolved: float32 [32, 128, 4096], P('gx', 'gy', 'vert')
The draws below stay inside these ranges and needn't reach their ends.
Inputs may be any that keep to these rules, and one draw needn't show every extreme that they name: `cell_type`: 0 marks a gas cell, 1 a wall cell, 2 an inflow cell; most cells are gas cells.
All inputs are finite; a program needn't handle non-finite values.
Results may differ from the reference program's by a relative error of at most 0.0003.
Values sent between devices are 32-bit elements; how exact they have to be, the bound alone decides.
No kernel may reach another device: no remote copies, remote signals or barrier semaphores. Data moves between devices by JAX's collectives and lax.ppermute only.
A program may use at most 128 MiB of HBM per device.

```python
import math
import jax
import jax.numpy as jnp
from jax import lax

NVX = 64
STEPS = 2
NV = 4096
NX = 32
NY = 128
N_VERT = 2


def draw_cell_type(key, part):
    roll = jax.random.randint(jax.random.fold_in(key, 7), (NX, NY), 0, 10)
    return jnp.where(roll == 0, 1, jnp.where(roll == 1, 2, 0)).astype(jnp.int32)


def level_of(own_key, shape, split, smallest, top_value):
    def one(dim, blocks):
        steps = jax.random.uniform(jax.random.fold_in(jax.random.fold_in(own_key, 6), dim), (blocks,), jnp.float32, smallest / len(split), top_value / len(split))
        return jnp.repeat(jnp.exp(steps), shape[dim] // blocks).reshape((-1,) + (1,) * (len(shape) - dim - 1))

    loudness = one(*split[0])
    for cut in split[1:]:
        loudness = loudness * one(*cut)
    return loudness


def scatter_about(stream_key, shape, width, reach, shards=(), kind=jnp.bfloat16):
    loudness = level_of(stream_key, shape, shards, -0.22, 0.18) if shards else 1.0
    result = jax.random.normal(stream_key, shape, jnp.float32) * width * loudness
    return jnp.minimum(jnp.maximum(result, -reach), reach).astype(kind)


def setup_inputs(seed: int = 0) -> dict:
    arg_keys = jax.random.split(jax.random.key(seed), 5)
    return {
        "distribution": scatter_about(arg_keys[0], (NX, NY, NV), 1.0, 6.0, ((0, 2), (1, 8), (2, 2)), jnp.float32),
        "density": jnp.clip(jnp.exp(math.log(3.0) - 2.3025851 * jax.random.uniform(arg_keys[1], (NX, NY), jnp.float32) ** level_of(arg_keys[1], (NX, NY), ((0, 2), (1, 8)), -0.2, 0.2)), 0.3, 3.0),
        "cell_type": draw_cell_type(jax.random.fold_in(arg_keys[4], 71), 0),
        "inflow": scatter_about(arg_keys[3], (NV,), 1.0, 6.0, ((0, 2),), jnp.float32),
    }


vel_max = 4.0
time_step = 0.1
grad_scale = 2.5
collision_rate = 0.2

def velocity_parts(index):
    spacing = 2.0 * vel_max / NVX
    row_portion = (index // NVX).astype(jnp.float32)
    col_part = (index % NVX).astype(jnp.float32)
    vel_x = (row_portion - 0.5 * (NVX - 1)) * spacing
    vel_y = (col_part - 0.5 * (NVX - 1)) * spacing
    return (vel_x, vel_y)

def kernel_tile(out_index, in_index):
    spacing = 2.0 * vel_max / NVX
    out_x, out_y = velocity_parts(out_index)
    in_x, in_y = velocity_parts(in_index)
    out_sq = out_x * out_x + out_y * out_y
    in_sq = in_x * in_x + in_y * in_y
    diff_sq = (out_x[:, None] - in_x[None, :]) ** 2 + (out_y[:, None] - in_y[None, :]) ** 2 + spacing * spacing
    energy = out_sq[:, None] - in_sq[None, :]
    radius = jnp.sqrt(diff_sq)
    far_part = 2.0 / radius * jnp.exp(-diff_sq / 8.0 - energy * energy / (8.0 * diff_sq))
    near_part = radius * jnp.exp(-(out_sq[:, None] + in_sq[None, :]) / 4.0)
    return grad_scale * spacing * spacing * (far_part - near_part)

def flux_change(strip, courant, axis):
    count = strip.shape[axis] - 4
    diff = lax.slice_in_dim(strip, 1, count + 4, axis=axis) - lax.slice_in_dim(strip, 0, count + 3, axis=axis)
    lower = lax.slice_in_dim(diff, 0, count + 2, axis=axis)
    upper = lax.slice_in_dim(diff, 1, count + 3, axis=axis)
    slope = 0.5 * (jnp.sign(lower) + jnp.sign(upper)) * jnp.minimum(jnp.abs(lower), jnp.abs(upper))
    forward = courant > 0
    upwind = jnp.where(forward, lax.slice_in_dim(strip, 1, count + 2, axis=axis), lax.slice_in_dim(strip, 2, count + 3, axis=axis))
    up_slope = jnp.where(forward, lax.slice_in_dim(slope, 0, count + 1, axis=axis), lax.slice_in_dim(slope, 1, count + 2, axis=axis))
    magnitude = jnp.abs(courant)
    flux = courant * upwind + 0.5 * magnitude * (1.0 - magnitude) * up_slope
    return lax.slice_in_dim(flux, 1, count + 1, axis=axis) - lax.slice_in_dim(flux, 0, count, axis=axis)

def advect(padded, courant_x, courant_y):
    row_term = flux_change(padded[:, 2:-2], courant_x, 0)
    col_term = flux_change(padded[2:-2], courant_y, 1)
    return padded[2:-2, 2:-2] - row_term - col_term

def reference(distribution, density, cell_type, inflow):
    all_index = jnp.arange(NV, dtype=jnp.int32)
    vel_x, vel_y = velocity_parts(all_index)
    courant_x = time_step * vel_x
    courant_y = time_step * vel_y
    collision_frequency = 1.0 + (vel_x * vel_x + vel_y * vel_y) / 8.0
    block_len = NV // N_VERT
    solid_wall_cell = (cell_type == 1)[:, :, None]
    inflow_cell = (cell_type == 2)[:, :, None]
    field = distribution
    for step in range(STEPS):
        padded = jnp.pad(field, ((2, 2), (2, 2), (0, 0)))
        transported_density = advect(padded, courant_x, courant_y)
        rows = transported_density.reshape(NX * NY, NV)

        def block_gain_term(block_id):
            out_index = block_id * block_len + jnp.arange(block_len, dtype=jnp.int32)
            tile = kernel_tile(out_index, all_index)
            return lax.dot_general(rows, tile, (((1,), (1,)), ((), ())), precision=lax.Precision.HIGHEST, preferred_element_type=jnp.float32)
        parts = lax.map(block_gain_term, jnp.arange(N_VERT, dtype=jnp.int32))
        gain_term = jnp.transpose(parts, (1, 0, 2)).reshape(NX, NY, NV)
        post_collision_density = transported_density + collision_rate * density[:, :, None] * (gain_term - collision_frequency * transported_density)
        field = jnp.where(solid_wall_cell, jnp.float32(0.0), jnp.where(inflow_cell, inflow[None, None, :], post_collision_density))
    return field
```

```python
import functools

import jax
import jax.numpy as jnp
from jax import lax
from jax.experimental import pallas as pl
from jax.experimental.pallas import tpu as pltpu
from jax.sharding import PartitionSpec as P

NVX = 64
STEPS = 2
HALF = NVX // 2
LANES = 128
GROUP = LANES // HALF

vel_max = 4.0
time_step = 0.1
grad_scale = 2.5
collision_rate = 0.2
spacing = 2.0 * vel_max / NVX
middle = 0.5 * (NVX - 1)
VMEM_LIMIT = 50 * 1024 * 1024


def velocity_parts(index):
    row_portion = (index // NVX).astype(jnp.float32)
    col_part = (index % NVX).astype(jnp.float32)
    vel_x = (row_portion - middle) * spacing
    vel_y = (col_part - middle) * spacing
    return (vel_x, vel_y)


def lane_index(shape):
    return lax.broadcasted_iota(jnp.int32, shape, len(shape) - 1)


def kgen_body(rows_in, groups_out, here_ref, hi_ref, lo_ref):
    source = pl.program_id(0)
    block = pl.program_id(1)
    me = here_ref[0]
    count = here_ref[1]
    local = groups_out * GROUP
    lane = lane_index((1, LANES))
    vy = ((lane % HALF).astype(jnp.float32) - middle) * spacing
    wy = (lax.broadcasted_iota(jnp.int32, (HALF, LANES), 0).astype(jnp.float32) - middle) * spacing
    same_sq = (vy - wy) ** 2 + spacing * spacing
    flip_sq = (vy + wy) ** 2 + spacing * spacing
    wy_sq = wy * wy
    first = lax.rem(me + source, count) * local + block * rows_in

    def one_row(j, carry):
        wx = ((first + j).astype(jnp.float32) - middle) * spacing
        in_sq = wx * wx + wy_sq
        in_gauss = 0.5 * jnp.exp(in_sq * -0.25)
        rows = pl.ds(pl.multiple_of(j * HALF, HALF), HALF)
        for g in range(groups_out):
            ix = me * local + g * GROUP + lane // HALF
            vx = (ix.astype(jnp.float32) - middle) * spacing
            out_sq = vx * vx + vy * vy
            out_gauss = jnp.exp(out_sq * -0.25)
            energy = out_sq - in_sq
            energy_sq = energy * energy
            gauss = out_gauss * in_gauss
            dx_sq = (vx - wx) ** 2

            def entry(dy_sq):
                diff_sq = dx_sq + dy_sq
                inverse = lax.rsqrt(diff_sq)
                decay = jnp.exp((diff_sq + energy_sq * (inverse * inverse)) * -0.125)
                return inverse * (decay - diff_sq * gauss)

            same = entry(same_sq)
            flip = entry(flip_sq)
            cols = slice(g * LANES, (g + 1) * LANES)
            for parity, value in ((0, same + flip), (1, same - flip)):
                high = value.astype(jnp.bfloat16)
                hi_ref[0, parity, rows, cols] = high
                lo_ref[0, parity, rows, cols] = (value - high.astype(jnp.float32)).astype(jnp.bfloat16)
        return carry

    lax.fori_loop(0, rows_in, one_row, 0)


def make_tiles(here, local, sources):
    size = local * HALF
    rows_in = 4
    block = pl.BlockSpec((1, 2, rows_in * HALF, size), lambda s, b: (s, 0, b, 0))
    shape = jax.ShapeDtypeStruct((sources, 2, size, size), jnp.bfloat16)
    entries = sources * 2 * size * size
    return pl.pallas_call(
        functools.partial(kgen_body, rows_in, local // GROUP),
        grid=(sources, local // rows_in),
        in_specs=[pl.BlockSpec(memory_space=pltpu.SMEM)],
        out_specs=[block, block],
        out_shape=[shape, shape],
        compiler_params=pltpu.CompilerParams(vmem_limit_bytes=VMEM_LIMIT),
        cost_estimate=pl.CostEstimate(flops=20 * entries, bytes_accessed=4 * entries, transcendentals=2 * entries),
        name="kernel_entries",
    )(here)


def minmod(a, b):
    return jnp.maximum(jnp.minimum(a, b), 0.0) + jnp.minimum(jnp.maximum(a, b), 0.0)


def transport_body(wide, here_ref, field_ref, xhalo_ref, ylo_ref, yhi_ref, adv_ref, fold_ref):
    rows_x, rows_y, _ = field_ref.shape
    has_low = here_ref[2] > 0
    has_high = here_ref[3] > 0
    start = here_ref[0] * here_ref[4] + pl.program_id(0) * wide
    vx, vy = velocity_parts(start + lane_index((1, wide)))
    ax = time_step * vx
    ay = time_step * vy
    bx = 0.5 * jnp.abs(ax) * (1.0 - jnp.abs(ax))
    by = 0.5 * jnp.abs(ay) * (1.0 - jnp.abs(ay))
    ahead_x = ax > 0
    ahead_y = ay > 0

    def row(i):
        if i < 0:
            return jnp.where(has_low, xhalo_ref[i + 2], 0.0)
        if i >= rows_x:
            return jnp.where(has_high, xhalo_ref[i - rows_x], 0.0)
        return field_ref[i]

    def edge(f0, f1, f2):
        return ay * f1 + by * minmod(f1 - f0, f2 - f1)

    at_y = lax.broadcasted_iota(jnp.int32, (rows_y, wide), 0)
    first_y = at_y == 0
    last_y = at_y == rows_y - 1
    lane = lane_index((rows_y, LANES))
    in_pair = (lane // HALF) % 2 * NVX
    straight = in_pair + lane % HALF
    mirrored = in_pair + (NVX - 1) - lane % HALF
    first_half = lane < LANES // 2

    def folded(rows):
        def pick(index):
            return jnp.where(
                first_half,
                jnp.take_along_axis(rows[:, :LANES], index, axis=1),
                jnp.take_along_axis(rows[:, LANES:], index, axis=1),
            )

        x, y = pick(straight), pick(mirrored)
        return x + y, x - y

    values = [row(-2), row(-1), row(0)]
    low = values[1] - values[0]
    high = values[2] - values[1]
    face = [ax * values[1] + bx * minmod(low, high)]
    for i in range(rows_x + 1):
        values = [values[1], values[2], row(i + 1)]
        low, high = high, values[2] - values[1]
        face.append(ax * values[1] + bx * minmod(low, high))
        if i == 0:
            continue
        x = i - 1
        here = values[0]
        row_term = jnp.where(ahead_x, face[x + 1] - face[x], face[x + 2] - face[x + 1])
        lo1 = ylo_ref[1, x : x + 1]
        lo0 = ylo_ref[0, x : x + 1]
        hi0 = yhi_ref[0, x : x + 1]
        hi1 = yhi_ref[1, x : x + 1]
        below = jnp.where(first_y, lo1, pltpu.roll(here, 1, 0))
        above = jnp.where(last_y, hi0, pltpu.roll(here, rows_y - 1, 0))
        mine = ay * here + by * minmod(here - below, above - here)
        edge_low = edge(lo0, lo1, here[0:1])
        edge_high = edge(here[rows_y - 1 : rows_y], hi0, hi1)
        mine_below = jnp.where(first_y, edge_low, pltpu.roll(mine, 1, 0))
        mine_above = jnp.where(last_y, edge_high, pltpu.roll(mine, rows_y - 1, 0))
        col_term = jnp.where(ahead_y, mine - mine_below, mine_above - mine)
        moved = here - row_term - col_term
        adv_ref[x] = moved
        for part in range(wide // (2 * LANES)):
            even, odd = folded(moved[:, part * 2 * LANES : (part + 1) * 2 * LANES])
            cols = slice(part * LANES, (part + 1) * LANES)
            at = slice(x * rows_y, (x + 1) * rows_y)
            fold_ref[0, at, cols] = even
            fold_ref[1, at, cols] = odd


def transport(here, field, xhalo, ylo, yhi):
    rows_x, rows_y, local_len = field.shape
    wide = 2 * LANES
    cells = rows_x * rows_y
    return pl.pallas_call(
        functools.partial(transport_body, wide),
        grid=(local_len // wide,),
        in_specs=[
            pl.BlockSpec(memory_space=pltpu.SMEM),
            pl.BlockSpec((rows_x, rows_y, wide), lambda i: (0, 0, i)),
            pl.BlockSpec((2, rows_y, wide), lambda i: (0, 0, i)),
            pl.BlockSpec((2, rows_x, wide), lambda i: (0, 0, i)),
            pl.BlockSpec((2, rows_x, wide), lambda i: (0, 0, i)),
        ],
        out_specs=[
            pl.BlockSpec((rows_x, rows_y, wide), lambda i: (0, 0, i)),
            pl.BlockSpec((2, cells, wide // 2), lambda i: (0, 0, i)),
        ],
        out_shape=[
            jax.ShapeDtypeStruct(field.shape, jnp.float32),
            jax.ShapeDtypeStruct((2, cells, local_len // 2), jnp.float32),
        ],
        compiler_params=pltpu.CompilerParams(vmem_limit_bytes=VMEM_LIMIT),
        cost_estimate=pl.CostEstimate(flops=40 * cells * local_len, bytes_accessed=16 * cells * local_len, transcendentals=0),
        name="transport",
    )(here, field, xhalo, ylo, yhi)


def split(value):
    high = value.astype(jnp.bfloat16)
    return high, (value - high.astype(jnp.float32)).astype(jnp.bfloat16)


def product(rows, rows_lo, tile, tile_lo):
    dot = functools.partial(jnp.dot, preferred_element_type=jnp.float32)
    return dot(rows, tile) + (dot(rows_lo, tile) + dot(rows, tile_lo))


def split_once(fold_ref, high, low):
    @pl.when(pl.program_id(0) == 0)
    def _():
        high[...], low[...] = split(fold_ref[...])


def own_body(fold_ref, hi_ref, lo_ref, out_ref, high, low):
    split_once(fold_ref, high, low)
    for parity in range(2):
        out_ref[parity] = product(high[parity], low[parity], hi_ref[0, parity], lo_ref[0, parity])


def collide_body(wide, here_ref, fold_ref, hi_ref, lo_ref, part_ref, adv_ref, density_ref, type_ref, inflow_ref, out_ref, high, low):
    split_once(fold_ref, high, low)
    even = part_ref[0] + product(high[0], low[0], hi_ref[0, 0], lo_ref[0, 0])
    odd = part_ref[1] + product(high[1], low[1], hi_ref[0, 1], lo_ref[0, 1])
    cells = even.shape[0]
    rows_x, rows_y, out_wide = out_ref.shape
    start = here_ref[0] * here_ref[4] + pl.program_id(0) * out_wide
    vx, vy = velocity_parts(start + lane_index((1, out_wide)))
    nu = 1.0 + (vx * vx + vy * vy) / 8.0
    plus = even + odd
    minus = even - odd
    lane = lane_index((cells, LANES))
    at_y = lane % NVX
    lower = at_y < HALF
    index = lane // NVX * HALF + jnp.where(lower, at_y, NVX - 1 - at_y)
    rate = collision_rate * density_ref[...]
    scale = grad_scale * spacing * spacing
    kind = type_ref[...]
    for part in range(wide // LANES):
        cols = slice(part * LANES, (part + 1) * LANES)
        for side in range(2):
            pick = index + side * (LANES // 2)
            gain = scale * jnp.where(
                lower,
                jnp.take_along_axis(plus[:, cols], pick, axis=1),
                jnp.take_along_axis(minus[:, cols], pick, axis=1),
            )
            at = slice((2 * part + side) * LANES, (2 * part + side + 1) * LANES)
            moved = adv_ref[:, :, at].reshape(cells, LANES)
            done = moved + rate * (gain - nu[:, at] * moved)
            done = jnp.where(kind == 1, 0.0, jnp.where(kind == 2, inflow_ref[:, at], done))
            out_ref[:, :, at] = done.reshape(rows_x, rows_y, LANES)


def own_gain(fold, tile_hi, tile_lo, source):
    _, cells, size = fold.shape
    wide = 2 * LANES
    tile = pl.BlockSpec((1, 2, size, wide), lambda i: (source, 0, 0, i))
    return pl.pallas_call(
        own_body,
        grid=(size // wide,),
        in_specs=[pl.BlockSpec((2, cells, size), lambda i: (0, 0, 0)), tile, tile],
        out_specs=pl.BlockSpec((2, cells, wide), lambda i: (0, 0, i)),
        out_shape=jax.ShapeDtypeStruct(fold.shape, jnp.float32),
        scratch_shapes=[pltpu.VMEM((2, cells, size), jnp.bfloat16)] * 2,
        compiler_params=pltpu.CompilerParams(vmem_limit_bytes=VMEM_LIMIT),
        cost_estimate=pl.CostEstimate(flops=12 * cells * size * size, bytes_accessed=8 * size * size + 16 * cells * size, transcendentals=0),
        name="own_gain",
    )(fold, tile_hi, tile_lo)


def collide(here, fold, tile_hi, tile_lo, source, part, advected, density, kind, inflow):
    _, cells, size = fold.shape
    rows_x, rows_y, local_len = advected.shape
    wide = 2 * LANES
    tile = pl.BlockSpec((1, 2, size, wide), lambda i: (source, 0, 0, i))
    block = pl.BlockSpec((rows_x, rows_y, 2 * wide), lambda i: (0, 0, i))
    column = pl.BlockSpec((cells, 1), lambda i: (0, 0))
    return pl.pallas_call(
        functools.partial(collide_body, wide),
        grid=(size // wide,),
        in_specs=[
            pl.BlockSpec(memory_space=pltpu.SMEM),
            pl.BlockSpec((2, cells, size), lambda i: (0, 0, 0)),
            tile,
            tile,
            pl.BlockSpec((2, cells, wide), lambda i: (0, 0, i)),
            block,
            column,
            column,
            pl.BlockSpec((1, 2 * wide), lambda i: (0, i)),
        ],
        out_specs=block,
        out_shape=jax.ShapeDtypeStruct(advected.shape, jnp.float32),
        scratch_shapes=[pltpu.VMEM((2, cells, size), jnp.bfloat16)] * 2,
        compiler_params=pltpu.CompilerParams(vmem_limit_bytes=VMEM_LIMIT),
        cost_estimate=pl.CostEstimate(flops=12 * cells * size * size, bytes_accessed=8 * size * size + 32 * cells * size, transcendentals=0),
        name="collide",
    )(here, fold, tile_hi, tile_lo, part, advected, density, kind, inflow)


def shifted(block, axis, by):
    count = lax.axis_size(axis)
    return lax.ppermute(block, axis, [(i, i + by) for i in range(count) if 0 <= i + by < count])


def per_device(distribution, density, cell_type, inflow):
    rows_x, rows_y, local_len = distribution.shape
    cells = rows_x * rows_y
    vert = lax.axis_index("vert")
    verts = lax.axis_size("vert")
    at_x = lax.axis_index("gx")
    size_x = lax.axis_size("gx")
    assert size_x == 2 and verts == 2
    here = jnp.stack(
        [vert, jnp.int32(verts), (at_x > 0).astype(jnp.int32), (at_x < size_x - 1).astype(jnp.int32), jnp.int32(local_len)]
    ).astype(jnp.int32)
    column_density = density.reshape(cells, 1)
    column_type = cell_type.reshape(cells, 1)
    row_inflow = inflow.reshape(1, local_len)
    tiles = None
    field = distribution
    for step in range(STEPS):
        ylo = shifted(jnp.transpose(field[:, -2:], (1, 0, 2)), "gy", 1)
        yhi = shifted(jnp.transpose(field[:, :2], (1, 0, 2)), "gy", -1)
        send_x = jnp.where(at_x == 0, field[-2:], field[:2])
        xhalo = lax.ppermute(send_x, "gx", [(0, 1), (1, 0)])
        if tiles is None:
            tiles = make_tiles(here, local_len // NVX, verts)
        advected, fold = transport(here, field, xhalo, ylo, yhi)
        other = lax.ppermute(fold, "vert", [(0, 1), (1, 0)])
        part = own_gain(fold, tiles[0], tiles[1], 0)
        field = collide(here, other, tiles[0], tiles[1], 1, part, advected, column_density, column_type, row_inflow)
    return field


def solution(mesh):
    placed = (P("gx", "gy", "vert"), P("gx", "gy"), P("gx", "gy"), P("vert"))
    return jax.shard_map(
        per_device, mesh=mesh, in_specs=placed, out_specs=P("gx", "gy", "vert"), check_vma=False
    )
```

```python
import functools
import math

import jax
import jax.numpy as jnp
from jax import lax
from jax.experimental import pallas as pl
from jax.experimental.pallas import tpu as pltpu
from jax.sharding import PartitionSpec as P

NVX = 64
STEPS = 2
HALF = NVX // 2
LANES = 128
GROUP = LANES // HALF

vel_max = 4.0
time_step = 0.1
grad_scale = 2.5
collision_rate = 0.2
spacing = 2.0 * vel_max / NVX
middle = 0.5 * (NVX - 1)

MIB = 1024 * 1024
WHOLE = pl.BlockSpec(memory_space=pltpu.VMEM)
SCALARS = pl.BlockSpec(memory_space=pltpu.SMEM)

EXPONENT = 0.125 * math.log2(math.e)
ENTRY_SCALE = grad_scale * spacing * spacing * math.sqrt(EXPONENT)


def room(mib):
    return pltpu.CompilerParams(vmem_limit_bytes=mib * MIB)


def in_vmem(value):
    return pltpu.with_memory_space_constraint(value, pltpu.VMEM)


def velocity_parts(index):
    row_portion = (index // NVX).astype(jnp.float32)
    col_part = (index % NVX).astype(jnp.float32)
    vel_x = (row_portion - middle) * spacing
    vel_y = (col_part - middle) * spacing
    return (vel_x, vel_y)


def iota(shape, dim):
    return lax.broadcasted_iota(jnp.int32, shape, dim)


def slot_order(slot):
    return lax.rem(slot, 2) * 2 + lax.div(slot, 2)


def entries_body(local, sources, here_ref, _density, _kind, hi_ref, lo_ref):
    me = here_ref[0]
    count = here_ref[1]
    groups = local // GROUP
    rows = 16
    lane = iota((1, LANES), 1)
    slot = slot_order(lane // HALF)
    vy = ((lane % HALF).astype(jnp.float32) - middle) * spacing
    out_x = [(me * local + g * GROUP + slot).astype(jnp.float32) for g in range(groups)]
    out_x = [(x - middle) * spacing for x in out_x]
    out_sq = [x * x + vy * vy for x in out_x]
    out_gauss = [jnp.exp(s * -0.25) for s in out_sq]

    def one(index, carry):
        source = lax.div(index, GROUP)
        r = lax.rem(index, GROUP)
        first = lax.rem(me + source, count) * local
        in_x_sq = []
        in_x_gauss = []
        for k in range(groups):
            wx = jnp.full((1, LANES), first + k * GROUP + r, jnp.int32).astype(jnp.float32)
            wx = (wx - middle) * spacing
            in_x_sq.append(wx * wx)
            in_x_gauss.append(jnp.exp(wx * wx * -0.25) * (0.5 / EXPONENT))
        for half in range(HALF // rows):
            wy = (iota((rows, LANES), 0) + half * rows).astype(jnp.float32)
            wy = (wy - middle) * spacing
            in_y_sq = EXPONENT * wy * wy
            in_y_gauss = jnp.exp(wy * wy * -0.25)
            dy_same = EXPONENT * ((vy - wy) ** 2 + spacing * spacing)
            dy_flip = EXPONENT * ((vy + wy) ** 2 + spacing * spacing)
            for m in range(1 - groups, groups):
                apart = (me * local - first + m * GROUP - r + slot).astype(jnp.float32) * spacing
                dx_sq = EXPONENT * apart * apart
                tables = []
                for dy in (dy_same, dy_flip):
                    distance = dx_sq + dy
                    inverse = lax.rsqrt(distance)
                    tables.append((distance, inverse, inverse * inverse))
                for g in range(max(0, m), min(groups, groups + m)):
                    k = g - m
                    energy = EXPONENT * (out_sq[g] - in_x_sq[k]) - in_y_sq
                    energy_sq = energy * energy
                    gauss = (out_gauss[g] * in_x_gauss[k]) * in_y_gauss
                    same, flip = (
                        inverse * (jnp.exp2(-distance - energy_sq * inverse_sq) - distance * gauss)
                        for distance, inverse, inverse_sq in tables
                    )
                    start = (k * GROUP + slot_order(r)) * HALF + half * rows
                    at = pl.ds(pl.multiple_of(start, rows), rows)
                    cols = slice(g * LANES, (g + 1) * LANES)
                    for parity, value in ((0, same + flip), (1, same - flip)):
                        high = value.astype(jnp.bfloat16)
                        hi_ref[source, parity, at, cols] = high
                        lo_ref[source, parity, at, cols] = (value - high.astype(jnp.float32)).astype(jnp.bfloat16)
        return carry

    lax.fori_loop(0, sources * GROUP, one, 0)


def make_entries(here, density, kind, local, sources):
    size = local * HALF
    count = sources * 2 * size * size
    shape = pltpu.VMEM((sources, 2, size, size), jnp.bfloat16)
    return pl.pallas_call(
        functools.partial(entries_body, local, sources),
        in_specs=[SCALARS, WHOLE, WHOLE],
        out_specs=[WHOLE, WHOLE],
        out_shape=[shape, shape],
        compiler_params=room(6),
        cost_estimate=pl.CostEstimate(flops=20 * count, bytes_accessed=4 * count, transcendentals=2 * count),
        name="kernel_entries",
    )(here, in_vmem(density), in_vmem(kind))


def minmod(a, b):
    return jnp.maximum(jnp.minimum(a, b), 0.0) + jnp.minimum(jnp.maximum(a, b), 0.0)


def fold_masks(rows):
    lane = iota((rows, LANES), 1)
    slot = lane // HALF
    even = slot % 2 == 0
    turned = jnp.where(even, 2 - slot, slot) * HALF + (HALF - 1) - lane % HALF
    return even, turned


def folded(a, b, even, turned):
    near = jnp.where(even, a, b)
    far = pltpu.roll(jnp.where(even, b, a), HALF, 1)
    lower = jnp.where(even, near, far)
    upper = jnp.take_along_axis(jnp.where(even, far, near), turned, axis=1)
    return lower + upper, lower - upper


def unfolded(lower, upper, even, turned):
    upper = jnp.take_along_axis(upper, turned, axis=1)
    near = jnp.where(even, lower, upper)
    far = pltpu.roll(jnp.where(even, upper, lower), LANES - HALF, 1)
    return jnp.where(even, near, far), jnp.where(even, far, near)


def transport_body(wide, rows_x, here_ref, field_ref, xhalo_ref, ylo_ref, yhi_ref, _hi, _lo, adv_ref, fold_ref, low_edge, high_edge):
    cells, local_len = field_ref.shape
    rows_y = cells // rows_x
    has_low = here_ref[2] > 0
    has_high = here_ref[3] > 0
    at_y = iota((rows_y, wide), 0)
    first_y = at_y == 0
    last_y = at_y == rows_y - 1
    even, turned = fold_masks(rows_y)

    def chunk(c, carry):
        cols = pl.ds(pl.multiple_of(c * wide, wide), wide)
        vx, vy = velocity_parts(here_ref[0] * local_len + c * wide + iota((1, wide), 1))
        ax = time_step * vx
        ay = time_step * vy
        bx = 0.5 * jnp.abs(ax) * (1.0 - jnp.abs(ax))
        by = 0.5 * jnp.abs(ay) * (1.0 - jnp.abs(ay))
        ahead_x = ax > 0
        ahead_y = ay > 0

        def face_y(f0, f1, f2):
            return ay * f1 + by * minmod(f1 - f0, f2 - f1)

        for x in range(rows_x):
            low_edge[x : x + 1] = field_ref[x * rows_y : x * rows_y + 1, cols]
            high_edge[x : x + 1] = field_ref[(x + 1) * rows_y - 1 : (x + 1) * rows_y, cols]
        low_edge[...] = face_y(ylo_ref[0, :, cols], ylo_ref[1, :, cols], low_edge[...])
        high_edge[...] = face_y(high_edge[...], yhi_ref[0, :, cols], yhi_ref[1, :, cols])

        def row(i):
            if i < 0:
                return jnp.where(has_low, xhalo_ref[i + 2, :, cols], 0.0)
            if i >= rows_x:
                return jnp.where(has_high, xhalo_ref[i - rows_x, :, cols], 0.0)
            return field_ref[i * rows_y : (i + 1) * rows_y, cols]

        near = [row(-2), row(-1), row(0)]
        low, high = near[1] - near[0], near[2] - near[1]
        face = [ax * near[1] + bx * minmod(low, high)]
        for i in range(rows_x + 1):
            near = [near[1], near[2], row(i + 1)]
            low, high = high, near[2] - near[1]
            face.append(ax * near[1] + bx * minmod(low, high))
            if i == 0:
                continue
            x = i - 1
            here = near[0]
            row_term = jnp.where(ahead_x, face[x + 1] - face[x], face[x + 2] - face[x + 1])
            below = jnp.where(first_y, ylo_ref[1, x : x + 1, cols], pltpu.roll(here, 1, 0))
            above = jnp.where(last_y, yhi_ref[0, x : x + 1, cols], pltpu.roll(here, rows_y - 1, 0))
            mine = face_y(below, here, above)
            mine_below = jnp.where(first_y, low_edge[x : x + 1], pltpu.roll(mine, 1, 0))
            mine_above = jnp.where(last_y, high_edge[x : x + 1], pltpu.roll(mine, rows_y - 1, 0))
            col_term = jnp.where(ahead_y, mine - mine_below, mine_above - mine)
            moved = here - row_term - col_term
            at = slice(x * rows_y, (x + 1) * rows_y)
            adv_ref[at, cols] = moved
            for part in range(wide // (2 * LANES)):
                first = 2 * part * LANES
                both = folded(moved[:, first : first + LANES], moved[:, first + LANES : first + 2 * LANES], even, turned)
                to = pl.ds(pl.multiple_of(c * (wide // 2) + part * LANES, LANES), LANES)
                fold_ref[0, at, to], fold_ref[1, at, to] = both
        return carry

    lax.fori_loop(0, local_len // wide, chunk, 0)


def transport(here, rows_x, field, xhalo, ylo, yhi, entries):
    cells, local_len = field.shape
    wide = 4 * LANES
    return pl.pallas_call(
        functools.partial(transport_body, wide, rows_x),
        in_specs=[SCALARS] + [WHOLE] * 6,
        out_specs=[WHOLE] * 2,
        out_shape=[pltpu.VMEM(field.shape, jnp.float32), pltpu.VMEM((2, cells, local_len // 2), jnp.float32)],
        scratch_shapes=[pltpu.VMEM((rows_x, wide), jnp.float32)] * 2,
        compiler_params=room(6),
        cost_estimate=pl.CostEstimate(flops=40 * cells * local_len, bytes_accessed=16 * cells * local_len, transcendentals=0),
        name="transport",
    )(here, in_vmem(field), in_vmem(xhalo), in_vmem(ylo), in_vmem(yhi), in_vmem(entries[0]), in_vmem(entries[1]))


def split_into(value_ref, high, low):
    for parity in range(2):
        value = value_ref[parity]
        rounded = value.astype(jnp.bfloat16)
        high[parity] = rounded
        low[parity] = (value - rounded.astype(jnp.float32)).astype(jnp.bfloat16)


def product(high, low, hi_ref, lo_ref, source, parity, cols):
    dot = functools.partial(jnp.dot, preferred_element_type=jnp.float32)
    tile = hi_ref[source, parity, :, cols]
    return dot(high[parity], tile) + (dot(low[parity], tile) + dot(high[parity], lo_ref[source, parity, :, cols]))


def own_body(wide, fold_ref, hi_ref, lo_ref, out_ref, high, low):
    split_into(fold_ref, high, low)
    for j in range(fold_ref.shape[2] // wide):
        cols = slice(j * wide, (j + 1) * wide)
        for parity in range(2):
            out_ref[parity, :, cols] = product(high, low, hi_ref, lo_ref, 0, parity, cols)


def own_gain(fold, entries):
    _, cells, size = fold.shape
    return pl.pallas_call(
        functools.partial(own_body, 2 * LANES),
        in_specs=[WHOLE] * 3,
        out_specs=WHOLE,
        out_shape=pltpu.VMEM(fold.shape, jnp.float32),
        scratch_shapes=[pltpu.VMEM(fold.shape, jnp.bfloat16)] * 2,
        compiler_params=room(8),
        cost_estimate=pl.CostEstimate(flops=12 * cells * size * size, bytes_accessed=8 * size * size + 16 * cells * size, transcendentals=0),
        name="own_gain",
    )(in_vmem(fold), in_vmem(entries[0]), in_vmem(entries[1]))


def collide_body(
    wide, rows_x, last, here_ref, fold_ref, hi_ref, lo_ref, part_ref, adv_ref, density_ref, type_ref, inflow_ref, *rest
):
    if last:
        out_ref, high, low, field, sems = rest
    else:
        field, up_ref, down_ref, xsend_ref, high, low = rest
    cells, local_len = adv_ref.shape
    rows_y = cells // rows_x
    split_into(fold_ref, high, low)
    even_slot, turned = fold_masks(cells)
    rate = jnp.broadcast_to(collision_rate * density_ref[...], (cells, LANES))
    gain_rate = rate * ENTRY_SCALE
    kind = jnp.broadcast_to(type_ref[...], (cells, LANES))
    wall = kind == 1
    inlet = kind == 2
    copies = []
    for j in range(local_len // (2 * wide)):
        cols = slice(j * wide, (j + 1) * wide)
        even, odd = (part_ref[p, :, cols] + product(high, low, hi_ref, lo_ref, 1, p, cols) for p in range(2))
        lower = even + odd
        upper = even - odd
        for part in range(wide // LANES):
            group = slice(part * LANES, (part + 1) * LANES)
            for side, gain in enumerate(unfolded(lower[:, group], upper[:, group], even_slot, turned)):
                first = 2 * (j * wide + part * LANES) + side * LANES
                at = slice(first, first + LANES)
                vx, vy = velocity_parts(here_ref[0] * local_len + first + iota((1, LANES), 1))
                nu = 1.0 + (vx * vx + vy * vy) / 8.0
                moved = adv_ref[:, at]
                done = moved + (gain_rate * gain - rate * (nu * moved))
                field[:, at] = jnp.where(wall, 0.0, jnp.where(inlet, inflow_ref[:, at], done))
        span = slice(2 * j * wide, 2 * (j + 1) * wide)
        if last:
            copy = pltpu.make_async_copy(field.at[:, span], out_ref.at[:, span], sems.at[j])
            copy.start()
            copies.append(copy)
        else:
            for layer in range(2):
                for x in range(rows_x):
                    first = x * rows_y + layer
                    down_ref[layer, x : x + 1, span] = field[first : first + 1, span]
                    first = (x + 1) * rows_y - 2 + layer
                    up_ref[layer, x : x + 1, span] = field[first : first + 1, span]
                first_row = field[layer * rows_y : (layer + 1) * rows_y, span]
                last_row = field[(rows_x - 2 + layer) * rows_y : (rows_x - 1 + layer) * rows_y, span]
                xsend_ref[layer, :, span] = jnp.where(here_ref[3] > 0, last_row, first_row)
    for copy in copies:
        copy.wait()


def collide(here, rows_x, fold, entries, part, advected, density, kind, inflow, last):
    _, cells, size = fold.shape
    local_len = advected.shape[1]
    wide = 2 * LANES
    halves = [pltpu.VMEM(fold.shape, jnp.bfloat16)] * 2
    if last:
        out_specs = pl.BlockSpec(memory_space=pl.ANY)
        out_shape = jax.ShapeDtypeStruct(advected.shape, jnp.float32)
        scratch = halves + [pltpu.VMEM(advected.shape, jnp.float32), pltpu.SemaphoreType.DMA((size // wide,))]
    else:
        edge_y = pltpu.VMEM((2, rows_x, local_len), jnp.float32)
        edge_x = pltpu.VMEM((2, cells // rows_x, local_len), jnp.float32)
        out_specs = [WHOLE] * 4
        out_shape = [pltpu.VMEM(advected.shape, jnp.float32), edge_y, edge_y, edge_x]
        scratch = halves
    return pl.pallas_call(
        functools.partial(collide_body, wide, rows_x, last),
        in_specs=[SCALARS] + [WHOLE] * 8,
        out_specs=out_specs,
        out_shape=out_shape,
        scratch_shapes=scratch,
        compiler_params=room(12),
        cost_estimate=pl.CostEstimate(flops=12 * cells * size * size, bytes_accessed=8 * size * size + 32 * cells * size, transcendentals=0),
        name="collide",
    )(here, in_vmem(fold), in_vmem(entries[0]), in_vmem(entries[1]), in_vmem(part), in_vmem(advected), density, kind, inflow)


def shifted(block, axis, by):
    count = lax.axis_size(axis)
    return lax.ppermute(block, axis, [(i, i + by) for i in range(count) if 0 <= i + by < count])


def per_device(distribution, density, cell_type, inflow):
    rows_x, rows_y, local_len = distribution.shape
    cells = rows_x * rows_y
    vert = lax.axis_index("vert")
    verts = lax.axis_size("vert")
    at_x = lax.axis_index("gx")
    size_x = lax.axis_size("gx")
    assert size_x == 2 and verts == 2
    here = jnp.stack([vert, jnp.int32(verts), (at_x > 0).astype(jnp.int32), (at_x < size_x - 1).astype(jnp.int32)])
    column_density = density.reshape(cells, 1)
    column_type = cell_type.reshape(cells, 1)
    row_inflow = inflow.reshape(1, local_len)
    swap = [(0, 1), (1, 0)]
    up = jnp.transpose(distribution[:, -2:], (1, 0, 2))
    down = jnp.transpose(distribution[:, :2], (1, 0, 2))
    send_x = jnp.where(at_x == 0, distribution[-2:], distribution[:2])
    field = distribution.reshape(cells, local_len)
    entries = None
    for step in range(STEPS):
        last = step == STEPS - 1
        ylo = shifted(up, "gy", 1)
        yhi = shifted(down, "gy", -1)
        xhalo = lax.ppermute(send_x, "gx", swap)
        if entries is None:
            entries = make_entries(here, column_density, column_type, local_len // NVX, verts)
        advected, fold = transport(here, rows_x, field, xhalo, ylo, yhi, entries)
        other = lax.ppermute(fold, "vert", swap)
        part = own_gain(fold, entries)
        out = collide(here, rows_x, other, entries, part, advected, column_density, column_type, row_inflow, last)
        if not last:
            field, up, down, send_x = out
    return out.reshape(rows_x, rows_y, local_len)


def solution(mesh):
    placed = (P("gx", "gy", "vert"), P("gx", "gy"), P("gx", "gy"), P("vert"))
    return jax.shard_map(
        per_device, mesh=mesh, in_specs=placed, out_specs=P("gx", "gy", "vert"), check_vma=False
    )
```

```python
import functools
import math

import jax
import jax.numpy as jnp
from jax import lax
from jax.experimental import pallas as pl
from jax.experimental.pallas import tpu as pltpu
from jax.sharding import PartitionSpec as P

NVX = 64
STEPS = 2
HALF = NVX // 2
LANES = 128
GROUP = LANES // HALF

vel_max = 4.0
time_step = 0.1
grad_scale = 2.5
collision_rate = 0.2
spacing = 2.0 * vel_max / NVX
middle = 0.5 * (NVX - 1)

MIB = 1024 * 1024
WHOLE = pl.BlockSpec(memory_space=pltpu.VMEM)
SCALARS = pl.BlockSpec(memory_space=pltpu.SMEM)

EXPONENT = 0.125 * math.log2(math.e)
ENTRY_SCALE = grad_scale * spacing * spacing * math.sqrt(EXPONENT)


def room(mib):
    return pltpu.CompilerParams(vmem_limit_bytes=mib * MIB)


def in_vmem(value):
    return pltpu.with_memory_space_constraint(value, pltpu.VMEM)


def velocity_parts(index):
    row_portion = (index // NVX).astype(jnp.float32)
    col_part = (index % NVX).astype(jnp.float32)
    vel_x = (row_portion - middle) * spacing
    vel_y = (col_part - middle) * spacing
    return (vel_x, vel_y)


def iota(shape, dim):
    return lax.broadcasted_iota(jnp.int32, shape, dim)


def slot_order(slot):
    return lax.rem(slot, 2) * 2 + lax.div(slot, 2)


def write_entries(local, here_ref, source, hi_ref, lo_ref, r, half):
    me = here_ref[0]
    first = lax.rem(me + source, here_ref[1]) * local
    groups = local // GROUP
    rows = HALF // 2
    lane = iota((1, LANES), 1)
    slot = slot_order(lane // HALF)
    vy = ((lane % HALF).astype(jnp.float32) - middle) * spacing
    wy = (iota((rows, LANES), 0) + half * rows).astype(jnp.float32)
    wy = (wy - middle) * spacing
    in_y_sq = EXPONENT * wy * wy
    in_y_gauss = jnp.exp(wy * wy * -0.25)
    dy_same = EXPONENT * ((vy - wy) ** 2 + spacing * spacing)
    dy_flip = EXPONENT * ((vy + wy) ** 2 + spacing * spacing)
    out_sq, out_gauss, in_sq, in_gauss = [], [], [], []
    for k in range(groups):
        vx = ((me * local + k * GROUP + slot).astype(jnp.float32) - middle) * spacing
        out_sq.append(EXPONENT * (vx * vx + vy * vy))
        out_gauss.append(jnp.exp((vx * vx + vy * vy) * -0.25))
        wx = jnp.full((1, LANES), first + k * GROUP + r, jnp.int32).astype(jnp.float32)
        wx = (wx - middle) * spacing
        in_sq.append(EXPONENT * wx * wx)
        in_gauss.append(jnp.exp(wx * wx * -0.25) * (0.5 / EXPONENT))
    for m in range(1 - groups, groups):
        apart = (me * local - first + m * GROUP - r + slot).astype(jnp.float32) * spacing
        dx_sq = EXPONENT * apart * apart
        tables = []
        for dy in (dy_same, dy_flip):
            distance = dx_sq + dy
            inverse = lax.rsqrt(distance)
            tables.append((distance, inverse, inverse * inverse))
        for g in range(max(0, m), min(groups, groups + m)):
            k = g - m
            energy = (out_sq[g] - in_sq[k]) - in_y_sq
            energy_sq = energy * energy
            gauss = (out_gauss[g] * in_gauss[k]) * in_y_gauss
            same, flip = (
                inverse * (jnp.exp2(-distance - energy_sq * inverse_sq) - distance * gauss)
                for distance, inverse, inverse_sq in tables
            )
            start = (k * GROUP + slot_order(r)) * HALF + half * rows
            at = pl.ds(pl.multiple_of(start, rows), rows)
            cols = slice(g * LANES, (g + 1) * LANES)
            for parity, value in ((0, same + flip), (1, same - flip)):
                high = value.astype(jnp.bfloat16)
                hi_ref[source, parity, at, cols] = high
                lo_ref[source, parity, at, cols] = (value - high.astype(jnp.float32)).astype(jnp.bfloat16)


def entries_body(local, sources, here_ref, *rest):
    hi_ref, lo_ref = rest[-2:]

    def one(index, carry):
        source = lax.div(index, 2 * GROUP)
        left = lax.rem(index, 2 * GROUP)
        write_entries(local, here_ref, source, hi_ref, lo_ref, lax.div(left, 2), lax.rem(left, 2))
        return carry

    lax.fori_loop(0, sources * 2 * GROUP, one, 0)


def make_entries(here, local, sources, ahead_of):
    size = local * HALF
    count = sources * 2 * size * size
    shape = pltpu.VMEM((sources, 2, size, size), jnp.bfloat16)
    return pl.pallas_call(
        functools.partial(entries_body, local, sources),
        in_specs=[SCALARS] + [WHOLE] * len(ahead_of),
        out_specs=[WHOLE, WHOLE],
        out_shape=[shape, shape],
        compiler_params=room(6),
        cost_estimate=pl.CostEstimate(flops=20 * count, bytes_accessed=4 * count, transcendentals=2 * count),
        name="kernel_entries",
    )(here, *map(in_vmem, ahead_of))


def pack_far(far, ahead, low_half):
    count = far.shape[0] // 2
    if ahead:
        return jnp.where(low_half, pltpu.roll(far[count:], LANES - HALF, 1), far[:count])
    return jnp.where(low_half, far[:count], pltpu.roll(far[count:], HALF, 1))


def unpack_far(packed, ahead):
    shift = HALF if ahead else LANES - HALF
    parts = [packed[:, i : i + LANES] for i in range(0, packed.shape[1], LANES)]
    turned = jnp.concatenate([pltpu.roll(p, shift, 1) for p in parts], axis=1)
    return jnp.concatenate([packed, turned], axis=0)


def write_edges(here_ref, rows_x, field, span, up_ref, down_ref, xsend_ref, far_ref):
    rows_y = field.shape[0] // rows_x
    for layer in range(2):
        first_row = field[layer * rows_y : (layer + 1) * rows_y, span]
        last_row = field[(rows_x - 2 + layer) * rows_y : (rows_x - 1 + layer) * rows_y, span]
        xsend_ref[layer, :, span] = jnp.where(here_ref[3] > 0, last_row, first_row)
    low_half = iota((rows_x // 2, LANES), 1) % NVX < HALF
    for ahead, to_ref, near, far in ((True, up_ref, rows_y - 1, rows_y - 2), (False, down_ref, 0, 1)):
        for x in range(rows_x):
            to_ref[x : x + 1, span] = field[x * rows_y + near : x * rows_y + near + 1, span]
            far_ref[x : x + 1, span] = field[x * rows_y + far : x * rows_y + far + 1, span]
        for i in range(span.start, span.stop, LANES):
            at = slice(i, i + LANES)
            to_ref[rows_x:, at] = pack_far(far_ref[:, at], ahead, low_half)


def edge_shapes(rows_x, rows_y, local_len):
    edge_y = pltpu.VMEM((rows_x + rows_x // 2, local_len), jnp.float32)
    return [edge_y, edge_y, pltpu.VMEM((2, rows_y, local_len), jnp.float32)]


def stage_body(wide, rows_x, here_ref, from_ref, field, up_ref, down_ref, xsend_ref, far_ref, sems):
    spans = [slice(i, i + wide) for i in range(0, field.shape[1], wide)]
    copies = [pltpu.make_async_copy(from_ref.at[:, s], field.at[:, s], sems.at[i]) for i, s in enumerate(spans)]
    for copy in copies:
        copy.start()
    for copy, span in zip(copies, spans):
        copy.wait()
        write_edges(here_ref, rows_x, field, span, up_ref, down_ref, xsend_ref, far_ref)


def stage(here, rows_x, field):
    cells, local_len = field.shape
    wide = local_len // 4
    return pl.pallas_call(
        functools.partial(stage_body, wide, rows_x),
        in_specs=[SCALARS, pl.BlockSpec(memory_space=pltpu.HBM)],
        out_specs=[WHOLE] * 4,
        out_shape=[pltpu.VMEM(field.shape, jnp.float32)] + edge_shapes(rows_x, cells // rows_x, local_len),
        scratch_shapes=[pltpu.VMEM((rows_x, local_len), jnp.float32), pltpu.SemaphoreType.DMA((4,))],
        compiler_params=room(4),
        name="stage",
    )(here, pltpu.with_memory_space_constraint(field, pltpu.HBM))


def minmod(a, b):
    return jnp.maximum(jnp.minimum(a, b), 0.0) + jnp.minimum(jnp.maximum(a, b), 0.0)


def fold_masks(rows):
    lane = iota((rows, LANES), 1)
    slot = lane // HALF
    even = slot % 2 == 0
    turned = jnp.where(even, 2 - slot, slot) * HALF + (HALF - 1) - lane % HALF
    return even, turned


def folded(a, b, even, turned):
    near = jnp.where(even, a, b)
    far = pltpu.roll(jnp.where(even, b, a), HALF, 1)
    lower = jnp.where(even, near, far)
    upper = jnp.take_along_axis(jnp.where(even, far, near), turned, axis=1)
    return lower + upper, lower - upper


def unfolded(lower, upper, even, turned):
    upper = jnp.take_along_axis(upper, turned, axis=1)
    near = jnp.where(even, lower, upper)
    far = pltpu.roll(jnp.where(even, upper, lower), LANES - HALF, 1)
    return jnp.where(even, near, far), jnp.where(even, far, near)


def transport_body(wide, rows_x, here_ref, field_ref, xhalo_ref, ylo_ref, yhi_ref, *rest):
    adv_ref, fold_ref, low_edge, high_edge = rest[-4:]
    cells, local_len = field_ref.shape
    rows_y = cells // rows_x
    has_low = here_ref[2] > 0
    has_high = here_ref[3] > 0
    at_y = iota((rows_y, wide), 0)
    first_y = at_y == 0
    last_y = at_y == rows_y - 1
    even, turned = fold_masks(rows_y)

    def chunk(c, carry):
        cols = pl.ds(pl.multiple_of(c * wide, wide), wide)
        vx, vy = velocity_parts(here_ref[0] * local_len + c * wide + iota((1, wide), 1))
        ax = time_step * vx
        ay = time_step * vy
        bx = 0.5 * jnp.abs(ax) * (1.0 - jnp.abs(ax))
        by = 0.5 * jnp.abs(ay) * (1.0 - jnp.abs(ay))
        ahead_x = ax > 0
        ahead_y = ay > 0

        def face_y(f0, f1, f2):
            return ay * f1 + by * minmod(f1 - f0, f2 - f1)

        for x in range(rows_x):
            low_edge[x : x + 1] = field_ref[x * rows_y : x * rows_y + 1, cols]
            high_edge[x : x + 1] = field_ref[(x + 1) * rows_y - 1 : (x + 1) * rows_y, cols]
        low_far = unpack_far(ylo_ref[rows_x:, cols], True)
        high_far = unpack_far(yhi_ref[rows_x:, cols], False)
        low_edge[...] = face_y(low_far, ylo_ref[:rows_x, cols], low_edge[...])
        high_edge[...] = face_y(high_edge[...], yhi_ref[:rows_x, cols], high_far)

        def row(i):
            if i < 0:
                return jnp.where(has_low, xhalo_ref[i + 2, :, cols], 0.0)
            if i >= rows_x:
                return jnp.where(has_high, xhalo_ref[i - rows_x, :, cols], 0.0)
            return field_ref[i * rows_y : (i + 1) * rows_y, cols]

        near = [row(-2), row(-1), row(0)]
        low, high = near[1] - near[0], near[2] - near[1]
        face = [ax * near[1] + bx * minmod(low, high)]
        for i in range(rows_x + 1):
            near = [near[1], near[2], row(i + 1)]
            low, high = high, near[2] - near[1]
            face.append(ax * near[1] + bx * minmod(low, high))
            if i == 0:
                continue
            x = i - 1
            here = near[0]
            row_term = jnp.where(ahead_x, face[x + 1] - face[x], face[x + 2] - face[x + 1])
            below = jnp.where(first_y, ylo_ref[x : x + 1, cols], pltpu.roll(here, 1, 0))
            above = jnp.where(last_y, yhi_ref[x : x + 1, cols], pltpu.roll(here, rows_y - 1, 0))
            mine = face_y(below, here, above)
            mine_below = jnp.where(first_y, low_edge[x : x + 1], pltpu.roll(mine, 1, 0))
            mine_above = jnp.where(last_y, high_edge[x : x + 1], pltpu.roll(mine, rows_y - 1, 0))
            col_term = jnp.where(ahead_y, mine - mine_below, mine_above - mine)
            moved = here - row_term - col_term
            at = slice(x * rows_y, (x + 1) * rows_y)
            adv_ref[at, cols] = moved
            for part in range(wide // (2 * LANES)):
                first = 2 * part * LANES
                both = folded(moved[:, first : first + LANES], moved[:, first + LANES : first + 2 * LANES], even, turned)
                to = pl.ds(pl.multiple_of(c * (wide // 2) + part * LANES, LANES), LANES)
                fold_ref[0, at, to], fold_ref[1, at, to] = both
        return carry

    lax.fori_loop(0, local_len // wide, chunk, 0)


def transport(here, rows_x, field, xhalo, ylo, yhi, entries):
    cells, local_len = field.shape
    wide = 4 * LANES
    return pl.pallas_call(
        functools.partial(transport_body, wide, rows_x),
        in_specs=[SCALARS] + [WHOLE] * (4 + len(entries)),
        out_specs=[WHOLE] * 2,
        out_shape=[pltpu.VMEM(field.shape, jnp.float32), pltpu.VMEM((2, cells, local_len // 2), jnp.float32)],
        scratch_shapes=[pltpu.VMEM((rows_x, wide), jnp.float32)] * 2,
        compiler_params=room(4),
        cost_estimate=pl.CostEstimate(flops=40 * cells * local_len, bytes_accessed=16 * cells * local_len, transcendentals=0),
        name="transport",
    )(here, in_vmem(field), in_vmem(xhalo), in_vmem(ylo), in_vmem(yhi), *map(in_vmem, entries))


def split_into(value_ref, high, low):
    for parity in range(2):
        value = value_ref[parity]
        rounded = value.astype(jnp.bfloat16)
        high[parity] = rounded
        low[parity] = (value - rounded.astype(jnp.float32)).astype(jnp.bfloat16)


def product(high, low, hi_ref, lo_ref, source, parity, cols):
    dot = functools.partial(jnp.dot, preferred_element_type=jnp.float32)
    tile = hi_ref[source, parity, :, cols]
    return dot(high[parity], tile) + (dot(low[parity], tile) + dot(high[parity], lo_ref[source, parity, :, cols]))


def own_body(wide, fold_ref, hi_ref, lo_ref, out_ref, high, low):
    split_into(fold_ref, high, low)
    for j in range(fold_ref.shape[2] // wide):
        cols = slice(j * wide, (j + 1) * wide)
        for parity in range(2):
            out_ref[parity, :, cols] = product(high, low, hi_ref, lo_ref, 0, parity, cols)


def own_gain(fold, entries):
    _, cells, size = fold.shape
    return pl.pallas_call(
        functools.partial(own_body, 2 * LANES),
        in_specs=[WHOLE] * 3,
        out_specs=WHOLE,
        out_shape=pltpu.VMEM(fold.shape, jnp.float32),
        scratch_shapes=[pltpu.VMEM(fold.shape, jnp.bfloat16)] * 2,
        compiler_params=room(8),
        cost_estimate=pl.CostEstimate(flops=12 * cells * size * size, bytes_accessed=8 * size * size + 16 * cells * size, transcendentals=0),
        name="own_gain",
    )(in_vmem(fold), *map(in_vmem, entries))


def collide_body(
    wide, rows_x, last, here_ref, fold_ref, hi_ref, lo_ref, part_ref, adv_ref, density_ref, type_ref, inflow_ref, *rest
):
    if last:
        out_ref, high, low, field, sems = rest
    else:
        field, up_ref, down_ref, xsend_ref, high, low, far_ref = rest
    cells, local_len = adv_ref.shape
    rows_y = cells // rows_x
    split_into(fold_ref, high, low)
    even_slot, turned = fold_masks(cells)
    rate = jnp.broadcast_to(collision_rate * density_ref[...], (cells, LANES))
    gain_rate = rate * ENTRY_SCALE
    kind = jnp.broadcast_to(type_ref[...], (cells, LANES))
    wall = kind == 1
    inlet = kind == 2
    copies = []
    for j in range(local_len // (2 * wide)):
        cols = slice(j * wide, (j + 1) * wide)
        even, odd = (part_ref[p, :, cols] + product(high, low, hi_ref, lo_ref, 1, p, cols) for p in range(2))
        lower = even + odd
        upper = even - odd
        for part in range(wide // LANES):
            group = slice(part * LANES, (part + 1) * LANES)
            for side, gain in enumerate(unfolded(lower[:, group], upper[:, group], even_slot, turned)):
                first = 2 * (j * wide + part * LANES) + side * LANES
                at = slice(first, first + LANES)
                vx, vy = velocity_parts(here_ref[0] * local_len + first + iota((1, LANES), 1))
                nu = 1.0 + (vx * vx + vy * vy) / 8.0
                moved = adv_ref[:, at]
                done = moved + (gain_rate * gain - rate * (nu * moved))
                field[:, at] = jnp.where(wall, 0.0, jnp.where(inlet, inflow_ref[:, at], done))
        span = slice(2 * j * wide, 2 * (j + 1) * wide)
        if last:
            copy = pltpu.make_async_copy(field.at[:, span], out_ref.at[:, span], sems.at[j])
            copy.start()
            copies.append(copy)
        else:
            write_edges(here_ref, rows_x, field, span, up_ref, down_ref, xsend_ref, far_ref)
    for copy in copies:
        copy.wait()


def collide(here, rows_x, fold, entries, part, advected, density, kind, inflow, last):
    _, cells, size = fold.shape
    local_len = advected.shape[1]
    wide = 2 * LANES
    halves = [pltpu.VMEM(fold.shape, jnp.bfloat16)] * 2
    if last:
        out_specs = pl.BlockSpec(memory_space=pl.ANY)
        out_shape = jax.ShapeDtypeStruct(advected.shape, jnp.float32)
        scratch = halves + [pltpu.VMEM(advected.shape, jnp.float32), pltpu.SemaphoreType.DMA((size // wide,))]
    else:
        out_specs = [WHOLE] * 4
        out_shape = [pltpu.VMEM(advected.shape, jnp.float32)] + edge_shapes(rows_x, cells // rows_x, local_len)
        scratch = halves + [pltpu.VMEM((rows_x, local_len), jnp.float32)]
    return pl.pallas_call(
        functools.partial(collide_body, wide, rows_x, last),
        in_specs=[SCALARS] + [WHOLE] * 8,
        out_specs=out_specs,
        out_shape=out_shape,
        scratch_shapes=scratch,
        compiler_params=room(12),
        cost_estimate=pl.CostEstimate(flops=12 * cells * size * size, bytes_accessed=8 * size * size + 32 * cells * size, transcendentals=0),
        name="collide",
    )(here, in_vmem(fold), in_vmem(entries[0]), in_vmem(entries[1]), in_vmem(part), in_vmem(advected), density, kind, inflow)


def shifted(block, axis, by):
    count = lax.axis_size(axis)
    return lax.ppermute(block, axis, [(i, i + by) for i in range(count) if 0 <= i + by < count])


def per_device(distribution, density, cell_type, inflow):
    rows_x, rows_y, local_len = distribution.shape
    cells = rows_x * rows_y
    vert = lax.axis_index("vert")
    verts = lax.axis_size("vert")
    at_x = lax.axis_index("gx")
    size_x = lax.axis_size("gx")
    assert size_x == 2 and verts == 2
    here = jnp.stack([vert, jnp.int32(verts), (at_x > 0).astype(jnp.int32), (at_x < size_x - 1).astype(jnp.int32)])
    column_density = density.reshape(cells, 1)
    column_type = cell_type.reshape(cells, 1)
    row_inflow = inflow.reshape(1, local_len)
    swap = [(0, 1), (1, 0)]
    field, up, down, send_x = stage(here, rows_x, distribution.reshape(cells, local_len))
    entries = None
    for step in range(STEPS):
        last = step == STEPS - 1
        ylo = shifted(up, "gy", 1)
        yhi = shifted(down, "gy", -1)
        xhalo = lax.ppermute(send_x, "gx", swap)
        if entries is None:
            entries = make_entries(here, local_len // NVX, verts, [column_density, column_type])
        advected, fold = transport(here, rows_x, field, xhalo, ylo, yhi, entries)
        other = lax.ppermute(fold, "vert", swap)
        part = own_gain(fold, entries)
        out = collide(here, rows_x, other, entries, part, advected, column_density, column_type, row_inflow, last)
        if not last:
            field, up, down, send_x = out
    return out.reshape(rows_x, rows_y, local_len)


def solution(mesh):
    placed = (P("gx", "gy", "vert"), P("gx", "gy"), P("gx", "gy"), P("vert"))
    return jax.shard_map(
        per_device, mesh=mesh, in_specs=placed, out_specs=P("gx", "gy", "vert"), check_vma=False
    )
```

```python
import functools
import math

import jax
import jax.numpy as jnp
from jax import lax
from jax.experimental import pallas as pl
from jax.experimental.pallas import tpu as pltpu
from jax.sharding import PartitionSpec as P

NVX = 64
STEPS = 2
HALF = NVX // 2
LANES = 128
GROUP = LANES // HALF

vel_max = 4.0
time_step = 0.1
grad_scale = 2.5
collision_rate = 0.2
spacing = 2.0 * vel_max / NVX
middle = 0.5 * (NVX - 1)

MIB = 1024 * 1024
WHOLE = pl.BlockSpec(memory_space=pltpu.VMEM)
SCALARS = pl.BlockSpec(memory_space=pltpu.SMEM)

EXPONENT = 0.125 * math.log2(math.e)
ENTRY_SCALE = grad_scale * spacing * spacing * math.sqrt(EXPONENT)


SMALL = pl.CostEstimate(flops=1, bytes_accessed=1, transcendentals=0)


def room(mib):
    return pltpu.CompilerParams(vmem_limit_bytes=mib * MIB)


def in_vmem(value):
    return pltpu.with_memory_space_constraint(value, pltpu.VMEM)


def velocity_parts(index):
    row_portion = (index // NVX).astype(jnp.float32)
    col_part = (index % NVX).astype(jnp.float32)
    vel_x = (row_portion - middle) * spacing
    vel_y = (col_part - middle) * spacing
    return (vel_x, vel_y)


def iota(shape, dim):
    return lax.broadcasted_iota(jnp.int32, shape, dim)


def slot_order(slot):
    return lax.rem(slot, 2) * 2 + lax.div(slot, 2)


def entries_body(local, sources, here_ref, *rest):
    hi_ref, lo_ref, energy_ref, gauss_ref = rest[-4:]
    me = here_ref[0]
    groups = local // GROUP
    rows = 8
    lane = iota((1, LANES), 1)
    slot = slot_order(lane // HALF)
    vy = ((lane % HALF).astype(jnp.float32) - middle) * spacing

    def one(index, carry):
        source = lax.div(index, GROUP)
        r = lax.rem(index, GROUP)
        first = lax.rem(me + source, here_ref[1]) * local
        pair, lanes = iota((groups * groups, LANES), 0), iota((groups * groups, LANES), 1)
        out_x = ((me * local + pair // groups * GROUP + slot_order(lanes // HALF)).astype(jnp.float32) - middle) * spacing
        out_y = ((lanes % HALF).astype(jnp.float32) - middle) * spacing
        in_x = ((first + pair % groups * GROUP + r).astype(jnp.float32) - middle) * spacing
        out_sq, in_sq = out_x * out_x + out_y * out_y, in_x * in_x
        energy_ref[...] = EXPONENT * (out_sq - in_sq)
        gauss_ref[...] = jnp.exp((out_sq + in_sq) * -0.25) * (0.5 / EXPONENT)
        for part in range(HALF // rows):
            wy = ((iota((rows, LANES), 0) + part * rows).astype(jnp.float32) - middle) * spacing
            in_y_sq = EXPONENT * wy * wy
            in_y_gauss = jnp.exp(wy * wy * -0.25)
            dy_same = EXPONENT * ((vy - wy) ** 2 + spacing * spacing)
            dy_flip = EXPONENT * ((vy + wy) ** 2 + spacing * spacing)
            for m in range(1 - groups, groups):
                apart = (me * local - first + m * GROUP - r + slot).astype(jnp.float32) * spacing
                dx_sq = EXPONENT * apart * apart
                same_sq, flip_sq = dx_sq + dy_same, dx_sq + dy_flip
                same_inv, flip_inv = lax.rsqrt(same_sq), lax.rsqrt(flip_sq)
                same_inv_sq, flip_inv_sq = same_inv * same_inv, flip_inv * flip_inv
                same_top, flip_top = jnp.log2(same_inv) - same_sq, jnp.log2(flip_inv) - flip_sq
                same_r, flip_r = same_sq * same_inv, flip_sq * flip_inv
                sum_r, gap_r = same_r + flip_r, same_r - flip_r
                for g in range(max(0, m), min(groups, groups + m)):
                    k = g - m
                    at = g * groups + k
                    energy = energy_ref[at : at + 1, :] - in_y_sq
                    energy_sq = energy * energy
                    gauss = gauss_ref[at : at + 1, :] * in_y_gauss
                    same = jnp.exp2(same_top - energy_sq * same_inv_sq)
                    flip = jnp.exp2(flip_top - energy_sq * flip_inv_sq)
                    to = (k * GROUP + slot_order(r)) * HALF + part * rows
                    to = pl.ds(pl.multiple_of(to, rows), rows)
                    cols = slice(g * LANES, (g + 1) * LANES)
                    values = ((same + flip) - gauss * sum_r, (same - flip) - gauss * gap_r)
                    for parity, value in enumerate(values):
                        high = value.astype(jnp.bfloat16)
                        hi_ref[source, parity, to, cols] = high
                        lo_ref[source, parity, to, cols] = (value - high.astype(jnp.float32)).astype(jnp.bfloat16)
        return carry

    lax.fori_loop(0, sources * GROUP, one, 0)


def make_entries(here, local, sources, ahead_of):
    size = local * HALF
    shape = pltpu.VMEM((sources, 2, size, size), jnp.bfloat16)
    return pl.pallas_call(
        functools.partial(entries_body, local, sources),
        in_specs=[SCALARS] + [WHOLE] * len(ahead_of),
        out_specs=[WHOLE, WHOLE],
        out_shape=[shape, shape],
        scratch_shapes=[pltpu.VMEM(((local // GROUP) ** 2, LANES), jnp.float32)] * 2,
        compiler_params=room(8),
        cost_estimate=SMALL,
        name="kernel_entries",
    )(here, *map(in_vmem, ahead_of))


def pack_far(far, ahead, low_half):
    count = far.shape[0] // 2
    if ahead:
        return jnp.where(low_half, pltpu.roll(far[count:], LANES - HALF, 1), far[:count])
    return jnp.where(low_half, far[:count], pltpu.roll(far[count:], HALF, 1))


def unpack_far(packed, ahead):
    shift = HALF if ahead else LANES - HALF
    parts = [packed[:, i : i + LANES] for i in range(0, packed.shape[1], LANES)]
    turned = jnp.concatenate([pltpu.roll(p, shift, 1) for p in parts], axis=1)
    return jnp.concatenate([packed, turned], axis=0)


def write_edges(here_ref, rows_x, field, span, up_ref, down_ref, xsend_ref, far_ref):
    rows_y = field.shape[0] // rows_x
    for layer in range(2):
        first_row = field[layer * rows_y : (layer + 1) * rows_y, span]
        last_row = field[(rows_x - 2 + layer) * rows_y : (rows_x - 1 + layer) * rows_y, span]
        xsend_ref[layer, :, span] = jnp.where(here_ref[3] > 0, last_row, first_row)
    low_half = iota((rows_x // 2, LANES), 1) % NVX < HALF
    for ahead, to_ref, near, far in ((True, up_ref, rows_y - 1, rows_y - 2), (False, down_ref, 0, 1)):
        for x in range(rows_x):
            to_ref[x : x + 1, span] = field[x * rows_y + near : x * rows_y + near + 1, span]
            far_ref[x : x + 1, span] = field[x * rows_y + far : x * rows_y + far + 1, span]
        for i in range(span.start, span.stop, LANES):
            at = slice(i, i + LANES)
            to_ref[rows_x:, at] = pack_far(far_ref[:, at], ahead, low_half)


def edge_shapes(rows_x, rows_y, local_len):
    edge_y = pltpu.VMEM((rows_x + rows_x // 2, local_len), jnp.float32)
    return [edge_y, edge_y, pltpu.VMEM((2, rows_y, local_len), jnp.float32)]


def stage_body(wide, rows_x, here_ref, from_ref, field, up_ref, down_ref, xsend_ref, far_ref, sems):
    spans = [slice(i, i + wide) for i in range(0, field.shape[1], wide)]
    copies = [pltpu.make_async_copy(from_ref.at[:, s], field.at[:, s], sems.at[i]) for i, s in enumerate(spans)]
    for copy in copies:
        copy.start()
    for copy, span in zip(copies, spans):
        copy.wait()
        write_edges(here_ref, rows_x, field, span, up_ref, down_ref, xsend_ref, far_ref)


def stage(here, rows_x, field):
    cells, local_len = field.shape
    wide = local_len // 4
    return pl.pallas_call(
        functools.partial(stage_body, wide, rows_x),
        in_specs=[SCALARS, pl.BlockSpec(memory_space=pltpu.HBM)],
        out_specs=[WHOLE] * 4,
        out_shape=[pltpu.VMEM(field.shape, jnp.float32)] + edge_shapes(rows_x, cells // rows_x, local_len),
        scratch_shapes=[pltpu.VMEM((rows_x, local_len), jnp.float32), pltpu.SemaphoreType.DMA((4,))],
        compiler_params=room(4),
        name="stage",
    )(here, pltpu.with_memory_space_constraint(field, pltpu.HBM))


def minmod(a, b):
    return jnp.maximum(jnp.minimum(a, b), 0.0) + jnp.minimum(jnp.maximum(a, b), 0.0)


def fold_masks(rows):
    lane = iota((rows, LANES), 1)
    slot = lane // HALF
    even = slot % 2 == 0
    turned = jnp.where(even, 2 - slot, slot) * HALF + (HALF - 1) - lane % HALF
    return even, turned


def folded(a, b, even, turned):
    near = jnp.where(even, a, b)
    far = pltpu.roll(jnp.where(even, b, a), HALF, 1)
    lower = jnp.where(even, near, far)
    upper = jnp.take_along_axis(jnp.where(even, far, near), turned, axis=1)
    return lower + upper, lower - upper


def unfolded(lower, upper, even, turned):
    upper = jnp.take_along_axis(upper, turned, axis=1)
    near = jnp.where(even, lower, upper)
    far = pltpu.roll(jnp.where(even, upper, lower), LANES - HALF, 1)
    return jnp.where(even, near, far), jnp.where(even, far, near)


def transport_body(wide, rows_x, here_ref, field_ref, xhalo_ref, ylo_ref, yhi_ref, *rest):
    adv_ref, fold_ref, low_edge, high_edge = rest[-4:]
    cells, local_len = field_ref.shape
    rows_y = cells // rows_x
    has_low = here_ref[2] > 0
    has_high = here_ref[3] > 0
    at_y = iota((rows_y, wide), 0)
    first_y = at_y == 0
    last_y = at_y == rows_y - 1
    even, turned = fold_masks(rows_y)

    def chunk(c, carry):
        cols = pl.ds(pl.multiple_of(c * wide, wide), wide)
        vx, vy = velocity_parts(here_ref[0] * local_len + c * wide + iota((1, wide), 1))
        ax = time_step * vx
        ay = time_step * vy
        bx = 0.5 * jnp.abs(ax) * (1.0 - jnp.abs(ax))
        by = 0.5 * jnp.abs(ay) * (1.0 - jnp.abs(ay))
        ahead_x = ax > 0
        ahead_y = ay > 0

        def face_y(f0, f1, f2):
            return ay * f1 + by * minmod(f1 - f0, f2 - f1)

        for x in range(rows_x):
            low_edge[x : x + 1] = field_ref[x * rows_y : x * rows_y + 1, cols]
            high_edge[x : x + 1] = field_ref[(x + 1) * rows_y - 1 : (x + 1) * rows_y, cols]
        low_far = unpack_far(ylo_ref[rows_x:, cols], True)
        high_far = unpack_far(yhi_ref[rows_x:, cols], False)
        low_edge[...] = face_y(low_far, ylo_ref[:rows_x, cols], low_edge[...])
        high_edge[...] = face_y(high_edge[...], yhi_ref[:rows_x, cols], high_far)

        def row(i):
            if i < 0:
                return jnp.where(has_low, xhalo_ref[i + 2, :, cols], 0.0)
            if i >= rows_x:
                return jnp.where(has_high, xhalo_ref[i - rows_x, :, cols], 0.0)
            return field_ref[i * rows_y : (i + 1) * rows_y, cols]

        near = [row(-2), row(-1), row(0)]
        low, high = near[1] - near[0], near[2] - near[1]
        face = [ax * near[1] + bx * minmod(low, high)]
        for i in range(rows_x + 1):
            near = [near[1], near[2], row(i + 1)]
            low, high = high, near[2] - near[1]
            face.append(ax * near[1] + bx * minmod(low, high))
            if i == 0:
                continue
            x = i - 1
            here = near[0]
            row_term = jnp.where(ahead_x, face[x + 1] - face[x], face[x + 2] - face[x + 1])
            below = jnp.where(first_y, ylo_ref[x : x + 1, cols], pltpu.roll(here, 1, 0))
            above = jnp.where(last_y, yhi_ref[x : x + 1, cols], pltpu.roll(here, rows_y - 1, 0))
            mine = face_y(below, here, above)
            mine_below = jnp.where(first_y, low_edge[x : x + 1], pltpu.roll(mine, 1, 0))
            mine_above = jnp.where(last_y, high_edge[x : x + 1], pltpu.roll(mine, rows_y - 1, 0))
            col_term = jnp.where(ahead_y, mine - mine_below, mine_above - mine)
            moved = here - row_term - col_term
            at = slice(x * rows_y, (x + 1) * rows_y)
            adv_ref[at, cols] = moved
            for part in range(wide // (2 * LANES)):
                first = 2 * part * LANES
                both = folded(moved[:, first : first + LANES], moved[:, first + LANES : first + 2 * LANES], even, turned)
                to = pl.ds(pl.multiple_of(c * (wide // 2) + part * LANES, LANES), LANES)
                fold_ref[0, at, to], fold_ref[1, at, to] = both
        return carry

    lax.fori_loop(0, local_len // wide, chunk, 0)


def transport(here, rows_x, field, xhalo, ylo, yhi, entries):
    cells, local_len = field.shape
    wide = 4 * LANES
    return pl.pallas_call(
        functools.partial(transport_body, wide, rows_x),
        in_specs=[SCALARS] + [WHOLE] * (4 + len(entries)),
        out_specs=[WHOLE] * 2,
        out_shape=[pltpu.VMEM(field.shape, jnp.float32), pltpu.VMEM((2, cells, local_len // 2), jnp.float32)],
        scratch_shapes=[pltpu.VMEM((rows_x, wide), jnp.float32)] * 2,
        compiler_params=room(4),
        cost_estimate=SMALL,
        name="transport",
    )(here, in_vmem(field), in_vmem(xhalo), in_vmem(ylo), in_vmem(yhi), *map(in_vmem, entries))


def split_into(value_ref, high, low):
    for parity in range(2):
        value = value_ref[parity]
        rounded = value.astype(jnp.bfloat16)
        high[parity] = rounded
        low[parity] = (value - rounded.astype(jnp.float32)).astype(jnp.bfloat16)


def product(high, low, hi_ref, lo_ref, source, parity, cols):
    dot = functools.partial(jnp.dot, preferred_element_type=jnp.float32)
    tile = hi_ref[source, parity, :, cols]
    return dot(high[parity], tile) + (dot(low[parity], tile) + dot(high[parity], lo_ref[source, parity, :, cols]))


def own_body(wide, fold_ref, hi_ref, lo_ref, out_ref, high, low):
    split_into(fold_ref, high, low)
    for j in range(fold_ref.shape[2] // wide):
        cols = slice(j * wide, (j + 1) * wide)
        for parity in range(2):
            out_ref[parity, :, cols] = product(high, low, hi_ref, lo_ref, 0, parity, cols)


def own_gain(fold, entries):
    _, cells, size = fold.shape
    return pl.pallas_call(
        functools.partial(own_body, 2 * LANES),
        in_specs=[WHOLE] * 3,
        out_specs=WHOLE,
        out_shape=pltpu.VMEM(fold.shape, jnp.float32),
        scratch_shapes=[pltpu.VMEM(fold.shape, jnp.bfloat16)] * 2,
        compiler_params=room(8),
        cost_estimate=SMALL,
        name="own_gain",
    )(in_vmem(fold), *map(in_vmem, entries))


def collide_body(
    wide, rows_x, last, here_ref, fold_ref, hi_ref, lo_ref, part_ref, adv_ref, density_ref, type_ref, inflow_ref, *rest
):
    if last:
        out_ref, high, low, field, sems = rest
    else:
        field, up_ref, down_ref, xsend_ref, high, low, far_ref = rest
    cells, local_len = adv_ref.shape
    rows_y = cells // rows_x
    split_into(fold_ref, high, low)
    even_slot, turned = fold_masks(cells)
    rate = jnp.broadcast_to(collision_rate * density_ref[...], (cells, LANES))
    gain_rate = rate * ENTRY_SCALE
    kind = jnp.broadcast_to(type_ref[...], (cells, LANES))
    wall = kind == 1
    inlet = kind == 2
    copies = []
    for j in range(local_len // (2 * wide)):
        cols = slice(j * wide, (j + 1) * wide)
        even, odd = (part_ref[p, :, cols] + product(high, low, hi_ref, lo_ref, 1, p, cols) for p in range(2))
        lower = even + odd
        upper = even - odd
        for part in range(wide // LANES):
            group = slice(part * LANES, (part + 1) * LANES)
            for side, gain in enumerate(unfolded(lower[:, group], upper[:, group], even_slot, turned)):
                first = 2 * (j * wide + part * LANES) + side * LANES
                at = slice(first, first + LANES)
                vx, vy = velocity_parts(here_ref[0] * local_len + first + iota((1, LANES), 1))
                nu = 1.0 + (vx * vx + vy * vy) / 8.0
                moved = adv_ref[:, at]
                done = moved + (gain_rate * gain - rate * (nu * moved))
                field[:, at] = jnp.where(wall, 0.0, jnp.where(inlet, inflow_ref[:, at], done))
        span = slice(2 * j * wide, 2 * (j + 1) * wide)
        if last:
            copy = pltpu.make_async_copy(field.at[:, span], out_ref.at[:, span], sems.at[j])
            copy.start()
            copies.append(copy)
        else:
            write_edges(here_ref, rows_x, field, span, up_ref, down_ref, xsend_ref, far_ref)
    for copy in copies:
        copy.wait()


def collide(here, rows_x, fold, entries, part, advected, density, kind, inflow, last):
    _, cells, size = fold.shape
    local_len = advected.shape[1]
    wide = 2 * LANES
    halves = [pltpu.VMEM(fold.shape, jnp.bfloat16)] * 2
    if last:
        out_specs = pl.BlockSpec(memory_space=pl.ANY)
        out_shape = jax.ShapeDtypeStruct(advected.shape, jnp.float32)
        scratch = halves + [pltpu.VMEM(advected.shape, jnp.float32), pltpu.SemaphoreType.DMA((size // wide,))]
    else:
        out_specs = [WHOLE] * 4
        out_shape = [pltpu.VMEM(advected.shape, jnp.float32)] + edge_shapes(rows_x, cells // rows_x, local_len)
        scratch = halves + [pltpu.VMEM((rows_x, local_len), jnp.float32)]
    return pl.pallas_call(
        functools.partial(collide_body, wide, rows_x, last),
        in_specs=[SCALARS] + [WHOLE] * 8,
        out_specs=out_specs,
        out_shape=out_shape,
        scratch_shapes=scratch,
        compiler_params=room(12),
        cost_estimate=SMALL,
        name="collide",
    )(here, in_vmem(fold), in_vmem(entries[0]), in_vmem(entries[1]), in_vmem(part), in_vmem(advected), density, kind, inflow)


def shifted(block, axis, by):
    count = lax.axis_size(axis)
    return lax.ppermute(block, axis, [(i, i + by) for i in range(count) if 0 <= i + by < count])


def per_device(distribution, density, cell_type, inflow):
    rows_x, rows_y, local_len = distribution.shape
    cells = rows_x * rows_y
    vert = lax.axis_index("vert")
    verts = lax.axis_size("vert")
    at_x = lax.axis_index("gx")
    size_x = lax.axis_size("gx")
    assert size_x == 2 and verts == 2
    here = jnp.stack([vert, jnp.int32(verts), (at_x > 0).astype(jnp.int32), (at_x < size_x - 1).astype(jnp.int32)])
    column_density = density.reshape(cells, 1)
    column_type = cell_type.reshape(cells, 1)
    row_inflow = inflow.reshape(1, local_len)
    swap = [(0, 1), (1, 0)]
    field, up, down, send_x = stage(here, rows_x, distribution.reshape(cells, local_len))
    entries = None
    for step in range(STEPS):
        last = step == STEPS - 1
        ylo = shifted(up, "gy", 1)
        yhi = shifted(down, "gy", -1)
        xhalo = lax.ppermute(send_x, "gx", swap)
        if entries is None:
            entries = make_entries(here, local_len // NVX, verts, [column_density, column_type])
        advected, fold = transport(here, rows_x, field, xhalo, ylo, yhi, entries)
        other = lax.ppermute(fold, "vert", swap)
        part = own_gain(fold, entries)
        out = collide(here, rows_x, other, entries, part, advected, column_density, column_type, row_inflow, last)
        if not last:
            field, up, down, send_x = out
    return out.reshape(rows_x, rows_y, local_len)


def solution(mesh):
    placed = (P("gx", "gy", "vert"), P("gx", "gy"), P("gx", "gy"), P("vert"))
    return jax.shard_map(
        per_device, mesh=mesh, in_specs=placed, out_specs=P("gx", "gy", "vert"), check_vma=False
    )
```

```python
import functools
import math

import jax
import jax.numpy as jnp
from jax import lax
from jax.experimental import pallas as pl
from jax.experimental.pallas import tpu as pltpu
from jax.sharding import PartitionSpec as P

NVX = 64
STEPS = 2
HALF = NVX // 2
LANES = 128
GROUP = LANES // HALF

vel_max = 4.0
time_step = 0.1
grad_scale = 2.5
collision_rate = 0.2
spacing = 2.0 * vel_max / NVX
middle = 0.5 * (NVX - 1)

MIB = 1024 * 1024
WHOLE = pl.BlockSpec(memory_space=pltpu.VMEM)
SCALARS = pl.BlockSpec(memory_space=pltpu.SMEM)

EXPONENT = 0.125 * math.log2(math.e)
ENTRY_SCALE = grad_scale * spacing * spacing * math.sqrt(EXPONENT)


SMALL = pl.CostEstimate(flops=1, bytes_accessed=1, transcendentals=0)


def room(mib):
    return pltpu.CompilerParams(vmem_limit_bytes=mib * MIB)


def in_vmem(value):
    return pltpu.with_memory_space_constraint(value, pltpu.VMEM)


def velocity_parts(index):
    row_portion = (index // NVX).astype(jnp.float32)
    col_part = (index % NVX).astype(jnp.float32)
    vel_x = (row_portion - middle) * spacing
    vel_y = (col_part - middle) * spacing
    return (vel_x, vel_y)


def iota(shape, dim):
    return lax.broadcasted_iota(jnp.int32, shape, dim)


def slot_order(slot):
    return lax.rem(slot, 2) * 2 + lax.div(slot, 2)


def entries_body(local, sources, here_ref, *rest):
    hi_ref, lo_ref, energy_ref, gauss_ref = rest[-4:]
    me = here_ref[0]
    groups = local // GROUP
    rows = 8
    lane = iota((1, LANES), 1)
    slot = slot_order(lane // HALF)
    vy = ((lane % HALF).astype(jnp.float32) - middle) * spacing

    def one(index, carry):
        source = lax.div(index, GROUP)
        r = lax.rem(index, GROUP)
        first = lax.rem(me + source, here_ref[1]) * local
        pair, lanes = iota((groups * groups, LANES), 0), iota((groups * groups, LANES), 1)
        out_x = ((me * local + pair // groups * GROUP + slot_order(lanes // HALF)).astype(jnp.float32) - middle) * spacing
        out_y = ((lanes % HALF).astype(jnp.float32) - middle) * spacing
        in_x = ((first + pair % groups * GROUP + r).astype(jnp.float32) - middle) * spacing
        out_sq, in_sq = out_x * out_x + out_y * out_y, in_x * in_x
        energy_ref[...] = EXPONENT * (out_sq - in_sq)
        gauss_ref[...] = jnp.exp((out_sq + in_sq) * -0.25) * (0.5 / EXPONENT)
        for part in range(HALF // rows):
            wy = ((iota((rows, LANES), 0) + part * rows).astype(jnp.float32) - middle) * spacing
            in_y_sq = EXPONENT * wy * wy
            in_y_gauss = jnp.exp(wy * wy * -0.25)
            dy_same = EXPONENT * ((vy - wy) ** 2 + spacing * spacing)
            dy_flip = EXPONENT * ((vy + wy) ** 2 + spacing * spacing)
            for m in range(1 - groups, groups):
                apart = (me * local - first + m * GROUP - r + slot).astype(jnp.float32) * spacing
                dx_sq = EXPONENT * apart * apart
                same_sq, flip_sq = dx_sq + dy_same, dx_sq + dy_flip
                same_inv, flip_inv = lax.rsqrt(same_sq), lax.rsqrt(flip_sq)
                same_inv_sq, flip_inv_sq = same_inv * same_inv, flip_inv * flip_inv
                same_top, flip_top = jnp.log2(same_inv) - same_sq, jnp.log2(flip_inv) - flip_sq
                same_r, flip_r = same_sq * same_inv, flip_sq * flip_inv
                sum_r, gap_r = same_r + flip_r, same_r - flip_r
                for g in range(max(0, m), min(groups, groups + m)):
                    k = g - m
                    at = g * groups + k
                    energy = energy_ref[at : at + 1, :] - in_y_sq
                    energy_sq = energy * energy
                    gauss = gauss_ref[at : at + 1, :] * in_y_gauss
                    same = jnp.exp2(same_top - energy_sq * same_inv_sq)
                    flip = jnp.exp2(flip_top - energy_sq * flip_inv_sq)
                    to = (k * GROUP + slot_order(r)) * HALF + part * rows
                    to = pl.ds(pl.multiple_of(to, rows), rows)
                    cols = slice(g * LANES, (g + 1) * LANES)
                    values = ((same + flip) - gauss * sum_r, (same - flip) - gauss * gap_r)
                    for parity, value in enumerate(values):
                        high = value.astype(jnp.bfloat16)
                        hi_ref[source, parity, to, cols] = high
                        lo_ref[source, parity, to, cols] = (value - high.astype(jnp.float32)).astype(jnp.bfloat16)
        return carry

    lax.fori_loop(0, sources * GROUP, one, 0)


def make_entries(here, local, sources, ahead_of):
    size = local * HALF
    shape = pltpu.VMEM((sources, 2, size, size), jnp.bfloat16)
    return pl.pallas_call(
        functools.partial(entries_body, local, sources),
        in_specs=[SCALARS] + [WHOLE] * len(ahead_of),
        out_specs=[WHOLE, WHOLE],
        out_shape=[shape, shape],
        scratch_shapes=[pltpu.VMEM(((local // GROUP) ** 2, LANES), jnp.float32)] * 2,
        compiler_params=room(8),
        cost_estimate=SMALL,
        name="kernel_entries",
    )(here, *map(in_vmem, ahead_of))


def pack_far(far, ahead, low_half):
    count = far.shape[0] // 2
    if ahead:
        return jnp.where(low_half, pltpu.roll(far[count:], LANES - HALF, 1), far[:count])
    return jnp.where(low_half, far[:count], pltpu.roll(far[count:], HALF, 1))


def unpack_far(packed, ahead):
    shift = HALF if ahead else LANES - HALF
    parts = [packed[:, i : i + LANES] for i in range(0, packed.shape[1], LANES)]
    turned = jnp.concatenate([pltpu.roll(p, shift, 1) for p in parts], axis=1)
    return jnp.concatenate([packed, turned], axis=0)


def write_edges(here_ref, rows_x, field, span, up_ref, down_ref, xsend_ref, far_ref):
    rows_y = field.shape[0] // rows_x
    for layer in range(2):
        first_row = field[layer * rows_y : (layer + 1) * rows_y, span]
        last_row = field[(rows_x - 2 + layer) * rows_y : (rows_x - 1 + layer) * rows_y, span]
        xsend_ref[layer, :, span] = jnp.where(here_ref[3] > 0, last_row, first_row)
    low_half = iota((rows_x // 2, LANES), 1) % NVX < HALF
    for ahead, to_ref, near, far in ((True, up_ref, rows_y - 1, rows_y - 2), (False, down_ref, 0, 1)):
        side = 1 if ahead else 0
        for x in range(rows_x):
            to_ref[x : x + 1, span] = field[x * rows_y + near : x * rows_y + near + 1, span]
            far_ref[side, x : x + 1, span] = field[x * rows_y + far : x * rows_y + far + 1, span]
        for i in range(span.start, span.stop, LANES):
            at = slice(i, i + LANES)
            to_ref[rows_x:, at] = pack_far(far_ref[side, :, at], ahead, low_half)


def edge_shapes(rows_x, rows_y, local_len):
    edge_y = pltpu.VMEM((rows_x + rows_x // 2, local_len), jnp.float32)
    layers_x = pltpu.VMEM((2, rows_y, local_len), jnp.float32)
    return [edge_y, edge_y, layers_x, pltpu.VMEM((2, rows_x, local_len), jnp.float32)]


def stage_body(wide, rows_x, here_ref, from_ref, field, up_ref, down_ref, xsend_ref, far_ref, sems):
    spans = [slice(i, i + wide) for i in range(0, field.shape[1], wide)]
    copies = [pltpu.make_async_copy(from_ref.at[:, s], field.at[:, s], sems.at[i]) for i, s in enumerate(spans)]
    for copy in copies:
        copy.start()
    for copy, span in zip(copies, spans):
        copy.wait()
        write_edges(here_ref, rows_x, field, span, up_ref, down_ref, xsend_ref, far_ref)


def stage(here, rows_x, field):
    cells, local_len = field.shape
    wide = local_len // 4
    return pl.pallas_call(
        functools.partial(stage_body, wide, rows_x),
        in_specs=[SCALARS, pl.BlockSpec(memory_space=pltpu.HBM)],
        out_specs=[WHOLE] * 5,
        out_shape=[pltpu.VMEM(field.shape, jnp.float32)] + edge_shapes(rows_x, cells // rows_x, local_len),
        scratch_shapes=[pltpu.SemaphoreType.DMA((4,))],
        compiler_params=room(4),
        name="stage",
    )(here, pltpu.with_memory_space_constraint(field, pltpu.HBM))


def minmod(a, b):
    return jnp.maximum(jnp.minimum(a, b), 0.0) + jnp.minimum(jnp.maximum(a, b), 0.0)


def fold_masks(rows):
    lane = iota((rows, LANES), 1)
    slot = lane // HALF
    even = slot % 2 == 0
    turned = jnp.where(even, 2 - slot, slot) * HALF + (HALF - 1) - lane % HALF
    return even, turned


def folded(a, b, even, turned):
    near = jnp.where(even, a, b)
    far = pltpu.roll(jnp.where(even, b, a), HALF, 1)
    lower = jnp.where(even, near, far)
    upper = jnp.take_along_axis(jnp.where(even, far, near), turned, axis=1)
    return lower + upper, lower - upper


def unfolded(lower, upper, even, turned):
    upper = jnp.take_along_axis(upper, turned, axis=1)
    near = jnp.where(even, lower, upper)
    far = pltpu.roll(jnp.where(even, upper, lower), LANES - HALF, 1)
    return jnp.where(even, near, far), jnp.where(even, far, near)


def transport_body(wide, rows_x, whole, here_ref, field_ref, xhalo_ref, *rest):
    if whole:
        ylo_ref, yhi_ref = rest[:2]
        adv_ref, fold_ref, low_edge, high_edge = rest[-4:]
    else:
        adv_ref, fold_ref = rest[-2:]
    cells, local_len = field_ref.shape
    rows_y = cells // rows_x
    has_low = here_ref[2] > 0
    has_high = here_ref[3] > 0
    at_y = iota((rows_y, wide), 0)
    first_y = at_y == 0
    last_y = at_y == rows_y - 1
    even, turned = fold_masks(rows_y)

    def chunk(c, carry):
        cols = pl.ds(pl.multiple_of(c * wide, wide), wide)
        vx, vy = velocity_parts(here_ref[0] * local_len + c * wide + iota((1, wide), 1))
        ax = time_step * vx
        ay = time_step * vy
        bx = 0.5 * jnp.abs(ax) * (1.0 - jnp.abs(ax))
        by = 0.5 * jnp.abs(ay) * (1.0 - jnp.abs(ay))
        ahead_x = ax > 0
        ahead_y = ay > 0

        def face_y(f0, f1, f2):
            return ay * f1 + by * minmod(f1 - f0, f2 - f1)

        if whole:
            for x in range(rows_x):
                low_edge[x : x + 1] = field_ref[x * rows_y : x * rows_y + 1, cols]
                high_edge[x : x + 1] = field_ref[(x + 1) * rows_y - 1 : (x + 1) * rows_y, cols]
            low_far = unpack_far(ylo_ref[rows_x:, cols], True)
            high_far = unpack_far(yhi_ref[rows_x:, cols], False)
            low_edge[...] = face_y(low_far, ylo_ref[:rows_x, cols], low_edge[...])
            high_edge[...] = face_y(high_edge[...], yhi_ref[:rows_x, cols], high_far)

        def row(i):
            if i < 0:
                return jnp.where(has_low, xhalo_ref[i + 2, :, cols], 0.0)
            if i >= rows_x:
                return jnp.where(has_high, xhalo_ref[i - rows_x, :, cols], 0.0)
            return field_ref[i * rows_y : (i + 1) * rows_y, cols]

        near = [row(-2), row(-1), row(0)]
        low, high = near[1] - near[0], near[2] - near[1]
        face = [ax * near[1] + bx * minmod(low, high)]
        for i in range(rows_x + 1):
            near = [near[1], near[2], row(i + 1)]
            low, high = high, near[2] - near[1]
            face.append(ax * near[1] + bx * minmod(low, high))
            if i == 0:
                continue
            x = i - 1
            here = near[0]
            row_term = jnp.where(ahead_x, face[x + 1] - face[x], face[x + 2] - face[x + 1])
            below, above = pltpu.roll(here, 1, 0), pltpu.roll(here, rows_y - 1, 0)
            if whole:
                below = jnp.where(first_y, ylo_ref[x : x + 1, cols], below)
                above = jnp.where(last_y, yhi_ref[x : x + 1, cols], above)
            mine = face_y(below, here, above)
            if not whole:
                mine = jnp.where(first_y | last_y, 0.0, mine)
            mine_below, mine_above = pltpu.roll(mine, 1, 0), pltpu.roll(mine, rows_y - 1, 0)
            if whole:
                mine_below = jnp.where(first_y, low_edge[x : x + 1], mine_below)
                mine_above = jnp.where(last_y, high_edge[x : x + 1], mine_above)
            col_term = jnp.where(ahead_y, mine - mine_below, mine_above - mine)
            moved = here - row_term - col_term
            at = slice(x * rows_y, (x + 1) * rows_y)
            adv_ref[at, cols] = moved
            for part in range(wide // (2 * LANES)):
                first = 2 * part * LANES
                both = folded(moved[:, first : first + LANES], moved[:, first + LANES : first + 2 * LANES], even, turned)
                to = pl.ds(pl.multiple_of(c * (wide // 2) + part * LANES, LANES), LANES)
                fold_ref[0, at, to], fold_ref[1, at, to] = both
        return carry

    lax.fori_loop(0, local_len // wide, chunk, 0)


def columns_body(wide, rows_x, here_ref, up_ref, down_ref, far_ref, ylo_ref, yhi_ref, adv_in, fold_in, *rest):
    adv_ref, fold_ref, added, added_fold = rest[-4:]
    cells, local_len = adv_in.shape
    rows_y = cells // rows_x
    half = rows_y // 2
    masks = fold_masks(rows_x)

    def chunk(c, carry):
        cols = pl.ds(pl.multiple_of(c * wide, wide), wide)
        fold_cols = pl.ds(pl.multiple_of(c * (wide // 2), wide // 2), wide // 2)
        _, vy = velocity_parts(here_ref[0] * local_len + c * wide + iota((1, wide), 1))
        ay = time_step * vy
        by = 0.5 * jnp.abs(ay) * (1.0 - jnp.abs(ay))
        ahead = ay > 0

        def face(f0, f1, f2):
            return ay * f1 + by * minmod(f1 - f0, f2 - f1)

        low_near, low = ylo_ref[:rows_x, cols], down_ref[:rows_x, cols]
        high, high_near = up_ref[:rows_x, cols], yhi_ref[:rows_x, cols]
        before = face(unpack_far(ylo_ref[rows_x:, cols], True), low_near, low)
        first = face(low_near, low, far_ref[0, :, cols])
        last = face(far_ref[1, :, cols], high, high_near)
        after = face(high, high_near, unpack_far(yhi_ref[rows_x:, cols], False))
        parts = [
            jnp.where(ahead, before - first, first),
            jnp.where(ahead, first, 0.0),
            jnp.where(ahead, 0.0, -last),
            jnp.where(ahead, -last, last - after),
        ]
        for i, part in enumerate(parts):
            at = slice(i * rows_x, (i + 1) * rows_x)
            added[at] = part
            for j in range(0, wide, 2 * LANES):
                both = folded(part[:, j : j + LANES], part[:, j + LANES : j + 2 * LANES], *masks)
                for parity in range(2):
                    added_fold[parity, at, j // 2 : j // 2 + LANES] = both[parity]

        def spread(ref, x, upper, at_y):
            i = 2 if upper else 0
            first, second = (ref[(i + k) * rows_x + x : (i + k) * rows_x + x + 1, :] for k in range(2))
            place = half - 2 if upper else 0
            return jnp.where(at_y == place, first, jnp.where(at_y == place + 1, second, 0.0))

        at_y = iota((half, wide), 0)
        at_y_fold = iota((half, wide // 2), 0)
        for x in range(rows_x):
            for upper in range(2):
                rows = slice(x * rows_y + upper * half, x * rows_y + (upper + 1) * half)
                adv_ref[rows, cols] = adv_in[rows, cols] + spread(added, x, upper, at_y)
                for parity in range(2):
                    more = spread(added_fold.at[parity], x, upper, at_y_fold)
                    fold_ref[parity, rows, fold_cols] = fold_in[parity, rows, fold_cols] + more
        return carry

    lax.fori_loop(0, local_len // wide, chunk, 0)


def transport(here, rows_x, field, xhalo, yhalos, entries):
    cells, local_len = field.shape
    wide = 4 * LANES
    return pl.pallas_call(
        functools.partial(transport_body, wide, rows_x, bool(yhalos)),
        in_specs=[SCALARS] + [WHOLE] * (2 + len(yhalos) + len(entries)),
        out_specs=[WHOLE] * 2,
        out_shape=[pltpu.VMEM(field.shape, jnp.float32), pltpu.VMEM((2, cells, local_len // 2), jnp.float32)],
        scratch_shapes=[pltpu.VMEM((rows_x, wide), jnp.float32)] * (2 if yhalos else 0),
        compiler_params=room(4),
        cost_estimate=SMALL,
        name="transport" if yhalos else "inner_transport",
    )(here, *map(in_vmem, (field, xhalo, *yhalos, *entries)))


def add_columns(here, rows_x, up, down, far, ylo, yhi, advected, fold, entries):
    wide = 4 * LANES
    return pl.pallas_call(
        functools.partial(columns_body, wide, rows_x),
        in_specs=[SCALARS] + [WHOLE] * (7 + len(entries)),
        out_specs=[WHOLE] * 2,
        out_shape=[pltpu.VMEM(advected.shape, jnp.float32), pltpu.VMEM(fold.shape, jnp.float32)],
        scratch_shapes=[pltpu.VMEM((4 * rows_x, wide), jnp.float32), pltpu.VMEM((2, 4 * rows_x, wide // 2), jnp.float32)],
        input_output_aliases={6: 0, 7: 1},
        compiler_params=room(4),
        cost_estimate=SMALL,
        name="add_columns",
    )(here, *map(in_vmem, (up, down, far, ylo, yhi, advected, fold, *entries)))


def split_into(value_ref, high, low):
    for parity in range(2):
        value = value_ref[parity]
        rounded = value.astype(jnp.bfloat16)
        high[parity] = rounded
        low[parity] = (value - rounded.astype(jnp.float32)).astype(jnp.bfloat16)


def product(high, low, hi_ref, lo_ref, source, parity, cols):
    dot = functools.partial(jnp.dot, preferred_element_type=jnp.float32)
    tile = hi_ref[source, parity, :, cols]
    return dot(high[parity], tile) + (dot(low[parity], tile) + dot(high[parity], lo_ref[source, parity, :, cols]))


def own_body(wide, fold_ref, hi_ref, lo_ref, out_ref, high, low):
    split_into(fold_ref, high, low)
    for j in range(fold_ref.shape[2] // wide):
        cols = slice(j * wide, (j + 1) * wide)
        for parity in range(2):
            out_ref[parity, :, cols] = product(high, low, hi_ref, lo_ref, 0, parity, cols)


def own_gain(fold, entries):
    _, cells, size = fold.shape
    return pl.pallas_call(
        functools.partial(own_body, 2 * LANES),
        in_specs=[WHOLE] * 3,
        out_specs=WHOLE,
        out_shape=pltpu.VMEM(fold.shape, jnp.float32),
        scratch_shapes=[pltpu.VMEM(fold.shape, jnp.bfloat16)] * 2,
        compiler_params=room(8),
        cost_estimate=SMALL,
        name="own_gain",
    )(in_vmem(fold), *map(in_vmem, entries))


def collide_body(
    wide, rows_x, last, here_ref, fold_ref, hi_ref, lo_ref, part_ref, adv_ref, density_ref, type_ref, inflow_ref, *rest
):
    if last:
        out_ref, high, low, field, sems = rest
    else:
        field, up_ref, down_ref, xsend_ref, far_ref, high, low = rest
    cells, local_len = adv_ref.shape
    rows_y = cells // rows_x
    split_into(fold_ref, high, low)
    even_slot, turned = fold_masks(cells)
    rate = jnp.broadcast_to(collision_rate * density_ref[...], (cells, LANES))
    gain_rate = rate * ENTRY_SCALE
    kind = jnp.broadcast_to(type_ref[...], (cells, LANES))
    wall = kind == 1
    inlet = kind == 2
    copies = []
    for j in range(local_len // (2 * wide)):
        cols = slice(j * wide, (j + 1) * wide)
        even, odd = (part_ref[p, :, cols] + product(high, low, hi_ref, lo_ref, 1, p, cols) for p in range(2))
        lower = even + odd
        upper = even - odd
        for part in range(wide // LANES):
            group = slice(part * LANES, (part + 1) * LANES)
            for side, gain in enumerate(unfolded(lower[:, group], upper[:, group], even_slot, turned)):
                first = 2 * (j * wide + part * LANES) + side * LANES
                at = slice(first, first + LANES)
                vx, vy = velocity_parts(here_ref[0] * local_len + first + iota((1, LANES), 1))
                nu = 1.0 + (vx * vx + vy * vy) / 8.0
                moved = adv_ref[:, at]
                done = moved + (gain_rate * gain - rate * (nu * moved))
                field[:, at] = jnp.where(wall, 0.0, jnp.where(inlet, inflow_ref[:, at], done))
        span = slice(2 * j * wide, 2 * (j + 1) * wide)
        if last:
            copy = pltpu.make_async_copy(field.at[:, span], out_ref.at[:, span], sems.at[j])
            copy.start()
            copies.append(copy)
        else:
            write_edges(here_ref, rows_x, field, span, up_ref, down_ref, xsend_ref, far_ref)
    for copy in copies:
        copy.wait()


def collide(here, rows_x, fold, entries, part, advected, density, kind, inflow, last):
    _, cells, size = fold.shape
    local_len = advected.shape[1]
    wide = 2 * LANES
    halves = [pltpu.VMEM(fold.shape, jnp.bfloat16)] * 2
    if last:
        out_specs = pl.BlockSpec(memory_space=pl.ANY)
        out_shape = jax.ShapeDtypeStruct(advected.shape, jnp.float32)
        scratch = halves + [pltpu.VMEM(advected.shape, jnp.float32), pltpu.SemaphoreType.DMA((size // wide,))]
    else:
        out_specs = [WHOLE] * 5
        out_shape = [pltpu.VMEM(advected.shape, jnp.float32)] + edge_shapes(rows_x, cells // rows_x, local_len)
        scratch = halves
    return pl.pallas_call(
        functools.partial(collide_body, wide, rows_x, last),
        in_specs=[SCALARS] + [WHOLE] * 8,
        out_specs=out_specs,
        out_shape=out_shape,
        scratch_shapes=scratch,
        compiler_params=room(12),
        cost_estimate=SMALL,
        name="collide",
    )(here, in_vmem(fold), in_vmem(entries[0]), in_vmem(entries[1]), in_vmem(part), in_vmem(advected), density, kind, inflow)


def shifted(block, axis, by):
    count = lax.axis_size(axis)
    return lax.ppermute(block, axis, [(i, i + by) for i in range(count) if 0 <= i + by < count])


def per_device(distribution, density, cell_type, inflow):
    rows_x, rows_y, local_len = distribution.shape
    cells = rows_x * rows_y
    vert = lax.axis_index("vert")
    verts = lax.axis_size("vert")
    at_x = lax.axis_index("gx")
    size_x = lax.axis_size("gx")
    assert size_x == 2 and verts == 2
    here = jnp.stack([vert, jnp.int32(verts), (at_x > 0).astype(jnp.int32), (at_x < size_x - 1).astype(jnp.int32)])
    column_density = density.reshape(cells, 1)
    column_type = cell_type.reshape(cells, 1)
    row_inflow = inflow.reshape(1, local_len)
    swap = [(0, 1), (1, 0)]
    field, up, down, send_x, far = stage(here, rows_x, distribution.reshape(cells, local_len))
    entries = None
    for step in range(STEPS):
        last = step == STEPS - 1
        ylo = shifted(up, "gy", 1)
        yhi = shifted(down, "gy", -1)
        xhalo = lax.ppermute(send_x, "gx", swap)
        if entries is None:
            entries = make_entries(here, local_len // NVX, verts, [column_density, column_type])
        if step == 0:
            advected, fold = transport(here, rows_x, field, xhalo, [ylo, yhi], entries)
        else:
            advected, fold = transport(here, rows_x, field, xhalo, [], entries)
            advected, fold = add_columns(here, rows_x, up, down, far, ylo, yhi, advected, fold, entries)
        other = lax.ppermute(fold, "vert", swap)
        part = own_gain(fold, entries)
        out = collide(here, rows_x, other, entries, part, advected, column_density, column_type, row_inflow, last)
        if not last:
            field, up, down, send_x, far = out
    return out.reshape(rows_x, rows_y, local_len)


def solution(mesh):
    placed = (P("gx", "gy", "vert"), P("gx", "gy"), P("gx", "gy"), P("vert"))
    return jax.shard_map(
        per_device, mesh=mesh, in_specs=placed, out_specs=P("gx", "gy", "vert"), check_vma=False
    )
```

```python
import functools
import math

import jax
import jax.numpy as jnp
from jax import lax
from jax.experimental import pallas as pl
from jax.experimental.pallas import tpu as pltpu
from jax.sharding import PartitionSpec as P

NVX = 64
STEPS = 2
HALF = NVX // 2
LANES = 128
GROUP = LANES // HALF

vel_max = 4.0
time_step = 0.1
grad_scale = 2.5
collision_rate = 0.2
spacing = 2.0 * vel_max / NVX
middle = 0.5 * (NVX - 1)

MIB = 1024 * 1024
WHOLE = pl.BlockSpec(memory_space=pltpu.VMEM)
SCALARS = pl.BlockSpec(memory_space=pltpu.SMEM)

EXPONENT = 0.125 * math.log2(math.e)
ENTRY_SCALE = grad_scale * spacing * spacing * math.sqrt(EXPONENT)


SMALL = pl.CostEstimate(flops=1, bytes_accessed=1, transcendentals=0)


def room(mib):
    return pltpu.CompilerParams(vmem_limit_bytes=mib * MIB)


def in_vmem(value):
    return pltpu.with_memory_space_constraint(value, pltpu.VMEM)


def velocity_parts(index):
    row_portion = (index // NVX).astype(jnp.float32)
    col_part = (index % NVX).astype(jnp.float32)
    vel_x = (row_portion - middle) * spacing
    vel_y = (col_part - middle) * spacing
    return (vel_x, vel_y)


def iota(shape, dim):
    return lax.broadcasted_iota(jnp.int32, shape, dim)


def slot_order(slot):
    return lax.rem(slot, 2) * 2 + lax.div(slot, 2)


def entries_body(local, sources, here_ref, *rest):
    hi_ref, lo_ref, energy_ref, gauss_ref = rest[-4:]
    me = here_ref[0]
    groups = local // GROUP
    rows = 8
    lane = iota((1, LANES), 1)
    slot = slot_order(lane // HALF)
    vy = ((lane % HALF).astype(jnp.float32) - middle) * spacing

    def one(index, carry):
        source = lax.div(index, GROUP)
        r = lax.rem(index, GROUP)
        first = lax.rem(me + source, here_ref[1]) * local
        pair, lanes = iota((groups * groups, LANES), 0), iota((groups * groups, LANES), 1)
        out_x = ((me * local + pair // groups * GROUP + slot_order(lanes // HALF)).astype(jnp.float32) - middle) * spacing
        out_y = ((lanes % HALF).astype(jnp.float32) - middle) * spacing
        in_x = ((first + pair % groups * GROUP + r).astype(jnp.float32) - middle) * spacing
        out_sq, in_sq = out_x * out_x + out_y * out_y, in_x * in_x
        energy_ref[...] = EXPONENT * (out_sq - in_sq)
        gauss_ref[...] = jnp.exp((out_sq + in_sq) * -0.25) * (0.5 / EXPONENT)
        for part in range(HALF // rows):
            wy = ((iota((rows, LANES), 0) + part * rows).astype(jnp.float32) - middle) * spacing
            in_y_sq = EXPONENT * wy * wy
            in_y_gauss = jnp.exp(wy * wy * -0.25)
            dy_same = EXPONENT * ((vy - wy) ** 2 + spacing * spacing)
            dy_flip = EXPONENT * ((vy + wy) ** 2 + spacing * spacing)
            for m in range(1 - groups, groups):
                apart = (me * local - first + m * GROUP - r + slot).astype(jnp.float32) * spacing
                dx_sq = EXPONENT * apart * apart
                same_sq, flip_sq = dx_sq + dy_same, dx_sq + dy_flip
                same_inv, flip_inv = lax.rsqrt(same_sq), lax.rsqrt(flip_sq)
                same_inv_sq, flip_inv_sq = same_inv * same_inv, flip_inv * flip_inv
                same_top, flip_top = jnp.log2(same_inv) - same_sq, jnp.log2(flip_inv) - flip_sq
                same_r, flip_r = same_sq * same_inv, flip_sq * flip_inv
                sum_r, gap_r = same_r + flip_r, same_r - flip_r
                for g in range(max(0, m), min(groups, groups + m)):
                    k = g - m
                    at = g * groups + k
                    energy = energy_ref[at : at + 1, :] - in_y_sq
                    energy_sq = energy * energy
                    gauss = gauss_ref[at : at + 1, :] * in_y_gauss
                    same = jnp.exp2(same_top - energy_sq * same_inv_sq)
                    flip = jnp.exp2(flip_top - energy_sq * flip_inv_sq)
                    to = (k * GROUP + slot_order(r)) * HALF + part * rows
                    to = pl.ds(pl.multiple_of(to, rows), rows)
                    cols = slice(g * LANES, (g + 1) * LANES)
                    values = ((same + flip) - gauss * sum_r, (same - flip) - gauss * gap_r)
                    for parity, value in enumerate(values):
                        high = value.astype(jnp.bfloat16)
                        hi_ref[source, parity, to, cols] = high
                        lo_ref[source, parity, to, cols] = (value - high.astype(jnp.float32)).astype(jnp.bfloat16)
        return carry

    lax.fori_loop(0, sources * GROUP, one, 0)


def make_entries(here, local, sources, ahead_of):
    size = local * HALF
    shape = pltpu.VMEM((sources, 2, size, size), jnp.bfloat16)
    return pl.pallas_call(
        functools.partial(entries_body, local, sources),
        in_specs=[SCALARS] + [WHOLE] * len(ahead_of),
        out_specs=[WHOLE, WHOLE],
        out_shape=[shape, shape],
        scratch_shapes=[pltpu.VMEM(((local // GROUP) ** 2, LANES), jnp.float32)] * 2,
        compiler_params=room(8),
        cost_estimate=SMALL,
        name="kernel_entries",
    )(here, *map(in_vmem, ahead_of))


def pack_far(far, ahead, low_half):
    count = far.shape[0] // 2
    if ahead:
        return jnp.where(low_half, pltpu.roll(far[count:], LANES - HALF, 1), far[:count])
    return jnp.where(low_half, far[:count], pltpu.roll(far[count:], HALF, 1))


def unpack_far(packed, ahead):
    shift = HALF if ahead else LANES - HALF
    parts = [packed[:, i : i + LANES] for i in range(0, packed.shape[1], LANES)]
    turned = jnp.concatenate([pltpu.roll(p, shift, 1) for p in parts], axis=1)
    return jnp.concatenate([packed, turned], axis=0)


def write_edges(here_ref, rows_x, field, span, one_ref, two_ref, xsend_ref, far_ref):
    rows_y = field.shape[0] // rows_x
    for layer in range(2):
        first_row = field[layer * rows_y : (layer + 1) * rows_y, span]
        last_row = field[(rows_x - 2 + layer) * rows_y : (rows_x - 1 + layer) * rows_y, span]
        xsend_ref[layer, :, span] = jnp.where(here_ref[3] > 0, last_row, first_row)
    low_half = iota((rows_x // 2, LANES), 1) % NVX < HALF
    odd = here_ref[4]
    for side, to_ref, down in ((0, one_ref, odd), (1, two_ref, 1 - odd)):
        near = (1 - down) * (rows_y - 1)
        far = down + (1 - down) * (rows_y - 2)
        for x in range(rows_x):
            to_ref[x : x + 1, span] = field[pl.ds(x * rows_y + near, 1), span]
            far_ref[side, x : x + 1, span] = field[pl.ds(x * rows_y + far, 1), span]
        for i in range(span.start, span.stop, LANES):
            at = slice(i, i + LANES)
            layer = far_ref[side, :, at]
            to_ref[rows_x:, at] = jnp.where(down > 0, pack_far(layer, False, low_half), pack_far(layer, True, low_half))


def edge_shapes(rows_x, rows_y, local_len):
    edge_y = pltpu.VMEM((rows_x + rows_x // 2, local_len), jnp.float32)
    layers_x = pltpu.VMEM((2, rows_y, local_len), jnp.float32)
    return [edge_y, edge_y, layers_x, pltpu.VMEM((2, rows_x, local_len), jnp.float32)]


def stage_body(wide, rows_x, here_ref, from_ref, field, one_ref, two_ref, xsend_ref, far_ref, sems):
    spans = [slice(i, i + wide) for i in range(0, field.shape[1], wide)]
    copies = [pltpu.make_async_copy(from_ref.at[:, s], field.at[:, s], sems.at[i]) for i, s in enumerate(spans)]
    for copy in copies:
        copy.start()
    for copy, span in zip(copies, spans):
        copy.wait()
        write_edges(here_ref, rows_x, field, span, one_ref, two_ref, xsend_ref, far_ref)


def stage(here, rows_x, field):
    cells, local_len = field.shape
    wide = local_len // 4
    return pl.pallas_call(
        functools.partial(stage_body, wide, rows_x),
        in_specs=[SCALARS, pl.BlockSpec(memory_space=pltpu.HBM)],
        out_specs=[WHOLE] * 5,
        out_shape=[pltpu.VMEM(field.shape, jnp.float32)] + edge_shapes(rows_x, cells // rows_x, local_len),
        scratch_shapes=[pltpu.SemaphoreType.DMA((4,))],
        compiler_params=room(4),
        name="stage",
    )(here, pltpu.with_memory_space_constraint(field, pltpu.HBM))


def beyond(here_ref, rows_x, one_ref, two_ref, cols):
    odd = here_ref[4] > 0
    one, two = one_ref[:, cols], two_ref[:, cols]
    low, high = jnp.where(odd, one, two), jnp.where(odd, two, one)
    return unpack_far(low[rows_x:], True), low[:rows_x], high[:rows_x], unpack_far(high[rows_x:], False)


def minmod(a, b):
    return jnp.maximum(jnp.minimum(a, b), 0.0) + jnp.minimum(jnp.maximum(a, b), 0.0)


def fold_masks(rows):
    lane = iota((rows, LANES), 1)
    slot = lane // HALF
    even = slot % 2 == 0
    turned = jnp.where(even, 2 - slot, slot) * HALF + (HALF - 1) - lane % HALF
    return even, turned


def folded(a, b, even, turned):
    near = jnp.where(even, a, b)
    far = pltpu.roll(jnp.where(even, b, a), HALF, 1)
    lower = jnp.where(even, near, far)
    upper = jnp.take_along_axis(jnp.where(even, far, near), turned, axis=1)
    return lower + upper, lower - upper


def unfolded(lower, upper, even, turned):
    upper = jnp.take_along_axis(upper, turned, axis=1)
    near = jnp.where(even, lower, upper)
    far = pltpu.roll(jnp.where(even, upper, lower), LANES - HALF, 1)
    return jnp.where(even, near, far), jnp.where(even, far, near)


def transport_body(wide, rows_x, whole, here_ref, field_ref, xhalo_ref, *rest):
    if whole:
        one_ref, two_ref = rest[:2]
        adv_ref, fold_ref, low_edge, high_edge, low_near, high_near = rest[-6:]
    else:
        adv_ref, fold_ref = rest[-2:]
    cells, local_len = field_ref.shape
    rows_y = cells // rows_x
    has_low = here_ref[2] > 0
    has_high = here_ref[3] > 0
    at_y = iota((rows_y, wide), 0)
    first_y = at_y == 0
    last_y = at_y == rows_y - 1
    even, turned = fold_masks(rows_y)

    def chunk(c, carry):
        cols = pl.ds(pl.multiple_of(c * wide, wide), wide)
        vx, vy = velocity_parts(here_ref[0] * local_len + c * wide + iota((1, wide), 1))
        ax = time_step * vx
        ay = time_step * vy
        bx = 0.5 * jnp.abs(ax) * (1.0 - jnp.abs(ax))
        by = 0.5 * jnp.abs(ay) * (1.0 - jnp.abs(ay))
        ahead_x = ax > 0
        ahead_y = ay > 0

        def face_y(f0, f1, f2):
            return ay * f1 + by * minmod(f1 - f0, f2 - f1)

        if whole:
            for x in range(rows_x):
                low_edge[x : x + 1] = field_ref[x * rows_y : x * rows_y + 1, cols]
                high_edge[x : x + 1] = field_ref[(x + 1) * rows_y - 1 : (x + 1) * rows_y, cols]
            low_far, low_near[...], high_near[...], high_far = beyond(here_ref, rows_x, one_ref, two_ref, cols)
            low_edge[...] = face_y(low_far, low_near[...], low_edge[...])
            high_edge[...] = face_y(high_edge[...], high_near[...], high_far)

        def row(i):
            if i < 0:
                return jnp.where(has_low, xhalo_ref[i + 2, :, cols], 0.0)
            if i >= rows_x:
                return jnp.where(has_high, xhalo_ref[i - rows_x, :, cols], 0.0)
            return field_ref[i * rows_y : (i + 1) * rows_y, cols]

        near = [row(-2), row(-1), row(0)]
        low, high = near[1] - near[0], near[2] - near[1]
        face = [ax * near[1] + bx * minmod(low, high)]
        for i in range(rows_x + 1):
            near = [near[1], near[2], row(i + 1)]
            low, high = high, near[2] - near[1]
            face.append(ax * near[1] + bx * minmod(low, high))
            if i == 0:
                continue
            x = i - 1
            here = near[0]
            row_term = jnp.where(ahead_x, face[x + 1] - face[x], face[x + 2] - face[x + 1])
            below, above = pltpu.roll(here, 1, 0), pltpu.roll(here, rows_y - 1, 0)
            if whole:
                below = jnp.where(first_y, low_near[x : x + 1], below)
                above = jnp.where(last_y, high_near[x : x + 1], above)
            mine = face_y(below, here, above)
            if not whole:
                mine = jnp.where(first_y | last_y, 0.0, mine)
            mine_below, mine_above = pltpu.roll(mine, 1, 0), pltpu.roll(mine, rows_y - 1, 0)
            if whole:
                mine_below = jnp.where(first_y, low_edge[x : x + 1], mine_below)
                mine_above = jnp.where(last_y, high_edge[x : x + 1], mine_above)
            col_term = jnp.where(ahead_y, mine - mine_below, mine_above - mine)
            moved = here - row_term - col_term
            at = slice(x * rows_y, (x + 1) * rows_y)
            adv_ref[at, cols] = moved
            for part in range(wide // (2 * LANES)):
                first = 2 * part * LANES
                both = folded(moved[:, first : first + LANES], moved[:, first + LANES : first + 2 * LANES], even, turned)
                to = pl.ds(pl.multiple_of(c * (wide // 2) + part * LANES, LANES), LANES)
                fold_ref[0, at, to], fold_ref[1, at, to] = both
        return carry

    lax.fori_loop(0, local_len // wide, chunk, 0)


def columns_body(wide, rows_x, here_ref, one_ref, two_ref, far_ref, one_halo, two_halo, adv_in, fold_in, *rest):
    adv_ref, fold_ref, added, added_fold = rest[-4:]
    cells, local_len = adv_in.shape
    rows_y = cells // rows_x
    half = rows_y // 2
    masks = fold_masks(rows_x)

    def chunk(c, carry):
        cols = pl.ds(pl.multiple_of(c * wide, wide), wide)
        fold_cols = pl.ds(pl.multiple_of(c * (wide // 2), wide // 2), wide // 2)
        _, vy = velocity_parts(here_ref[0] * local_len + c * wide + iota((1, wide), 1))
        ay = time_step * vy
        by = 0.5 * jnp.abs(ay) * (1.0 - jnp.abs(ay))
        ahead = ay > 0

        def face(f0, f1, f2):
            return ay * f1 + by * minmod(f1 - f0, f2 - f1)

        low_far, low_near, high_near, high_far = beyond(here_ref, rows_x, one_halo, two_halo, cols)
        odd = here_ref[4] > 0
        one, two = one_ref[:rows_x, cols], two_ref[:rows_x, cols]
        low, high = jnp.where(odd, one, two), jnp.where(odd, two, one)
        one, two = far_ref[0, :, cols], far_ref[1, :, cols]
        second, last_but_one = jnp.where(odd, one, two), jnp.where(odd, two, one)
        before = face(low_far, low_near, low)
        first = face(low_near, low, second)
        last = face(last_but_one, high, high_near)
        after = face(high, high_near, high_far)
        parts = [
            jnp.where(ahead, before - first, first),
            jnp.where(ahead, first, 0.0),
            jnp.where(ahead, 0.0, -last),
            jnp.where(ahead, -last, last - after),
        ]
        for i, part in enumerate(parts):
            at = slice(i * rows_x, (i + 1) * rows_x)
            added[at] = part
            for j in range(0, wide, 2 * LANES):
                both = folded(part[:, j : j + LANES], part[:, j + LANES : j + 2 * LANES], *masks)
                for parity in range(2):
                    added_fold[parity, at, j // 2 : j // 2 + LANES] = both[parity]

        def spread(ref, x, upper, at_y):
            i = 2 if upper else 0
            first, second = (ref[(i + k) * rows_x + x : (i + k) * rows_x + x + 1, :] for k in range(2))
            place = half - 2 if upper else 0
            return jnp.where(at_y == place, first, jnp.where(at_y == place + 1, second, 0.0))

        at_y = iota((half, wide), 0)
        at_y_fold = iota((half, wide // 2), 0)
        for x in range(rows_x):
            for upper in range(2):
                rows = slice(x * rows_y + upper * half, x * rows_y + (upper + 1) * half)
                adv_ref[rows, cols] = adv_in[rows, cols] + spread(added, x, upper, at_y)
                for parity in range(2):
                    more = spread(added_fold.at[parity], x, upper, at_y_fold)
                    fold_ref[parity, rows, fold_cols] = fold_in[parity, rows, fold_cols] + more
        return carry

    lax.fori_loop(0, local_len // wide, chunk, 0)


def transport(here, rows_x, field, xhalo, yhalos, entries):
    cells, local_len = field.shape
    wide = 4 * LANES
    return pl.pallas_call(
        functools.partial(transport_body, wide, rows_x, bool(yhalos)),
        in_specs=[SCALARS] + [WHOLE] * (2 + len(yhalos) + len(entries)),
        out_specs=[WHOLE] * 2,
        out_shape=[pltpu.VMEM(field.shape, jnp.float32), pltpu.VMEM((2, cells, local_len // 2), jnp.float32)],
        scratch_shapes=[pltpu.VMEM((rows_x, wide), jnp.float32)] * (4 if yhalos else 0),
        compiler_params=room(4),
        cost_estimate=SMALL,
        name="transport" if yhalos else "inner_transport",
    )(here, *map(in_vmem, (field, xhalo, *yhalos, *entries)))


def add_columns(here, rows_x, one, two, far, one_halo, two_halo, advected, fold, entries):
    wide = 4 * LANES
    return pl.pallas_call(
        functools.partial(columns_body, wide, rows_x),
        in_specs=[SCALARS] + [WHOLE] * (7 + len(entries)),
        out_specs=[WHOLE] * 2,
        out_shape=[pltpu.VMEM(advected.shape, jnp.float32), pltpu.VMEM(fold.shape, jnp.float32)],
        scratch_shapes=[pltpu.VMEM((4 * rows_x, wide), jnp.float32), pltpu.VMEM((2, 4 * rows_x, wide // 2), jnp.float32)],
        input_output_aliases={6: 0, 7: 1},
        compiler_params=room(4),
        cost_estimate=SMALL,
        name="add_columns",
    )(here, *map(in_vmem, (one, two, far, one_halo, two_halo, advected, fold, *entries)))


def split_into(value_ref, high, low):
    for parity in range(2):
        value = value_ref[parity]
        rounded = value.astype(jnp.bfloat16)
        high[parity] = rounded
        low[parity] = (value - rounded.astype(jnp.float32)).astype(jnp.bfloat16)


def product(high, low, hi_ref, lo_ref, source, parity, cols):
    dot = functools.partial(jnp.dot, preferred_element_type=jnp.float32)
    tile = hi_ref[source, parity, :, cols]
    return dot(high[parity], tile) + (dot(low[parity], tile) + dot(high[parity], lo_ref[source, parity, :, cols]))


def own_body(wide, fold_ref, hi_ref, lo_ref, out_ref, high, low):
    split_into(fold_ref, high, low)
    for j in range(fold_ref.shape[2] // wide):
        cols = slice(j * wide, (j + 1) * wide)
        for parity in range(2):
            out_ref[parity, :, cols] = product(high, low, hi_ref, lo_ref, 0, parity, cols)


def own_gain(fold, entries):
    _, cells, size = fold.shape
    return pl.pallas_call(
        functools.partial(own_body, 2 * LANES),
        in_specs=[WHOLE] * 3,
        out_specs=WHOLE,
        out_shape=pltpu.VMEM(fold.shape, jnp.float32),
        scratch_shapes=[pltpu.VMEM(fold.shape, jnp.bfloat16)] * 2,
        compiler_params=room(8),
        cost_estimate=SMALL,
        name="own_gain",
    )(in_vmem(fold), *map(in_vmem, entries))


def collide_body(
    wide, rows_x, last, here_ref, fold_ref, hi_ref, lo_ref, part_ref, adv_ref, density_ref, type_ref, inflow_ref, *rest
):
    if last:
        out_ref, high, low, field, sems = rest
    else:
        field, one_ref, two_ref, xsend_ref, far_ref, high, low = rest
    cells, local_len = adv_ref.shape
    rows_y = cells // rows_x
    split_into(fold_ref, high, low)
    even_slot, turned = fold_masks(cells)
    rate = jnp.broadcast_to(collision_rate * density_ref[...], (cells, LANES))
    gain_rate = rate * ENTRY_SCALE
    kind = jnp.broadcast_to(type_ref[...], (cells, LANES))
    wall = kind == 1
    inlet = kind == 2
    copies = []
    for j in range(local_len // (2 * wide)):
        cols = slice(j * wide, (j + 1) * wide)
        even, odd = (part_ref[p, :, cols] + product(high, low, hi_ref, lo_ref, 1, p, cols) for p in range(2))
        lower = even + odd
        upper = even - odd
        for part in range(wide // LANES):
            group = slice(part * LANES, (part + 1) * LANES)
            for side, gain in enumerate(unfolded(lower[:, group], upper[:, group], even_slot, turned)):
                first = 2 * (j * wide + part * LANES) + side * LANES
                at = slice(first, first + LANES)
                vx, vy = velocity_parts(here_ref[0] * local_len + first + iota((1, LANES), 1))
                nu = 1.0 + (vx * vx + vy * vy) / 8.0
                moved = adv_ref[:, at]
                done = moved + (gain_rate * gain - rate * (nu * moved))
                field[:, at] = jnp.where(wall, 0.0, jnp.where(inlet, inflow_ref[:, at], done))
        span = slice(2 * j * wide, 2 * (j + 1) * wide)
        if last:
            copy = pltpu.make_async_copy(field.at[:, span], out_ref.at[:, span], sems.at[j])
            copy.start()
            copies.append(copy)
        else:
            write_edges(here_ref, rows_x, field, span, one_ref, two_ref, xsend_ref, far_ref)
    for copy in copies:
        copy.wait()


def collide(here, rows_x, fold, entries, part, advected, density, kind, inflow, last):
    _, cells, size = fold.shape
    local_len = advected.shape[1]
    wide = 2 * LANES
    halves = [pltpu.VMEM(fold.shape, jnp.bfloat16)] * 2
    if last:
        out_specs = pl.BlockSpec(memory_space=pl.ANY)
        out_shape = jax.ShapeDtypeStruct(advected.shape, jnp.float32)
        scratch = halves + [pltpu.VMEM(advected.shape, jnp.float32), pltpu.SemaphoreType.DMA((size // wide,))]
    else:
        out_specs = [WHOLE] * 5
        out_shape = [pltpu.VMEM(advected.shape, jnp.float32)] + edge_shapes(rows_x, cells // rows_x, local_len)
        scratch = halves
    return pl.pallas_call(
        functools.partial(collide_body, wide, rows_x, last),
        in_specs=[SCALARS] + [WHOLE] * 8,
        out_specs=out_specs,
        out_shape=out_shape,
        scratch_shapes=scratch,
        compiler_params=room(12),
        cost_estimate=SMALL,
        name="collide",
    )(here, in_vmem(fold), in_vmem(entries[0]), in_vmem(entries[1]), in_vmem(part), in_vmem(advected), density, kind, inflow)


def swapped(block, axis, first):
    pairs = [(i, i + 1) for i in range(first, lax.axis_size(axis) - 1, 2)]
    return lax.ppermute(block, axis, [pair for i, j in pairs for pair in ((i, j), (j, i))])


def per_device(distribution, density, cell_type, inflow):
    rows_x, rows_y, local_len = distribution.shape
    cells = rows_x * rows_y
    vert = lax.axis_index("vert")
    verts = lax.axis_size("vert")
    at_x = lax.axis_index("gx")
    size_x = lax.axis_size("gx")
    assert size_x == 2 and verts == 2
    here = jnp.stack([vert, jnp.int32(verts), (at_x > 0).astype(jnp.int32), (at_x < size_x - 1).astype(jnp.int32), lax.axis_index("gy") % 2])
    column_density = density.reshape(cells, 1)
    column_type = cell_type.reshape(cells, 1)
    row_inflow = inflow.reshape(1, local_len)
    swap = [(0, 1), (1, 0)]
    field, one, two, send_x, far = stage(here, rows_x, distribution.reshape(cells, local_len))
    entries = None
    for step in range(STEPS):
        last = step == STEPS - 1
        one_halo = swapped(one, "gy", 0)
        two_halo = swapped(two, "gy", 1)
        xhalo = lax.ppermute(send_x, "gx", swap)
        if entries is None:
            entries = make_entries(here, local_len // NVX, verts, [column_density, column_type])
        if step == 0:
            advected, fold = transport(here, rows_x, field, xhalo, [one_halo, two_halo], entries)
        else:
            advected, fold = transport(here, rows_x, field, xhalo, [], entries)
            advected, fold = add_columns(here, rows_x, one, two, far, one_halo, two_halo, advected, fold, entries)
        other = lax.ppermute(fold, "vert", swap)
        part = own_gain(fold, entries)
        out = collide(here, rows_x, other, entries, part, advected, column_density, column_type, row_inflow, last)
        if not last:
            field, one, two, send_x, far = out
    return out.reshape(rows_x, rows_y, local_len)


def solution(mesh):
    placed = (P("gx", "gy", "vert"), P("gx", "gy"), P("gx", "gy"), P("vert"))
    return jax.shard_map(
        per_device, mesh=mesh, in_specs=placed, out_specs=P("gx", "gy", "vert"), check_vma=False
    )
```

```python
import functools
import math

import jax
import jax.numpy as jnp
from jax import lax
from jax.experimental import pallas as pl
from jax.experimental.pallas import tpu as pltpu
from jax.sharding import PartitionSpec as P

NVX = 64
STEPS = 2
HALF = NVX // 2
LANES = 128
GROUP = LANES // HALF

vel_max = 4.0
time_step = 0.1
grad_scale = 2.5
collision_rate = 0.2
spacing = 2.0 * vel_max / NVX
middle = 0.5 * (NVX - 1)

MIB = 1024 * 1024
WHOLE = pl.BlockSpec(memory_space=pltpu.VMEM)

EXPONENT = 0.125 * math.log2(math.e)
ENTRY_SCALE = grad_scale * spacing * spacing * math.sqrt(EXPONENT)


SMALL = pl.CostEstimate(flops=1, bytes_accessed=1, transcendentals=0)


def place():
    at_x = lax.axis_index("gx")
    more = (at_x > 0, at_x < lax.axis_size("gx") - 1)
    return [lax.axis_index("vert"), lax.axis_size("vert"), *(m.astype(jnp.int32) for m in more), lax.axis_index("gy") % 2]


def room(mib):
    return pltpu.CompilerParams(vmem_limit_bytes=mib * MIB)


def in_vmem(value):
    return pltpu.with_memory_space_constraint(value, pltpu.VMEM)


def velocity_parts(index):
    row_portion = (index // NVX).astype(jnp.float32)
    col_part = (index % NVX).astype(jnp.float32)
    vel_x = (row_portion - middle) * spacing
    vel_y = (col_part - middle) * spacing
    return (vel_x, vel_y)


def iota(shape, dim):
    return lax.broadcasted_iota(jnp.int32, shape, dim)


def slot_order(slot):
    return lax.rem(slot, 2) * 2 + lax.div(slot, 2)


def entries_body(local, sources, *rest):
    here_ref = place()
    hi_ref, lo_ref, energy_ref, gauss_ref = rest[-4:]
    me = here_ref[0]
    groups = local // GROUP
    rows = 8
    lane = iota((1, LANES), 1)
    slot = slot_order(lane // HALF)
    vy = ((lane % HALF).astype(jnp.float32) - middle) * spacing

    def one(index, carry):
        source = lax.div(index, GROUP)
        r = lax.rem(index, GROUP)
        first = lax.rem(me + source, here_ref[1]) * local
        pair, lanes = iota((groups * groups, LANES), 0), iota((groups * groups, LANES), 1)
        out_x = ((me * local + pair // groups * GROUP + slot_order(lanes // HALF)).astype(jnp.float32) - middle) * spacing
        out_y = ((lanes % HALF).astype(jnp.float32) - middle) * spacing
        in_x = ((first + pair % groups * GROUP + r).astype(jnp.float32) - middle) * spacing
        out_sq, in_sq = out_x * out_x + out_y * out_y, in_x * in_x
        energy_ref[...] = EXPONENT * (out_sq - in_sq)
        gauss_ref[...] = jnp.exp((out_sq + in_sq) * -0.25) * (0.5 / EXPONENT)
        for part in range(HALF // rows):
            wy = ((iota((rows, LANES), 0) + part * rows).astype(jnp.float32) - middle) * spacing
            in_y_sq = EXPONENT * wy * wy
            in_y_gauss = jnp.exp(wy * wy * -0.25)
            dy_same = EXPONENT * ((vy - wy) ** 2 + spacing * spacing)
            dy_flip = EXPONENT * ((vy + wy) ** 2 + spacing * spacing)
            for m in range(1 - groups, groups):
                apart = (me * local - first + m * GROUP - r + slot).astype(jnp.float32) * spacing
                dx_sq = EXPONENT * apart * apart
                same_sq, flip_sq = dx_sq + dy_same, dx_sq + dy_flip
                same_inv, flip_inv = lax.rsqrt(same_sq), lax.rsqrt(flip_sq)
                same_inv_sq, flip_inv_sq = same_inv * same_inv, flip_inv * flip_inv
                same_top, flip_top = jnp.log2(same_inv) - same_sq, jnp.log2(flip_inv) - flip_sq
                same_r, flip_r = same_sq * same_inv, flip_sq * flip_inv
                sum_r, gap_r = same_r + flip_r, same_r - flip_r
                for g in range(max(0, m), min(groups, groups + m)):
                    k = g - m
                    at = g * groups + k
                    energy = energy_ref[at : at + 1, :] - in_y_sq
                    energy_sq = energy * energy
                    gauss = gauss_ref[at : at + 1, :] * in_y_gauss
                    same = jnp.exp2(same_top - energy_sq * same_inv_sq)
                    flip = jnp.exp2(flip_top - energy_sq * flip_inv_sq)
                    to = (k * GROUP + slot_order(r)) * HALF + part * rows
                    to = pl.ds(pl.multiple_of(to, rows), rows)
                    cols = slice(g * LANES, (g + 1) * LANES)
                    values = ((same + flip) - gauss * sum_r, (same - flip) - gauss * gap_r)
                    for parity, value in enumerate(values):
                        high = value.astype(jnp.bfloat16)
                        hi_ref[source, parity, to, cols] = high
                        lo_ref[source, parity, to, cols] = (value - high.astype(jnp.float32)).astype(jnp.bfloat16)
        return carry

    lax.fori_loop(0, sources * GROUP, one, 0)


def make_entries(local, sources, ahead_of):
    size = local * HALF
    shape = pltpu.VMEM((sources, 2, size, size), jnp.bfloat16)
    return pl.pallas_call(
        functools.partial(entries_body, local, sources),
        in_specs=[WHOLE] * len(ahead_of),
        out_specs=[WHOLE, WHOLE],
        out_shape=[shape, shape],
        scratch_shapes=[pltpu.VMEM(((local // GROUP) ** 2, LANES), jnp.float32)] * 2,
        compiler_params=room(8),
        cost_estimate=SMALL,
        name="kernel_entries",
    )(*map(in_vmem, ahead_of))


def pack_far(far, ahead, low_half):
    count = far.shape[0] // 2
    if ahead:
        return jnp.where(low_half, pltpu.roll(far[count:], LANES - HALF, 1), far[:count])
    return jnp.where(low_half, far[:count], pltpu.roll(far[count:], HALF, 1))


def unpack_far(packed, ahead):
    shift = HALF if ahead else LANES - HALF
    parts = [packed[:, i : i + LANES] for i in range(0, packed.shape[1], LANES)]
    turned = jnp.concatenate([pltpu.roll(p, shift, 1) for p in parts], axis=1)
    return jnp.concatenate([packed, turned], axis=0)


def outer_columns(field, rows_x, span, upper):
    rows_y = field.shape[0] // rows_x
    half = rows_y // 2
    at = iota((half, span.stop - span.start), 0)
    shift = 1 - half if upper else 0
    nears, fars = [], []
    for first in range(0, rows_x, half):
        near = far = None
        for s in range(half):
            start = (first + s) * rows_y + (half if upper else 0)
            turned = pltpu.roll(field[start : start + half, span], (s + shift) % half, 0)
            near = turned if near is None else jnp.where(at == s, turned, near)
            beside = (s - 1 if upper else s + 1) % half
            far = turned if far is None else jnp.where(at == beside, turned, far)
        nears.append(near)
        fars.append(pltpu.roll(far, 1 if upper else half - 1, 0))
    return jnp.concatenate(nears, axis=0), jnp.concatenate(fars, axis=0)


def write_edges(here_ref, rows_x, field, span, edge_refs):
    one_ref, two_ref, xsend_ref, far_ref = edge_refs
    rows_y = field.shape[0] // rows_x
    to_next = here_ref[3] > 0
    for layer in range(2):
        low_row, high_row = (field[x * rows_y : (x + 1) * rows_y, span] for x in (layer, rows_x - 2 + layer))
        xsend_ref[layer, :, span] = jnp.where(to_next, high_row, low_row)
    odd = here_ref[4] > 0
    low_near, low_far = outer_columns(field, rows_x, span, False)
    high_near, high_far = outer_columns(field, rows_x, span, True)
    one_ref[:rows_x, span] = jnp.where(odd, low_near, high_near)
    two_ref[:rows_x, span] = jnp.where(odd, high_near, low_near)
    far_ref[0, :, span] = jnp.where(odd, low_far, high_far)
    far_ref[1, :, span] = jnp.where(odd, high_far, low_far)
    low_half = iota((rows_x // 2, LANES), 1) % NVX < HALF
    for i in range(0, span.stop - span.start, LANES):
        at = slice(span.start + i, span.start + i + LANES)
        low = pack_far(low_far[:, i : i + LANES], False, low_half)
        high = pack_far(high_far[:, i : i + LANES], True, low_half)
        one_ref[rows_x:, at] = jnp.where(odd, low, high)
        two_ref[rows_x:, at] = jnp.where(odd, high, low)


def edge_shapes(rows_x, rows_y, local_len):
    edge_y = pltpu.VMEM((rows_x + rows_x // 2, local_len), jnp.float32)
    layers_x = pltpu.VMEM((2, rows_y, local_len), jnp.float32)
    return [edge_y, edge_y, layers_x, pltpu.VMEM((2, rows_x, local_len), jnp.float32)]


def stage_body(wide, rows_x, from_ref, field, *rest):
    here_ref = place()
    *edge_refs, sems = rest
    spans = [slice(i, i + wide) for i in range(0, field.shape[1], wide)]
    copies = [pltpu.make_async_copy(from_ref.at[:, s], field.at[:, s], sems.at[i]) for i, s in enumerate(spans)]
    for copy in copies:
        copy.start()
    for copy, span in zip(copies, spans):
        copy.wait()
        write_edges(here_ref, rows_x, field, span, edge_refs)


def stage(rows_x, field):
    cells, local_len = field.shape
    wide = local_len // 4
    return pl.pallas_call(
        functools.partial(stage_body, wide, rows_x),
        in_specs=[pl.BlockSpec(memory_space=pltpu.HBM)],
        out_specs=[WHOLE] * 5,
        out_shape=[pltpu.VMEM(field.shape, jnp.float32)] + edge_shapes(rows_x, cells // rows_x, local_len),
        scratch_shapes=[pltpu.SemaphoreType.DMA((4,))],
        compiler_params=room(4),
        name="stage",
    )(pltpu.with_memory_space_constraint(field, pltpu.HBM))


def beyond(here_ref, rows_x, one_ref, two_ref, cols):
    odd = here_ref[4] > 0
    one, two = one_ref[:, cols], two_ref[:, cols]
    low, high = jnp.where(odd, one, two), jnp.where(odd, two, one)
    return unpack_far(low[rows_x:], True), low[:rows_x], high[:rows_x], unpack_far(high[rows_x:], False)


def minmod(a, b):
    return jnp.maximum(jnp.minimum(a, b), 0.0) + jnp.minimum(jnp.maximum(a, b), 0.0)


def fold_masks(rows):
    lane = iota((rows, LANES), 1)
    slot = lane // HALF
    even = slot % 2 == 0
    turned = jnp.where(even, 2 - slot, slot) * HALF + (HALF - 1) - lane % HALF
    return even, turned


def folded(a, b, even, turned):
    near = jnp.where(even, a, b)
    far = pltpu.roll(jnp.where(even, b, a), HALF, 1)
    lower = jnp.where(even, near, far)
    upper = jnp.take_along_axis(jnp.where(even, far, near), turned, axis=1)
    return lower + upper, lower - upper


def unfolded(lower, upper, even, turned):
    upper = jnp.take_along_axis(upper, turned, axis=1)
    near = jnp.where(even, lower, upper)
    far = pltpu.roll(jnp.where(even, upper, lower), LANES - HALF, 1)
    return jnp.where(even, near, far), jnp.where(even, far, near)


def transport_body(wide, rows_x, whole, field_ref, xhalo_ref, *rest):
    here_ref = place()
    if whole:
        one_halo, two_halo, one_ref, two_ref = rest[:4]
        adv_ref, fold_ref, low_edge, high_edge, low_near, high_near = rest[-6:]
    else:
        adv_ref, fold_ref = rest[-2:]
    cells, local_len = field_ref.shape
    rows_y = cells // rows_x
    has_low = here_ref[2] > 0
    has_high = here_ref[3] > 0
    at_y = iota((rows_y, wide), 0)
    first_y = at_y == 0
    last_y = at_y == rows_y - 1
    even, turned = fold_masks(rows_y)

    def chunk(c, carry):
        cols = pl.ds(pl.multiple_of(c * wide, wide), wide)
        vx, vy = velocity_parts(here_ref[0] * local_len + c * wide + iota((1, wide), 1))
        ax = time_step * vx
        ay = time_step * vy
        bx = 0.5 * jnp.abs(ax) * (1.0 - jnp.abs(ax))
        by = 0.5 * jnp.abs(ay) * (1.0 - jnp.abs(ay))
        ahead_x = ax > 0
        ahead_y = ay > 0

        def face_y(f0, f1, f2):
            return ay * f1 + by * minmod(f1 - f0, f2 - f1)

        if whole:
            low_far, low_near[...], high_near[...], high_far = beyond(here_ref, rows_x, one_halo, two_halo, cols)
            odd = here_ref[4] > 0
            one, two = one_ref[:rows_x, cols], two_ref[:rows_x, cols]
            low_edge[...] = face_y(low_far, low_near[...], jnp.where(odd, one, two))
            high_edge[...] = face_y(jnp.where(odd, two, one), high_near[...], high_far)

        def row(i):
            if i < 0:
                return jnp.where(has_low, xhalo_ref[i + 2, :, cols], 0.0)
            if i >= rows_x:
                return jnp.where(has_high, xhalo_ref[i - rows_x, :, cols], 0.0)
            return field_ref[i * rows_y : (i + 1) * rows_y, cols]

        near = [row(-2), row(-1), row(0)]
        low, high = near[1] - near[0], near[2] - near[1]
        face = [ax * near[1] + bx * minmod(low, high)]
        for i in range(rows_x + 1):
            near = [near[1], near[2], row(i + 1)]
            low, high = high, near[2] - near[1]
            face.append(ax * near[1] + bx * minmod(low, high))
            if i == 0:
                continue
            x = i - 1
            here = near[0]
            row_term = jnp.where(ahead_x, face[x + 1] - face[x], face[x + 2] - face[x + 1])
            if whole:
                below = jnp.where(first_y, low_near[x : x + 1], pltpu.roll(here, 1, 0))
                above = jnp.where(last_y, high_near[x : x + 1], pltpu.roll(here, rows_y - 1, 0))
                mine = face_y(below, here, above)
                mine_below = jnp.where(first_y, low_edge[x : x + 1], pltpu.roll(mine, 1, 0))
                mine_above = jnp.where(last_y, high_edge[x : x + 1], pltpu.roll(mine, rows_y - 1, 0))
                col_term = jnp.where(ahead_y, mine - mine_below, mine_above - mine)
            else:
                rise = here - pltpu.roll(here, 1, 0)
                mine = ay * here + by * minmod(rise, pltpu.roll(rise, rows_y - 1, 0))
                mine = jnp.where(first_y | last_y, 0.0, mine)
                step = mine - pltpu.roll(mine, 1, 0)
                col_term = jnp.where(ahead_y, step, pltpu.roll(step, rows_y - 1, 0))
            moved = here - row_term - col_term
            at = slice(x * rows_y, (x + 1) * rows_y)
            adv_ref[at, cols] = moved
            for part in range(wide // (2 * LANES)):
                first = 2 * part * LANES
                both = folded(moved[:, first : first + LANES], moved[:, first + LANES : first + 2 * LANES], even, turned)
                to = pl.ds(pl.multiple_of(c * (wide // 2) + part * LANES, LANES), LANES)
                fold_ref[0, at, to], fold_ref[1, at, to] = both
        return carry

    lax.fori_loop(0, local_len // wide, chunk, 0)


def columns_body(wide, rows_x, one_ref, two_ref, far_ref, one_halo, two_halo, adv_in, fold_in, *rest):
    here_ref = place()
    adv_ref, fold_ref = rest[-2:]
    cells, local_len = adv_in.shape
    rows_y = cells // rows_x
    half = rows_y // 2
    masks = fold_masks(rows_x)

    def spread(parts, from_ref, to_ref, cols):
        at = iota((half, parts[0].shape[1]), 0)
        even = at % 2 == 0
        for first in range(0, rows_x, half):
            for upper in range(2):
                a, b = (part[first : first + half] for part in parts[2 * upper : 2 * upper + 2])
                b = pltpu.roll(b, 1, 0)
                pairs = jnp.where(even, a, b), jnp.where(even, b, a)
                place = upper * (half - 2)
                here = (at == place) | (at == place + 1)
                done = []
                for s in range(half):
                    start = (first + s) * rows_y + upper * half
                    rows = slice(start, start + half)
                    more = jnp.where(here, pltpu.roll(pairs[s % 2], (place - s) % half, 0), 0.0)
                    done.append((rows, from_ref[rows, cols] + more))
                for rows, value in done:
                    to_ref[rows, cols] = value

    def chunk(c, carry):
        cols = pl.ds(pl.multiple_of(c * wide, wide), wide)
        fold_cols = pl.ds(pl.multiple_of(c * (wide // 2), wide // 2), wide // 2)
        _, vy = velocity_parts(here_ref[0] * local_len + c * wide + iota((1, wide), 1))
        ay = time_step * vy
        by = 0.5 * jnp.abs(ay) * (1.0 - jnp.abs(ay))
        ahead = ay > 0

        def face(f0, f1, f2):
            return ay * f1 + by * minmod(f1 - f0, f2 - f1)

        low_far, low_near, high_near, high_far = beyond(here_ref, rows_x, one_halo, two_halo, cols)
        odd = here_ref[4] > 0
        one, two = one_ref[:rows_x, cols], two_ref[:rows_x, cols]
        low, high = jnp.where(odd, one, two), jnp.where(odd, two, one)
        one, two = far_ref[0, :, cols], far_ref[1, :, cols]
        second, last_but_one = jnp.where(odd, one, two), jnp.where(odd, two, one)
        before = face(low_far, low_near, low)
        first = face(low_near, low, second)
        last = face(last_but_one, high, high_near)
        after = face(high, high_near, high_far)
        parts = [
            jnp.where(ahead, before - first, first),
            jnp.where(ahead, first, 0.0),
            jnp.where(ahead, 0.0, -last),
            jnp.where(ahead, -last, last - after),
        ]
        spread(parts, adv_in, adv_ref, cols)
        both = []
        for part in parts:
            pairs = [folded(part[:, j : j + LANES], part[:, j + LANES : j + 2 * LANES], *masks) for j in range(0, wide, 2 * LANES)]
            both.append([jnp.concatenate(tiles, axis=1) for tiles in zip(*pairs)])
        for parity in range(2):
            spread([pair[parity] for pair in both], fold_in.at[parity], fold_ref.at[parity], fold_cols)
        return carry

    lax.fori_loop(0, local_len // wide, chunk, 0)


def transport(rows_x, field, xhalo, yhalos, entries):
    cells, local_len = field.shape
    wide = 4 * LANES
    return pl.pallas_call(
        functools.partial(transport_body, wide, rows_x, bool(yhalos)),
        in_specs=[WHOLE] * (2 + len(yhalos) + len(entries)),
        out_specs=[WHOLE] * 2,
        out_shape=[pltpu.VMEM(field.shape, jnp.float32), pltpu.VMEM((2, cells, local_len // 2), jnp.float32)],
        scratch_shapes=[pltpu.VMEM((rows_x, wide), jnp.float32)] * (4 if yhalos else 0),
        compiler_params=room(4),
        cost_estimate=SMALL,
        name="transport" if yhalos else "inner_transport",
    )(*map(in_vmem, (field, xhalo, *yhalos, *entries)))


def add_columns(rows_x, one, two, far, one_halo, two_halo, advected, fold, entries):
    wide = 4 * LANES
    return pl.pallas_call(
        functools.partial(columns_body, wide, rows_x),
        in_specs=[WHOLE] * (7 + len(entries)),
        out_specs=[WHOLE] * 2,
        out_shape=[pltpu.VMEM(advected.shape, jnp.float32), pltpu.VMEM(fold.shape, jnp.float32)],
        input_output_aliases={5: 0, 6: 1},
        compiler_params=room(4),
        cost_estimate=SMALL,
        name="add_columns",
    )(*map(in_vmem, (one, two, far, one_halo, two_halo, advected, fold, *entries)))


def split_into(value_ref, high, low):
    for parity in range(2):
        value = value_ref[parity]
        rounded = value.astype(jnp.bfloat16)
        high[parity] = rounded
        low[parity] = (value - rounded.astype(jnp.float32)).astype(jnp.bfloat16)


def product(high, low, hi_ref, lo_ref, source, parity, cols):
    dot = functools.partial(jnp.dot, preferred_element_type=jnp.float32)
    tile = hi_ref[source, parity, :, cols]
    return dot(high[parity], tile) + (dot(low[parity], tile) + dot(high[parity], lo_ref[source, parity, :, cols]))


def own_body(wide, fold_ref, hi_ref, lo_ref, out_ref, high, low):
    split_into(fold_ref, high, low)
    for j in range(fold_ref.shape[2] // wide):
        cols = slice(j * wide, (j + 1) * wide)
        for parity in range(2):
            out_ref[parity, :, cols] = product(high, low, hi_ref, lo_ref, 0, parity, cols)


def own_gain(fold, entries):
    _, cells, size = fold.shape
    return pl.pallas_call(
        functools.partial(own_body, 2 * LANES),
        in_specs=[WHOLE] * 3,
        out_specs=WHOLE,
        out_shape=pltpu.VMEM(fold.shape, jnp.float32),
        scratch_shapes=[pltpu.VMEM(fold.shape, jnp.bfloat16)] * 2,
        compiler_params=room(8),
        cost_estimate=SMALL,
        name="own_gain",
    )(in_vmem(fold), *map(in_vmem, entries))


def collide_body(
    wide, rows_x, last, fold_ref, hi_ref, lo_ref, part_ref, adv_ref, density_ref, type_ref, inflow_ref, *rest
):
    here_ref = place()
    if last:
        out_ref, high, low, field, sems = rest
    else:
        field, *edge_refs, high, low = rest
    cells, local_len = adv_ref.shape
    rows_y = cells // rows_x
    split_into(fold_ref, high, low)
    even_slot, turned = fold_masks(cells)
    rate = jnp.broadcast_to(collision_rate * density_ref[...], (cells, LANES))
    kind = jnp.broadcast_to(type_ref[...], (cells, LANES))
    wall = kind == 1
    inlet = kind == 2
    copies = []
    for j in range(local_len // (2 * wide)):
        cols = slice(j * wide, (j + 1) * wide)
        even, odd = (part_ref[p, :, cols] + product(high, low, hi_ref, lo_ref, 1, p, cols) for p in range(2))
        lower = even + odd
        upper = even - odd
        for part in range(wide // LANES):
            group = slice(part * LANES, (part + 1) * LANES)
            for side, gain in enumerate(unfolded(lower[:, group], upper[:, group], even_slot, turned)):
                first = 2 * (j * wide + part * LANES) + side * LANES
                at = slice(first, first + LANES)
                vx, vy = velocity_parts(here_ref[0] * local_len + first + iota((1, LANES), 1))
                nu = 1.0 + (vx * vx + vy * vy) / 8.0
                moved = adv_ref[:, at]
                done = moved + rate * (ENTRY_SCALE * gain - nu * moved)
                field[:, at] = jnp.where(wall, 0.0, jnp.where(inlet, inflow_ref[:, at], done))
            span = slice(first - LANES, first + LANES)
            if last:
                i = first // (2 * LANES)
                copy = pltpu.make_async_copy(field.at[:, span], out_ref.at[:, span], sems.at[i])
                copy.start()
                copies.append(copy)
            else:
                write_edges(here_ref, rows_x, field, span, edge_refs)
    for copy in copies:
        copy.wait()


def collide(rows_x, fold, entries, part, advected, density, kind, inflow, last):
    _, cells, size = fold.shape
    local_len = advected.shape[1]
    wide = 2 * LANES
    halves = [pltpu.VMEM(fold.shape, jnp.bfloat16)] * 2
    if last:
        out_specs = pl.BlockSpec(memory_space=pl.ANY)
        out_shape = jax.ShapeDtypeStruct(advected.shape, jnp.float32)
        scratch = halves + [pltpu.VMEM(advected.shape, jnp.float32), pltpu.SemaphoreType.DMA((size // LANES,))]
    else:
        out_specs = [WHOLE] * 5
        out_shape = [pltpu.VMEM(advected.shape, jnp.float32)] + edge_shapes(rows_x, cells // rows_x, local_len)
        scratch = halves
    return pl.pallas_call(
        functools.partial(collide_body, wide, rows_x, last),
        in_specs=[WHOLE] * 8,
        out_specs=out_specs,
        out_shape=out_shape,
        scratch_shapes=scratch,
        compiler_params=room(12),
        cost_estimate=SMALL,
        name="collide",
    )(in_vmem(fold), in_vmem(entries[0]), in_vmem(entries[1]), in_vmem(part), in_vmem(advected), density, kind, inflow)


def swapped(block, axis, first):
    pairs = [(i, i + 1) for i in range(first, lax.axis_size(axis) - 1, 2)]
    return lax.ppermute(block, axis, [pair for i, j in pairs for pair in ((i, j), (j, i))])


def per_device(distribution, density, cell_type, inflow):
    rows_x, rows_y, local_len = distribution.shape
    cells = rows_x * rows_y
    vert = lax.axis_index("vert")
    verts = lax.axis_size("vert")
    at_x = lax.axis_index("gx")
    size_x = lax.axis_size("gx")
    assert size_x == 2 and verts == 2
    column_density = density.reshape(cells, 1)
    column_type = cell_type.reshape(cells, 1)
    row_inflow = inflow.reshape(1, local_len)
    swap = [(0, 1), (1, 0)]
    field, one, two, send_x, far = stage(rows_x, distribution.reshape(cells, local_len))
    entries = None
    for step in range(STEPS):
        last = step == STEPS - 1
        one_halo = swapped(one, "gy", 0)
        two_halo = swapped(two, "gy", 1)
        xhalo = lax.ppermute(send_x, "gx", swap)
        if entries is None:
            entries = make_entries(local_len // NVX, verts, [column_density, column_type])
        if step == 0:
            advected, fold = transport(rows_x, field, xhalo, [one_halo, two_halo, one, two], entries)
        else:
            advected, fold = transport(rows_x, field, xhalo, [], entries)
            advected, fold = add_columns(rows_x, one, two, far, one_halo, two_halo, advected, fold, entries)
        other = lax.ppermute(fold, "vert", swap)
        part = own_gain(fold, entries)
        out = collide(rows_x, other, entries, part, advected, column_density, column_type, row_inflow, last)
        if not last:
            field, one, two, send_x, far = out
    return out.reshape(rows_x, rows_y, local_len)


def solution(mesh):
    placed = (P("gx", "gy", "vert"), P("gx", "gy"), P("gx", "gy"), P("vert"))
    return jax.shard_map(
        per_device, mesh=mesh, in_specs=placed, out_specs=P("gx", "gy", "vert"), check_vma=False
    )
```

```python
import functools
import math

import jax
import jax.numpy as jnp
from jax import lax
from jax.experimental import pallas as pl
from jax.experimental.pallas import tpu as pltpu
from jax.sharding import PartitionSpec as P

NVX = 64
STEPS = 2
HALF = NVX // 2
LANES = 128
GROUP = LANES // HALF

vel_max = 4.0
time_step = 0.1
grad_scale = 2.5
collision_rate = 0.2
spacing = 2.0 * vel_max / NVX
middle = 0.5 * (NVX - 1)

MIB = 1024 * 1024
WHOLE = pl.BlockSpec(memory_space=pltpu.VMEM)

EXPONENT = 0.125 * math.log2(math.e)
ENTRY_SCALE = grad_scale * spacing * spacing * math.sqrt(EXPONENT)


SMALL = pl.CostEstimate(flops=1, bytes_accessed=1, transcendentals=0)


def place():
    at_x = lax.axis_index("gx")
    more = (at_x > 0, at_x < lax.axis_size("gx") - 1)
    return [lax.axis_index("vert"), lax.axis_size("vert"), *(m.astype(jnp.int32) for m in more), lax.axis_index("gy") % 2]


def room(mib):
    return pltpu.CompilerParams(vmem_limit_bytes=mib * MIB)


def in_vmem(value):
    return pltpu.with_memory_space_constraint(value, pltpu.VMEM)


def velocity_parts(index):
    row_portion = (index // NVX).astype(jnp.float32)
    col_part = (index % NVX).astype(jnp.float32)
    vel_x = (row_portion - middle) * spacing
    vel_y = (col_part - middle) * spacing
    return (vel_x, vel_y)


def iota(shape, dim):
    return lax.broadcasted_iota(jnp.int32, shape, dim)


def slot_order(slot):
    return lax.rem(slot, 2) * 2 + lax.div(slot, 2)


def entries_body(local, sources, *rest):
    here_ref = place()
    hi_ref, lo_ref, energy_ref, gauss_ref = rest[-4:]
    me = here_ref[0]
    groups = local // GROUP
    rows = 8
    lane = iota((1, LANES), 1)
    slot = slot_order(lane // HALF)
    vy = ((lane % HALF).astype(jnp.float32) - middle) * spacing

    def one(index, carry):
        source = lax.div(index, GROUP)
        r = lax.rem(index, GROUP)
        first = lax.rem(me + source, here_ref[1]) * local
        pair, lanes = iota((groups * groups, LANES), 0), iota((groups * groups, LANES), 1)
        out_x = ((me * local + pair // groups * GROUP + slot_order(lanes // HALF)).astype(jnp.float32) - middle) * spacing
        out_y = ((lanes % HALF).astype(jnp.float32) - middle) * spacing
        in_x = ((first + pair % groups * GROUP + r).astype(jnp.float32) - middle) * spacing
        out_sq, in_sq = out_x * out_x + out_y * out_y, in_x * in_x
        energy_ref[...] = EXPONENT * (out_sq - in_sq)
        gauss_ref[...] = jnp.exp((out_sq + in_sq) * -0.25) * (0.5 / EXPONENT)
        for part in range(HALF // rows):
            wy = ((iota((rows, LANES), 0) + part * rows).astype(jnp.float32) - middle) * spacing
            in_y_sq = EXPONENT * wy * wy
            in_y_gauss = jnp.exp(wy * wy * -0.25)
            dy_same = EXPONENT * ((vy - wy) ** 2 + spacing * spacing)
            dy_flip = EXPONENT * ((vy + wy) ** 2 + spacing * spacing)
            for m in range(1 - groups, groups):
                apart = (me * local - first + m * GROUP - r + slot).astype(jnp.float32) * spacing
                dx_sq = EXPONENT * apart * apart
                same_sq, flip_sq = dx_sq + dy_same, dx_sq + dy_flip
                same_inv, flip_inv = lax.rsqrt(same_sq), lax.rsqrt(flip_sq)
                same_inv_sq, flip_inv_sq = same_inv * same_inv, flip_inv * flip_inv
                same_top, flip_top = jnp.log2(same_inv) - same_sq, jnp.log2(flip_inv) - flip_sq
                same_r, flip_r = same_sq * same_inv, flip_sq * flip_inv
                sum_r, gap_r = same_r + flip_r, same_r - flip_r
                for g in range(max(0, m), min(groups, groups + m)):
                    k = g - m
                    at = g * groups + k
                    energy = energy_ref[at : at + 1, :] - in_y_sq
                    energy_sq = energy * energy
                    gauss = gauss_ref[at : at + 1, :] * in_y_gauss
                    same = jnp.exp2(same_top - energy_sq * same_inv_sq)
                    flip = jnp.exp2(flip_top - energy_sq * flip_inv_sq)
                    to = (k * GROUP + slot_order(r)) * HALF + part * rows
                    to = pl.ds(pl.multiple_of(to, rows), rows)
                    cols = slice(g * LANES, (g + 1) * LANES)
                    values = ((same + flip) - gauss * sum_r, (same - flip) - gauss * gap_r)
                    for parity, value in enumerate(values):
                        high = value.astype(jnp.bfloat16)
                        hi_ref[source, parity, to, cols] = high
                        lo_ref[source, parity, to, cols] = (value - high.astype(jnp.float32)).astype(jnp.bfloat16)
        return carry

    lax.fori_loop(0, sources * GROUP, one, 0)


def make_entries(local, sources, ahead_of):
    size = local * HALF
    shape = pltpu.VMEM((sources, 2, size, size), jnp.bfloat16)
    return pl.pallas_call(
        functools.partial(entries_body, local, sources),
        in_specs=[WHOLE] * len(ahead_of),
        out_specs=[WHOLE, WHOLE],
        out_shape=[shape, shape],
        scratch_shapes=[pltpu.VMEM(((local // GROUP) ** 2, LANES), jnp.float32)] * 2,
        compiler_params=room(8),
        cost_estimate=SMALL,
        name="kernel_entries",
    )(*map(in_vmem, ahead_of))


def pack_far(far, ahead, low_half):
    count = far.shape[0] // 2
    if ahead:
        return jnp.where(low_half, pltpu.roll(far[count:], LANES - HALF, 1), far[:count])
    return jnp.where(low_half, far[:count], pltpu.roll(far[count:], HALF, 1))


def unpack_far(packed, ahead):
    shift = HALF if ahead else LANES - HALF
    parts = [packed[:, i : i + LANES] for i in range(0, packed.shape[1], LANES)]
    turned = jnp.concatenate([pltpu.roll(p, shift, 1) for p in parts], axis=1)
    return jnp.concatenate([packed, turned], axis=0)


def outer_columns(field, rows_x, span, upper):
    rows_y = field.shape[0] // rows_x
    half = rows_y // 2
    at = iota((half, span.stop - span.start), 0)
    shift = 1 - half if upper else 0
    nears, fars = [], []
    for first in range(0, rows_x, half):
        near = far = None
        for s in range(half):
            start = (first + s) * rows_y + (half if upper else 0)
            turned = pltpu.roll(field[start : start + half, span], (s + shift) % half, 0)
            near = turned if near is None else jnp.where(at == s, turned, near)
            beside = (s - 1 if upper else s + 1) % half
            far = turned if far is None else jnp.where(at == beside, turned, far)
        nears.append(near)
        fars.append(pltpu.roll(far, 1 if upper else half - 1, 0))
    return jnp.concatenate(nears, axis=0), jnp.concatenate(fars, axis=0)


def write_edges(here_ref, rows_x, field, span, edge_refs):
    one_ref, two_ref, xsend_ref, far_ref = edge_refs
    rows_y = field.shape[0] // rows_x
    to_next = here_ref[3] > 0
    for layer in range(2):
        low_row, high_row = (field[x * rows_y : (x + 1) * rows_y, span] for x in (layer, rows_x - 2 + layer))
        xsend_ref[layer, :, span] = jnp.where(to_next, high_row, low_row)
    odd = here_ref[4] > 0
    low_near, low_far = outer_columns(field, rows_x, span, False)
    high_near, high_far = outer_columns(field, rows_x, span, True)
    one_ref[:rows_x, span] = jnp.where(odd, low_near, high_near)
    two_ref[:rows_x, span] = jnp.where(odd, high_near, low_near)
    far_ref[0, :, span] = jnp.where(odd, low_far, high_far)
    far_ref[1, :, span] = jnp.where(odd, high_far, low_far)
    low_half = iota((rows_x // 2, LANES), 1) % NVX < HALF
    for i in range(0, span.stop - span.start, LANES):
        at = slice(span.start + i, span.start + i + LANES)
        low = pack_far(low_far[:, i : i + LANES], False, low_half)
        high = pack_far(high_far[:, i : i + LANES], True, low_half)
        one_ref[rows_x:, at] = jnp.where(odd, low, high)
        two_ref[rows_x:, at] = jnp.where(odd, high, low)


def edge_shapes(rows_x, rows_y, local_len):
    edge_y = pltpu.VMEM((rows_x + rows_x // 2, local_len), jnp.float32)
    layers_x = pltpu.VMEM((2, rows_y, local_len), jnp.float32)
    return [edge_y, edge_y, layers_x, pltpu.VMEM((2, rows_x, local_len), jnp.float32)]


def stage_body(wide, rows_x, from_ref, field, *rest):
    here_ref = place()
    *edge_refs, sems = rest
    spans = [slice(i, i + wide) for i in range(0, field.shape[1], wide)]
    copies = [pltpu.make_async_copy(from_ref.at[:, s], field.at[:, s], sems.at[i]) for i, s in enumerate(spans)]
    for copy in copies:
        copy.start()
    for copy, span in zip(copies, spans):
        copy.wait()
        write_edges(here_ref, rows_x, field, span, edge_refs)


def stage(rows_x, field):
    cells, local_len = field.shape
    wide = local_len // 4
    return pl.pallas_call(
        functools.partial(stage_body, wide, rows_x),
        in_specs=[pl.BlockSpec(memory_space=pltpu.HBM)],
        out_specs=[WHOLE] * 5,
        out_shape=[pltpu.VMEM(field.shape, jnp.float32)] + edge_shapes(rows_x, cells // rows_x, local_len),
        scratch_shapes=[pltpu.SemaphoreType.DMA((4,))],
        compiler_params=room(4),
        name="stage",
    )(pltpu.with_memory_space_constraint(field, pltpu.HBM))


def beyond(here_ref, rows_x, one_ref, two_ref, cols):
    odd = here_ref[4] > 0
    one, two = one_ref[:, cols], two_ref[:, cols]
    low, high = jnp.where(odd, one, two), jnp.where(odd, two, one)
    return unpack_far(low[rows_x:], True), low[:rows_x], high[:rows_x], unpack_far(high[rows_x:], False)


def minmod(a, b):
    return jnp.maximum(jnp.minimum(a, b), 0.0) + jnp.minimum(jnp.maximum(a, b), 0.0)


def fold_masks(rows):
    lane = iota((rows, LANES), 1)
    slot = lane // HALF
    even = slot % 2 == 0
    turned = jnp.where(even, 2 - slot, slot) * HALF + (HALF - 1) - lane % HALF
    return even, turned


def folded(a, b, even, turned):
    near = jnp.where(even, a, b)
    far = pltpu.roll(jnp.where(even, b, a), HALF, 1)
    lower = jnp.where(even, near, far)
    upper = jnp.take_along_axis(jnp.where(even, far, near), turned, axis=1)
    return lower + upper, lower - upper


def unfolded(lower, upper, even, turned):
    upper = jnp.take_along_axis(upper, turned, axis=1)
    near = jnp.where(even, lower, upper)
    far = pltpu.roll(jnp.where(even, upper, lower), LANES - HALF, 1)
    return jnp.where(even, near, far), jnp.where(even, far, near)


def transport_body(wide, rows_x, whole, field_ref, xhalo_ref, *rest):
    here_ref = place()
    if whole:
        one_halo, two_halo, one_ref, two_ref = rest[:4]
        adv_ref, fold_ref, low_edge, high_edge, low_near, high_near = rest[-6:]
    else:
        adv_ref, fold_ref = rest[-2:]
    cells, local_len = field_ref.shape
    rows_y = cells // rows_x
    has_low = here_ref[2] > 0
    has_high = here_ref[3] > 0
    at_y = iota((rows_y, wide), 0)
    first_y = at_y == 0
    last_y = at_y == rows_y - 1
    even, turned = fold_masks(rows_y)

    def chunk(c, carry):
        cols = pl.ds(pl.multiple_of(c * wide, wide), wide)
        vx, vy = velocity_parts(here_ref[0] * local_len + c * wide + iota((1, wide), 1))
        ax = time_step * vx
        ay = time_step * vy
        bx = 0.5 * jnp.abs(ax) * (1.0 - jnp.abs(ax))
        by = 0.5 * jnp.abs(ay) * (1.0 - jnp.abs(ay))
        ahead_x = ax > 0
        ahead_y = ay > 0

        def face_y(f0, f1, f2):
            return ay * f1 + by * minmod(f1 - f0, f2 - f1)

        if whole:
            low_far, low_near[...], high_near[...], high_far = beyond(here_ref, rows_x, one_halo, two_halo, cols)
            odd = here_ref[4] > 0
            one, two = one_ref[:rows_x, cols], two_ref[:rows_x, cols]
            low_edge[...] = face_y(low_far, low_near[...], jnp.where(odd, one, two))
            high_edge[...] = face_y(jnp.where(odd, two, one), high_near[...], high_far)

        def row(i):
            if i < 0:
                return jnp.where(has_low, xhalo_ref[i + 2, :, cols], 0.0)
            if i >= rows_x:
                return jnp.where(has_high, xhalo_ref[i - rows_x, :, cols], 0.0)
            return field_ref[i * rows_y : (i + 1) * rows_y, cols]

        near = [row(-2), row(-1), row(0)]
        low, high = near[1] - near[0], near[2] - near[1]
        face = [ax * near[1] + bx * minmod(low, high)]
        for i in range(rows_x + 1):
            near = [near[1], near[2], row(i + 1)]
            low, high = high, near[2] - near[1]
            face.append(ax * near[1] + bx * minmod(low, high))
            if i == 0:
                continue
            x = i - 1
            here = near[0]
            row_term = jnp.where(ahead_x, face[x + 1] - face[x], face[x + 2] - face[x + 1])
            if whole:
                below = jnp.where(first_y, low_near[x : x + 1], pltpu.roll(here, 1, 0))
                above = jnp.where(last_y, high_near[x : x + 1], pltpu.roll(here, rows_y - 1, 0))
                mine = face_y(below, here, above)
                mine_below = jnp.where(first_y, low_edge[x : x + 1], pltpu.roll(mine, 1, 0))
                mine_above = jnp.where(last_y, high_edge[x : x + 1], pltpu.roll(mine, rows_y - 1, 0))
                col_term = jnp.where(ahead_y, mine - mine_below, mine_above - mine)
            else:
                rise = here - pltpu.roll(here, 1, 0)
                mine = ay * here + by * minmod(rise, pltpu.roll(rise, rows_y - 1, 0))
                mine = jnp.where(first_y | last_y, 0.0, mine)
                step = mine - pltpu.roll(mine, 1, 0)
                col_term = jnp.where(ahead_y, step, pltpu.roll(step, rows_y - 1, 0))
            moved = here - row_term - col_term
            at = slice(x * rows_y, (x + 1) * rows_y)
            adv_ref[at, cols] = moved
            for part in range(wide // (2 * LANES)):
                first = 2 * part * LANES
                both = folded(moved[:, first : first + LANES], moved[:, first + LANES : first + 2 * LANES], even, turned)
                to = pl.ds(pl.multiple_of(c * (wide // 2) + part * LANES, LANES), LANES)
                fold_ref[0, at, to], fold_ref[1, at, to] = both
        return carry

    lax.fori_loop(0, local_len // wide, chunk, 0)


def columns_body(wide, rows_x, one_ref, two_ref, far_ref, one_halo, two_halo, adv_in, fold_in, *rest):
    here_ref = place()
    adv_ref, fold_ref = rest[-2:]
    cells, local_len = adv_in.shape
    rows_y = cells // rows_x
    half = rows_y // 2
    masks = fold_masks(rows_x)

    def spread(parts, from_ref, to_ref, cols):
        at = iota((half, parts[0].shape[1]), 0)
        even = at % 2 == 0
        for first in range(0, rows_x, half):
            for upper in range(2):
                a, b = (part[first : first + half] for part in parts[2 * upper : 2 * upper + 2])
                b = pltpu.roll(b, 1, 0)
                pairs = jnp.where(even, a, b), jnp.where(even, b, a)
                place = upper * (half - 2)
                here = (at == place) | (at == place + 1)
                done = []
                for s in range(half):
                    start = (first + s) * rows_y + upper * half
                    rows = slice(start, start + half)
                    more = jnp.where(here, pltpu.roll(pairs[s % 2], (place - s) % half, 0), 0.0)
                    done.append((rows, from_ref[rows, cols] + more))
                for rows, value in done:
                    to_ref[rows, cols] = value

    def chunk(c, carry):
        cols = pl.ds(pl.multiple_of(c * wide, wide), wide)
        fold_cols = pl.ds(pl.multiple_of(c * (wide // 2), wide // 2), wide // 2)
        _, vy = velocity_parts(here_ref[0] * local_len + c * wide + iota((1, wide), 1))
        ay = time_step * vy
        by = 0.5 * jnp.abs(ay) * (1.0 - jnp.abs(ay))
        ahead = ay > 0

        def face(f0, f1, f2):
            return ay * f1 + by * minmod(f1 - f0, f2 - f1)

        low_far, low_near, high_near, high_far = beyond(here_ref, rows_x, one_halo, two_halo, cols)
        odd = here_ref[4] > 0
        one, two = one_ref[:rows_x, cols], two_ref[:rows_x, cols]
        low, high = jnp.where(odd, one, two), jnp.where(odd, two, one)
        one, two = far_ref[0, :, cols], far_ref[1, :, cols]
        second, last_but_one = jnp.where(odd, one, two), jnp.where(odd, two, one)
        before = face(low_far, low_near, low)
        first = face(low_near, low, second)
        last = face(last_but_one, high, high_near)
        after = face(high, high_near, high_far)
        parts = [
            jnp.where(ahead, before - first, first),
            jnp.where(ahead, first, 0.0),
            jnp.where(ahead, 0.0, -last),
            jnp.where(ahead, -last, last - after),
        ]
        spread(parts, adv_in, adv_ref, cols)
        both = []
        for part in parts:
            pairs = [folded(part[:, j : j + LANES], part[:, j + LANES : j + 2 * LANES], *masks) for j in range(0, wide, 2 * LANES)]
            both.append([jnp.concatenate(tiles, axis=1) for tiles in zip(*pairs)])
        for parity in range(2):
            spread([pair[parity] for pair in both], fold_in.at[parity], fold_ref.at[parity], fold_cols)
        return carry

    lax.fori_loop(0, local_len // wide, chunk, 0)


def transport(rows_x, field, xhalo, yhalos, entries):
    cells, local_len = field.shape
    wide = 4 * LANES
    return pl.pallas_call(
        functools.partial(transport_body, wide, rows_x, bool(yhalos)),
        in_specs=[WHOLE] * (2 + len(yhalos) + len(entries)),
        out_specs=[WHOLE] * 2,
        out_shape=[pltpu.VMEM(field.shape, jnp.float32), pltpu.VMEM((2, cells, local_len // 2), jnp.float32)],
        scratch_shapes=[pltpu.VMEM((rows_x, wide), jnp.float32)] * (4 if yhalos else 0),
        compiler_params=room(4),
        cost_estimate=SMALL,
        name="transport" if yhalos else "inner_transport",
    )(*map(in_vmem, (field, xhalo, *yhalos, *entries)))


def add_columns(rows_x, one, two, far, one_halo, two_halo, advected, fold, entries):
    wide = 4 * LANES
    return pl.pallas_call(
        functools.partial(columns_body, wide, rows_x),
        in_specs=[WHOLE] * (7 + len(entries)),
        out_specs=[WHOLE] * 2,
        out_shape=[pltpu.VMEM(advected.shape, jnp.float32), pltpu.VMEM(fold.shape, jnp.float32)],
        input_output_aliases={5: 0, 6: 1},
        compiler_params=room(4),
        cost_estimate=SMALL,
        name="add_columns",
    )(*map(in_vmem, (one, two, far, one_halo, two_halo, advected, fold, *entries)))


def split_into(value_ref, high, low):
    for parity in range(2):
        value = value_ref[parity]
        rounded = value.astype(jnp.bfloat16)
        high[parity] = rounded
        low[parity] = (value - rounded.astype(jnp.float32)).astype(jnp.bfloat16)


def product(high, low, hi_ref, lo_ref, source, parity, cols):
    dot = functools.partial(jnp.dot, preferred_element_type=jnp.float32)
    tile = hi_ref[source, parity, :, cols]
    return dot(high[parity], tile) + (dot(low[parity], tile) + dot(high[parity], lo_ref[source, parity, :, cols]))


def own_body(wide, fold_ref, hi_ref, lo_ref, adv_ref, density_ref, out_ref, keep_ref, high, low):
    here_ref = place()
    split_into(fold_ref, high, low)
    for j in range(fold_ref.shape[2] // wide):
        cols = slice(j * wide, (j + 1) * wide)
        for parity in range(2):
            out_ref[parity, :, cols] = product(high, low, hi_ref, lo_ref, 0, parity, cols)
    cells, local_len = adv_ref.shape
    rate = jnp.broadcast_to(collision_rate * density_ref[...], (cells, LANES))
    for first in range(0, local_len, LANES):
        at = slice(first, first + LANES)
        vx, vy = velocity_parts(here_ref[0] * local_len + first + iota((1, LANES), 1))
        nu = 1.0 + (vx * vx + vy * vy) / 8.0
        keep_ref[:, at] = adv_ref[:, at] * (1.0 - rate * nu)


def own_gain(fold, entries, advected, density):
    _, cells, size = fold.shape
    return pl.pallas_call(
        functools.partial(own_body, 2 * LANES),
        in_specs=[WHOLE] * 5,
        out_specs=[WHOLE] * 2,
        out_shape=[pltpu.VMEM(fold.shape, jnp.float32), pltpu.VMEM(advected.shape, jnp.float32)],
        scratch_shapes=[pltpu.VMEM(fold.shape, jnp.bfloat16)] * 2,
        compiler_params=room(8),
        cost_estimate=SMALL,
        name="own_gain",
    )(*map(in_vmem, (fold, *entries, advected, density)))


def collide_body(
    wide, rows_x, last, fold_ref, hi_ref, lo_ref, part_ref, keep_ref, density_ref, type_ref, inflow_ref, *rest
):
    here_ref = place()
    if last:
        out_ref, high, low, field, sems = rest
    else:
        field, *edge_refs, high, low = rest
    cells, local_len = keep_ref.shape
    split_into(fold_ref, high, low)
    even_slot, turned = fold_masks(cells)
    gain_rate = jnp.broadcast_to(collision_rate * ENTRY_SCALE * density_ref[...], (cells, LANES))
    kind = jnp.broadcast_to(type_ref[...], (cells, LANES))
    wall = kind == 1
    inlet = kind == 2
    copies = []
    for j in range(local_len // (2 * wide)):
        cols = slice(j * wide, (j + 1) * wide)
        even, odd = (part_ref[p, :, cols] + product(high, low, hi_ref, lo_ref, 1, p, cols) for p in range(2))
        lower = even + odd
        upper = even - odd
        for part in range(wide // LANES):
            group = slice(part * LANES, (part + 1) * LANES)
            for side, gain in enumerate(unfolded(lower[:, group], upper[:, group], even_slot, turned)):
                first = 2 * (j * wide + part * LANES) + side * LANES
                at = slice(first, first + LANES)
                done = keep_ref[:, at] + gain_rate * gain
                field[:, at] = jnp.where(wall, 0.0, jnp.where(inlet, inflow_ref[:, at], done))
            span = slice(first - LANES, first + LANES)
            if last:
                i = first // (2 * LANES)
                copy = pltpu.make_async_copy(field.at[:, span], out_ref.at[:, span], sems.at[i])
                copy.start()
                copies.append(copy)
            else:
                write_edges(here_ref, rows_x, field, span, edge_refs)
    for copy in copies:
        copy.wait()


def collide(rows_x, fold, entries, part, kept, density, kind, inflow, last):
    _, cells, size = fold.shape
    local_len = kept.shape[1]
    wide = 2 * LANES
    halves = [pltpu.VMEM(fold.shape, jnp.bfloat16)] * 2
    if last:
        out_specs = pl.BlockSpec(memory_space=pl.ANY)
        out_shape = jax.ShapeDtypeStruct(kept.shape, jnp.float32)
        scratch = halves + [pltpu.VMEM(kept.shape, jnp.float32), pltpu.SemaphoreType.DMA((size // LANES,))]
    else:
        out_specs = [WHOLE] * 5
        out_shape = [pltpu.VMEM(kept.shape, jnp.float32)] + edge_shapes(rows_x, cells // rows_x, local_len)
        scratch = halves
    return pl.pallas_call(
        functools.partial(collide_body, wide, rows_x, last),
        in_specs=[WHOLE] * 8,
        out_specs=out_specs,
        out_shape=out_shape,
        scratch_shapes=scratch,
        compiler_params=room(12),
        cost_estimate=SMALL,
        name="collide",
    )(in_vmem(fold), in_vmem(entries[0]), in_vmem(entries[1]), in_vmem(part), in_vmem(kept), density, kind, inflow)


def swapped(block, axis, first):
    pairs = [(i, i + 1) for i in range(first, lax.axis_size(axis) - 1, 2)]
    return lax.ppermute(block, axis, [pair for i, j in pairs for pair in ((i, j), (j, i))])


def per_device(distribution, density, cell_type, inflow):
    rows_x, rows_y, local_len = distribution.shape
    cells = rows_x * rows_y
    vert = lax.axis_index("vert")
    verts = lax.axis_size("vert")
    at_x = lax.axis_index("gx")
    size_x = lax.axis_size("gx")
    assert size_x == 2 and verts == 2
    column_density = density.reshape(cells, 1)
    column_type = cell_type.reshape(cells, 1)
    row_inflow = inflow.reshape(1, local_len)
    swap = [(0, 1), (1, 0)]
    field, one, two, send_x, far = stage(rows_x, distribution.reshape(cells, local_len))
    entries = None
    for step in range(STEPS):
        last = step == STEPS - 1
        one_halo = swapped(one, "gy", 0)
        two_halo = swapped(two, "gy", 1)
        xhalo = lax.ppermute(send_x, "gx", swap)
        if entries is None:
            entries = make_entries(local_len // NVX, verts, [column_density, column_type])
        if step == 0:
            advected, fold = transport(rows_x, field, xhalo, [one_halo, two_halo, one, two], entries)
        else:
            advected, fold = transport(rows_x, field, xhalo, [], entries)
            advected, fold = add_columns(rows_x, one, two, far, one_halo, two_halo, advected, fold, entries)
        other = lax.ppermute(fold, "vert", swap)
        part, kept = own_gain(fold, entries, advected, column_density)
        out = collide(rows_x, other, entries, part, kept, column_density, column_type, row_inflow, last)
        if not last:
            field, one, two, send_x, far = out
    return out.reshape(rows_x, rows_y, local_len)


def solution(mesh):
    placed = (P("gx", "gy", "vert"), P("gx", "gy"), P("gx", "gy"), P("vert"))
    return jax.shard_map(
        per_device, mesh=mesh, in_specs=placed, out_specs=P("gx", "gy", "vert"), check_vma=False
    )
```

```python
import functools
import math

import jax
import jax.numpy as jnp
from jax import lax
from jax.experimental import pallas as pl
from jax.experimental.pallas import tpu as pltpu
from jax.sharding import PartitionSpec as P

NVX = 64
STEPS = 2
HALF = NVX // 2
LANES = 128
GROUP = LANES // HALF

vel_max = 4.0
time_step = 0.1
grad_scale = 2.5
collision_rate = 0.2
spacing = 2.0 * vel_max / NVX
middle = 0.5 * (NVX - 1)

MIB = 1024 * 1024
WHOLE = pl.BlockSpec(memory_space=pltpu.VMEM)

EXPONENT = 0.125 * math.log2(math.e)
ENTRY_SCALE = grad_scale * spacing * spacing * math.sqrt(EXPONENT)


SMALL = pl.CostEstimate(flops=1, bytes_accessed=1, transcendentals=0)


def place():
    at_x = lax.axis_index("gx")
    more = (at_x > 0, at_x < lax.axis_size("gx") - 1)
    return [lax.axis_index("vert"), lax.axis_size("vert"), *(m.astype(jnp.int32) for m in more), lax.axis_index("gy") % 2]


def room(mib):
    return pltpu.CompilerParams(vmem_limit_bytes=mib * MIB)


def in_vmem(value):
    return pltpu.with_memory_space_constraint(value, pltpu.VMEM)


def velocity_parts(index):
    row_portion = (index // NVX).astype(jnp.float32)
    col_part = (index % NVX).astype(jnp.float32)
    vel_x = (row_portion - middle) * spacing
    vel_y = (col_part - middle) * spacing
    return (vel_x, vel_y)


def iota(shape, dim):
    return lax.broadcasted_iota(jnp.int32, shape, dim)


def slot_order(slot):
    return lax.rem(slot, 2) * 2 + lax.div(slot, 2)


def entries_body(local, sources, *rest):
    here_ref = place()
    hi_ref, lo_ref, energy_ref, gauss_ref = rest[-4:]
    me = here_ref[0]
    groups = local // GROUP
    rows = 8
    lane = iota((1, LANES), 1)
    slot = slot_order(lane // HALF)
    vy = ((lane % HALF).astype(jnp.float32) - middle) * spacing

    def one(index, carry):
        source = lax.div(index, GROUP)
        r = lax.rem(index, GROUP)
        first = lax.rem(me + source, here_ref[1]) * local
        pair, lanes = iota((groups * groups, LANES), 0), iota((groups * groups, LANES), 1)
        out_x = ((me * local + pair // groups * GROUP + slot_order(lanes // HALF)).astype(jnp.float32) - middle) * spacing
        out_y = ((lanes % HALF).astype(jnp.float32) - middle) * spacing
        in_x = ((first + pair % groups * GROUP + r).astype(jnp.float32) - middle) * spacing
        out_sq, in_sq = out_x * out_x + out_y * out_y, in_x * in_x
        energy_ref[...] = EXPONENT * (out_sq - in_sq)
        gauss_ref[...] = jnp.exp((out_sq + in_sq) * -0.25) * (0.5 / EXPONENT)
        for part in range(HALF // rows):
            wy = ((iota((rows, LANES), 0) + part * rows).astype(jnp.float32) - middle) * spacing
            in_y_sq = EXPONENT * wy * wy
            in_y_gauss = jnp.exp(wy * wy * -0.25)
            dy_same = EXPONENT * ((vy - wy) ** 2 + spacing * spacing)
            dy_flip = EXPONENT * ((vy + wy) ** 2 + spacing * spacing)
            for m in range(1 - groups, groups):
                apart = (me * local - first + m * GROUP - r + slot).astype(jnp.float32) * spacing
                dx_sq = EXPONENT * apart * apart
                same_sq, flip_sq = dx_sq + dy_same, dx_sq + dy_flip
                same_inv, flip_inv = lax.rsqrt(same_sq), lax.rsqrt(flip_sq)
                same_inv_sq, flip_inv_sq = same_inv * same_inv, flip_inv * flip_inv
                same_top, flip_top = jnp.log2(same_inv) - same_sq, jnp.log2(flip_inv) - flip_sq
                same_r, flip_r = same_sq * same_inv, flip_sq * flip_inv
                sum_r, gap_r = same_r + flip_r, same_r - flip_r
                for g in range(max(0, m), min(groups, groups + m)):
                    k = g - m
                    at = g * groups + k
                    energy = energy_ref[at : at + 1, :] - in_y_sq
                    energy_sq = energy * energy
                    gauss = gauss_ref[at : at + 1, :] * in_y_gauss
                    same = jnp.exp2(same_top - energy_sq * same_inv_sq)
                    flip = jnp.exp2(flip_top - energy_sq * flip_inv_sq)
                    to = (k * GROUP + slot_order(r)) * HALF + part * rows
                    to = pl.ds(pl.multiple_of(to, rows), rows)
                    cols = slice(g * LANES, (g + 1) * LANES)
                    values = ((same + flip) - gauss * sum_r, (same - flip) - gauss * gap_r)
                    for parity, value in enumerate(values):
                        high = value.astype(jnp.bfloat16)
                        hi_ref[source, parity, to, cols] = high
                        lo_ref[source, parity, to, cols] = (value - high.astype(jnp.float32)).astype(jnp.bfloat16)
        return carry

    lax.fori_loop(0, sources * GROUP, one, 0)


def make_entries(local, sources, ahead_of):
    size = local * HALF
    shape = pltpu.VMEM((sources, 2, size, size), jnp.bfloat16)
    return pl.pallas_call(
        functools.partial(entries_body, local, sources),
        in_specs=[WHOLE] * len(ahead_of),
        out_specs=[WHOLE, WHOLE],
        out_shape=[shape, shape],
        scratch_shapes=[pltpu.VMEM(((local // GROUP) ** 2, LANES), jnp.float32)] * 2,
        compiler_params=room(8),
        cost_estimate=SMALL,
        name="kernel_entries",
    )(*map(in_vmem, ahead_of))


def pack_far(far, ahead, low_half):
    count = far.shape[0] // 2
    if ahead:
        return jnp.where(low_half, pltpu.roll(far[count:], LANES - HALF, 1), far[:count])
    return jnp.where(low_half, far[:count], pltpu.roll(far[count:], HALF, 1))


def unpack_far(packed, ahead):
    shift = HALF if ahead else LANES - HALF
    parts = [packed[:, i : i + LANES] for i in range(0, packed.shape[1], LANES)]
    turned = jnp.concatenate([pltpu.roll(p, shift, 1) for p in parts], axis=1)
    return jnp.concatenate([packed, turned], axis=0)


def outer_columns(field, rows_x, span, upper):
    rows_y = field.shape[0] // rows_x
    half = rows_y // 2
    at = iota((half, span.stop - span.start), 0)
    shift = 1 - half if upper else 0
    nears, fars = [], []
    for first in range(0, rows_x, half):
        near = far = None
        for s in range(half):
            start = (first + s) * rows_y + (half if upper else 0)
            turned = pltpu.roll(field[start : start + half, span], (s + shift) % half, 0)
            near = turned if near is None else jnp.where(at == s, turned, near)
            beside = (s - 1 if upper else s + 1) % half
            far = turned if far is None else jnp.where(at == beside, turned, far)
        nears.append(near)
        fars.append(pltpu.roll(far, 1 if upper else half - 1, 0))
    return jnp.concatenate(nears, axis=0), jnp.concatenate(fars, axis=0)


def write_edges(here_ref, rows_x, field, span, edge_refs):
    one_ref, two_ref, xsend_ref, far_ref = edge_refs
    rows_y = field.shape[0] // rows_x
    to_next = here_ref[3] > 0
    for layer in range(2):
        low_row, high_row = (field[x * rows_y : (x + 1) * rows_y, span] for x in (layer, rows_x - 2 + layer))
        xsend_ref[layer, :, span] = jnp.where(to_next, high_row, low_row)
    odd = here_ref[4] > 0
    low_near, low_far = outer_columns(field, rows_x, span, False)
    high_near, high_far = outer_columns(field, rows_x, span, True)
    one_ref[:rows_x, span] = jnp.where(odd, low_near, high_near)
    two_ref[:rows_x, span] = jnp.where(odd, high_near, low_near)
    far_ref[0, :, span] = jnp.where(odd, low_far, high_far)
    far_ref[1, :, span] = jnp.where(odd, high_far, low_far)
    low_half = iota((rows_x // 2, LANES), 1) % NVX < HALF
    for i in range(0, span.stop - span.start, LANES):
        at = slice(span.start + i, span.start + i + LANES)
        low = pack_far(low_far[:, i : i + LANES], False, low_half)
        high = pack_far(high_far[:, i : i + LANES], True, low_half)
        one_ref[rows_x:, at] = jnp.where(odd, low, high)
        two_ref[rows_x:, at] = jnp.where(odd, high, low)


def edge_shapes(rows_x, rows_y, local_len):
    edge_y = pltpu.VMEM((rows_x + rows_x // 2, local_len), jnp.float32)
    layers_x = pltpu.VMEM((2, rows_y, local_len), jnp.float32)
    return [edge_y, edge_y, layers_x, pltpu.VMEM((2, rows_x, local_len), jnp.float32)]


def stage_body(wide, rows_x, from_ref, field, *rest):
    here_ref = place()
    *edge_refs, sems = rest
    spans = [slice(i, i + wide) for i in range(0, field.shape[1], wide)]
    copies = [pltpu.make_async_copy(from_ref.at[:, s], field.at[:, s], sems.at[i]) for i, s in enumerate(spans)]
    for copy in copies:
        copy.start()
    for copy, span in zip(copies, spans):
        copy.wait()
        write_edges(here_ref, rows_x, field, span, edge_refs)


def stage(rows_x, field):
    cells, local_len = field.shape
    wide = local_len // 4
    return pl.pallas_call(
        functools.partial(stage_body, wide, rows_x),
        in_specs=[pl.BlockSpec(memory_space=pltpu.HBM)],
        out_specs=[WHOLE] * 5,
        out_shape=[pltpu.VMEM(field.shape, jnp.float32)] + edge_shapes(rows_x, cells // rows_x, local_len),
        scratch_shapes=[pltpu.SemaphoreType.DMA((4,))],
        compiler_params=room(4),
        name="stage",
    )(pltpu.with_memory_space_constraint(field, pltpu.HBM))


def beyond(here_ref, rows_x, one_ref, two_ref, cols):
    odd = here_ref[4] > 0
    one, two = one_ref[:, cols], two_ref[:, cols]
    low, high = jnp.where(odd, one, two), jnp.where(odd, two, one)
    return unpack_far(low[rows_x:], True), low[:rows_x], high[:rows_x], unpack_far(high[rows_x:], False)


def minmod(a, b):
    return jnp.maximum(jnp.minimum(a, b), 0.0) + jnp.minimum(jnp.maximum(a, b), 0.0)


def fold_masks(rows):
    lane = iota((rows, LANES), 1)
    slot = lane // HALF
    even = slot % 2 == 0
    turned = jnp.where(even, 2 - slot, slot) * HALF + (HALF - 1) - lane % HALF
    return even, turned


def folded(a, b, even, turned):
    near = jnp.where(even, a, b)
    far = pltpu.roll(jnp.where(even, b, a), HALF, 1)
    lower = jnp.where(even, near, far)
    upper = jnp.take_along_axis(jnp.where(even, far, near), turned, axis=1)
    return lower + upper, lower - upper


def unfolded(lower, upper, even, turned):
    upper = jnp.take_along_axis(upper, turned, axis=1)
    near = jnp.where(even, lower, upper)
    far = pltpu.roll(jnp.where(even, upper, lower), LANES - HALF, 1)
    return jnp.where(even, near, far), jnp.where(even, far, near)


def transport_body(wide, rows_x, whole, field_ref, xhalo_ref, *rest):
    here_ref = place()
    if whole:
        one_halo, two_halo, one_ref, two_ref = rest[:4]
        adv_ref, fold_ref, low_edge, high_edge, low_near, high_near = rest[-6:]
    else:
        adv_ref, fold_ref = rest[-2:]
    cells, local_len = field_ref.shape
    rows_y = cells // rows_x
    has_low = here_ref[2] > 0
    has_high = here_ref[3] > 0
    at_y = iota((rows_y, wide), 0)
    first_y = at_y == 0
    last_y = at_y == rows_y - 1
    even, turned = fold_masks(rows_y)

    def chunk(c, carry):
        cols = pl.ds(pl.multiple_of(c * wide, wide), wide)
        vx, vy = velocity_parts(here_ref[0] * local_len + c * wide + iota((1, wide), 1))
        ax = time_step * vx
        ay = time_step * vy
        bx = 0.5 * jnp.abs(ax) * (1.0 - jnp.abs(ax))
        by = 0.5 * jnp.abs(ay) * (1.0 - jnp.abs(ay))
        ahead_x = ax > 0
        ahead_y = ay > 0

        def face_y(f0, f1, f2):
            return ay * f1 + by * minmod(f1 - f0, f2 - f1)

        if whole:
            low_far, low_near[...], high_near[...], high_far = beyond(here_ref, rows_x, one_halo, two_halo, cols)
            odd = here_ref[4] > 0
            one, two = one_ref[:rows_x, cols], two_ref[:rows_x, cols]
            low_edge[...] = face_y(low_far, low_near[...], jnp.where(odd, one, two))
            high_edge[...] = face_y(jnp.where(odd, two, one), high_near[...], high_far)

        def row(i):
            if i < 0:
                return jnp.where(has_low, xhalo_ref[i + 2, :, cols], 0.0)
            if i >= rows_x:
                return jnp.where(has_high, xhalo_ref[i - rows_x, :, cols], 0.0)
            return field_ref[i * rows_y : (i + 1) * rows_y, cols]

        near = [row(-2), row(-1), row(0)]
        low, high = near[1] - near[0], near[2] - near[1]
        face = [ax * near[1] + bx * minmod(low, high)]
        for i in range(rows_x + 1):
            near = [near[1], near[2], row(i + 1)]
            low, high = high, near[2] - near[1]
            face.append(ax * near[1] + bx * minmod(low, high))
            if i == 0:
                continue
            x = i - 1
            here = near[0]
            row_term = jnp.where(ahead_x, face[x + 1] - face[x], face[x + 2] - face[x + 1])
            if whole:
                below = jnp.where(first_y, low_near[x : x + 1], pltpu.roll(here, 1, 0))
                above = jnp.where(last_y, high_near[x : x + 1], pltpu.roll(here, rows_y - 1, 0))
                mine = face_y(below, here, above)
                mine_below = jnp.where(first_y, low_edge[x : x + 1], pltpu.roll(mine, 1, 0))
                mine_above = jnp.where(last_y, high_edge[x : x + 1], pltpu.roll(mine, rows_y - 1, 0))
                col_term = jnp.where(ahead_y, mine - mine_below, mine_above - mine)
            else:
                rise = here - pltpu.roll(here, 1, 0)
                mine = ay * here + by * minmod(rise, pltpu.roll(rise, rows_y - 1, 0))
                mine = jnp.where(first_y | last_y, 0.0, mine)
                step = mine - pltpu.roll(mine, 1, 0)
                col_term = jnp.where(ahead_y, step, pltpu.roll(step, rows_y - 1, 0))
            moved = here - row_term - col_term
            at = slice(x * rows_y, (x + 1) * rows_y)
            adv_ref[at, cols] = moved
            for part in range(wide // (2 * LANES)):
                first = 2 * part * LANES
                both = folded(moved[:, first : first + LANES], moved[:, first + LANES : first + 2 * LANES], even, turned)
                to = pl.ds(pl.multiple_of(c * (wide // 2) + part * LANES, LANES), LANES)
                fold_ref[0, at, to], fold_ref[1, at, to] = both
        return carry

    lax.fori_loop(0, local_len // wide, chunk, 0)


def columns_body(wide, rows_x, one_ref, two_ref, far_ref, one_halo, two_halo, adv_in, fold_in, *rest):
    here_ref = place()
    adv_ref, fold_ref = rest[-2:]
    cells, local_len = adv_in.shape
    rows_y = cells // rows_x
    half = rows_y // 2
    masks = fold_masks(rows_x)

    def spread(parts, from_ref, to_ref, cols):
        at = iota((half, parts[0].shape[1]), 0)
        even = at % 2 == 0
        for first in range(0, rows_x, half):
            for upper in range(2):
                a, b = (part[first : first + half] for part in parts[2 * upper : 2 * upper + 2])
                b = pltpu.roll(b, 1, 0)
                pairs = jnp.where(even, a, b), jnp.where(even, b, a)
                place = upper * (half - 2)
                here = (at == place) | (at == place + 1)
                done = []
                for s in range(half):
                    start = (first + s) * rows_y + upper * half
                    rows = slice(start, start + half)
                    more = jnp.where(here, pltpu.roll(pairs[s % 2], (place - s) % half, 0), 0.0)
                    done.append((rows, from_ref[rows, cols] + more))
                for rows, value in done:
                    to_ref[rows, cols] = value

    def chunk(c, carry):
        cols = pl.ds(pl.multiple_of(c * wide, wide), wide)
        fold_cols = pl.ds(pl.multiple_of(c * (wide // 2), wide // 2), wide // 2)
        _, vy = velocity_parts(here_ref[0] * local_len + c * wide + iota((1, wide), 1))
        ay = time_step * vy
        by = 0.5 * jnp.abs(ay) * (1.0 - jnp.abs(ay))
        ahead = ay > 0

        def face(f0, f1, f2):
            return ay * f1 + by * minmod(f1 - f0, f2 - f1)

        low_far, low_near, high_near, high_far = beyond(here_ref, rows_x, one_halo, two_halo, cols)
        odd = here_ref[4] > 0
        one, two = one_ref[:rows_x, cols], two_ref[:rows_x, cols]
        low, high = jnp.where(odd, one, two), jnp.where(odd, two, one)
        one, two = far_ref[0, :, cols], far_ref[1, :, cols]
        second, last_but_one = jnp.where(odd, one, two), jnp.where(odd, two, one)
        before = face(low_far, low_near, low)
        first = face(low_near, low, second)
        last = face(last_but_one, high, high_near)
        after = face(high, high_near, high_far)
        parts = [
            jnp.where(ahead, before - first, first),
            jnp.where(ahead, first, 0.0),
            jnp.where(ahead, 0.0, -last),
            jnp.where(ahead, -last, last - after),
        ]
        spread(parts, adv_in, adv_ref, cols)
        both = []
        for part in parts:
            pairs = [folded(part[:, j : j + LANES], part[:, j + LANES : j + 2 * LANES], *masks) for j in range(0, wide, 2 * LANES)]
            both.append([jnp.concatenate(tiles, axis=1) for tiles in zip(*pairs)])
        for parity in range(2):
            spread([pair[parity] for pair in both], fold_in.at[parity], fold_ref.at[parity], fold_cols)
        return carry

    lax.fori_loop(0, local_len // wide, chunk, 0)


def transport(rows_x, field, xhalo, yhalos, entries):
    cells, local_len = field.shape
    wide = 4 * LANES
    return pl.pallas_call(
        functools.partial(transport_body, wide, rows_x, bool(yhalos)),
        in_specs=[WHOLE] * (2 + len(yhalos) + len(entries)),
        out_specs=[WHOLE] * 2,
        out_shape=[pltpu.VMEM(field.shape, jnp.float32), pltpu.VMEM((2, cells, local_len // 2), jnp.float32)],
        scratch_shapes=[pltpu.VMEM((rows_x, wide), jnp.float32)] * (4 if yhalos else 0),
        compiler_params=room(4),
        cost_estimate=SMALL,
        name="transport" if yhalos else "inner_transport",
    )(*map(in_vmem, (field, xhalo, *yhalos, *entries)))


def add_columns(rows_x, one, two, far, one_halo, two_halo, advected, fold, entries):
    wide = 4 * LANES
    return pl.pallas_call(
        functools.partial(columns_body, wide, rows_x),
        in_specs=[WHOLE] * (7 + len(entries)),
        out_specs=[WHOLE] * 2,
        out_shape=[pltpu.VMEM(advected.shape, jnp.float32), pltpu.VMEM(fold.shape, jnp.float32)],
        input_output_aliases={5: 0, 6: 1},
        compiler_params=room(4),
        cost_estimate=SMALL,
        name="add_columns",
    )(*map(in_vmem, (one, two, far, one_halo, two_halo, advected, fold, *entries)))


def split_into(value_ref, high, low):
    for parity in range(2):
        value = value_ref[parity]
        rounded = value.astype(jnp.bfloat16)
        high[parity] = rounded
        low[parity] = (value - rounded.astype(jnp.float32)).astype(jnp.bfloat16)


def product(high, low, hi_ref, lo_ref, source, parity, cols):
    dot = functools.partial(jnp.dot, preferred_element_type=jnp.float32)
    tile = hi_ref[source, parity, :, cols]
    return dot(high[parity], tile) + (dot(low[parity], tile) + dot(high[parity], lo_ref[source, parity, :, cols]))


def own_body(wide, fold_ref, hi_ref, lo_ref, adv_ref, density_ref, type_ref, inflow_ref, out_ref, keep_ref, high, low):
    here_ref = place()
    split_into(fold_ref, high, low)
    for j in range(fold_ref.shape[2] // wide):
        cols = slice(j * wide, (j + 1) * wide)
        for parity in range(2):
            out_ref[parity, :, cols] = product(high, low, hi_ref, lo_ref, 0, parity, cols)
    cells, local_len = adv_ref.shape
    rate = jnp.broadcast_to(collision_rate * density_ref[...], (cells, LANES))
    kind = jnp.broadcast_to(type_ref[...], (cells, LANES))
    wall, inlet = kind == 1, kind == 2
    for first in range(0, local_len, LANES):
        at = slice(first, first + LANES)
        vx, vy = velocity_parts(here_ref[0] * local_len + first + iota((1, LANES), 1))
        nu = 1.0 + (vx * vx + vy * vy) / 8.0
        kept = adv_ref[:, at] * (1.0 - rate * nu)
        keep_ref[:, at] = jnp.where(wall, 0.0, jnp.where(inlet, inflow_ref[:, at], kept))


def own_gain(fold, entries, advected, density, kind, inflow):
    _, cells, size = fold.shape
    return pl.pallas_call(
        functools.partial(own_body, 2 * LANES),
        in_specs=[WHOLE] * 7,
        out_specs=[WHOLE] * 2,
        out_shape=[pltpu.VMEM(fold.shape, jnp.float32), pltpu.VMEM(advected.shape, jnp.float32)],
        scratch_shapes=[pltpu.VMEM(fold.shape, jnp.bfloat16)] * 2,
        compiler_params=room(8),
        cost_estimate=SMALL,
        name="own_gain",
    )(*map(in_vmem, (fold, *entries, advected, density, kind)), inflow)


def collide_body(
    wide, rows_x, last, fold_ref, hi_ref, lo_ref, part_ref, keep_ref, density_ref, type_ref, *rest
):
    here_ref = place()
    if last:
        out_ref, high, low, field, sems = rest
    else:
        field, *edge_refs, high, low = rest
    cells, local_len = keep_ref.shape
    split_into(fold_ref, high, low)
    even_slot, turned = fold_masks(cells)
    gas = (type_ref[...] != 1) & (type_ref[...] != 2)
    gain_rate = jnp.where(gas, collision_rate * ENTRY_SCALE * density_ref[...], 0.0)
    gain_rate = jnp.broadcast_to(gain_rate, (cells, LANES))
    copies = []
    for j in range(local_len // (2 * wide)):
        cols = slice(j * wide, (j + 1) * wide)
        even, odd = (part_ref[p, :, cols] + product(high, low, hi_ref, lo_ref, 1, p, cols) for p in range(2))
        lower = even + odd
        upper = even - odd
        for part in range(wide // LANES):
            group = slice(part * LANES, (part + 1) * LANES)
            for side, gain in enumerate(unfolded(lower[:, group], upper[:, group], even_slot, turned)):
                first = 2 * (j * wide + part * LANES) + side * LANES
                at = slice(first, first + LANES)
                field[:, at] = keep_ref[:, at] + gain_rate * gain
            span = slice(first - LANES, first + LANES)
            if last:
                i = first // (2 * LANES)
                copy = pltpu.make_async_copy(field.at[:, span], out_ref.at[:, span], sems.at[i])
                copy.start()
                copies.append(copy)
            else:
                write_edges(here_ref, rows_x, field, span, edge_refs)
    for copy in copies:
        copy.wait()


def collide(rows_x, fold, entries, part, kept, density, kind, last):
    _, cells, size = fold.shape
    local_len = kept.shape[1]
    wide = 2 * LANES
    halves = [pltpu.VMEM(fold.shape, jnp.bfloat16)] * 2
    if last:
        out_specs = pl.BlockSpec(memory_space=pl.ANY)
        out_shape = jax.ShapeDtypeStruct(kept.shape, jnp.float32)
        scratch = halves + [pltpu.VMEM(kept.shape, jnp.float32), pltpu.SemaphoreType.DMA((size // LANES,))]
    else:
        out_specs = [WHOLE] * 5
        out_shape = [pltpu.VMEM(kept.shape, jnp.float32)] + edge_shapes(rows_x, cells // rows_x, local_len)
        scratch = halves
    return pl.pallas_call(
        functools.partial(collide_body, wide, rows_x, last),
        in_specs=[WHOLE] * 7,
        out_specs=out_specs,
        out_shape=out_shape,
        scratch_shapes=scratch,
        compiler_params=room(12),
        cost_estimate=SMALL,
        name="collide",
    )(in_vmem(fold), in_vmem(entries[0]), in_vmem(entries[1]), in_vmem(part), in_vmem(kept), density, kind)


def swapped(block, axis, first):
    pairs = [(i, i + 1) for i in range(first, lax.axis_size(axis) - 1, 2)]
    return lax.ppermute(block, axis, [pair for i, j in pairs for pair in ((i, j), (j, i))])


def per_device(distribution, density, cell_type, inflow):
    rows_x, rows_y, local_len = distribution.shape
    cells = rows_x * rows_y
    vert = lax.axis_index("vert")
    verts = lax.axis_size("vert")
    at_x = lax.axis_index("gx")
    size_x = lax.axis_size("gx")
    assert size_x == 2 and verts == 2
    column_density = density.reshape(cells, 1)
    column_type = cell_type.reshape(cells, 1)
    row_inflow = inflow.reshape(1, local_len)
    swap = [(0, 1), (1, 0)]
    field, one, two, send_x, far = stage(rows_x, distribution.reshape(cells, local_len))
    entries = None
    for step in range(STEPS):
        last = step == STEPS - 1
        one_halo = swapped(one, "gy", 0)
        two_halo = swapped(two, "gy", 1)
        xhalo = lax.ppermute(send_x, "gx", swap)
        if entries is None:
            entries = make_entries(local_len // NVX, verts, [column_density, column_type])
        if step == 0:
            advected, fold = transport(rows_x, field, xhalo, [one_halo, two_halo, one, two], entries)
        else:
            advected, fold = transport(rows_x, field, xhalo, [], entries)
            advected, fold = add_columns(rows_x, one, two, far, one_halo, two_halo, advected, fold, entries)
        other = lax.ppermute(fold, "vert", swap)
        part, kept = own_gain(fold, entries, advected, column_density, column_type, row_inflow)
        out = collide(rows_x, other, entries, part, kept, column_density, column_type, last)
        if not last:
            field, one, two, send_x, far = out
    return out.reshape(rows_x, rows_y, local_len)


def solution(mesh):
    placed = (P("gx", "gy", "vert"), P("gx", "gy"), P("gx", "gy"), P("vert"))
    return jax.shard_map(
        per_device, mesh=mesh, in_specs=placed, out_specs=P("gx", "gy", "vert"), check_vma=False
    )
```

```python
import functools
import math

import jax
import jax.numpy as jnp
from jax import lax
from jax.experimental import pallas as pl
from jax.experimental.pallas import tpu as pltpu
from jax.sharding import PartitionSpec as P

NVX = 64
STEPS = 2
HALF = NVX // 2
LANES = 128
GROUP = LANES // HALF

vel_max = 4.0
time_step = 0.1
grad_scale = 2.5
collision_rate = 0.2
spacing = 2.0 * vel_max / NVX
middle = 0.5 * (NVX - 1)

MIB = 1024 * 1024
WHOLE = pl.BlockSpec(memory_space=pltpu.VMEM)

EXPONENT = 0.125 * math.log2(math.e)
ENTRY_SCALE = grad_scale * spacing * spacing * math.sqrt(EXPONENT)


SMALL = pl.CostEstimate(flops=1, bytes_accessed=1, transcendentals=0)


def place():
    at_x = lax.axis_index("gx")
    more = (at_x > 0, at_x < lax.axis_size("gx") - 1)
    return [lax.axis_index("vert"), lax.axis_size("vert"), *(m.astype(jnp.int32) for m in more), lax.axis_index("gy") % 2]


def room(mib):
    return pltpu.CompilerParams(vmem_limit_bytes=mib * MIB)


def in_vmem(value):
    return pltpu.with_memory_space_constraint(value, pltpu.VMEM)


def velocity_parts(index):
    row_portion = (index // NVX).astype(jnp.float32)
    col_part = (index % NVX).astype(jnp.float32)
    vel_x = (row_portion - middle) * spacing
    vel_y = (col_part - middle) * spacing
    return (vel_x, vel_y)


def iota(shape, dim):
    return lax.broadcasted_iota(jnp.int32, shape, dim)


def slot_order(slot):
    return lax.rem(slot, 2) * 2 + lax.div(slot, 2)


def entries_body(local, sources, *rest):
    here_ref = place()
    hi_ref, lo_ref, energy_ref, gauss_ref = rest[-4:]
    me = here_ref[0]
    groups = local // GROUP
    rows = 8
    lane = iota((1, LANES), 1)
    slot = slot_order(lane // HALF)
    vy = ((lane % HALF).astype(jnp.float32) - middle) * spacing

    def one(index, carry):
        source = lax.div(index, GROUP)
        r = lax.rem(index, GROUP)
        first = lax.rem(me + source, here_ref[1]) * local
        pair, lanes = iota((groups * groups, LANES), 0), iota((groups * groups, LANES), 1)
        out_x = ((me * local + pair // groups * GROUP + slot_order(lanes // HALF)).astype(jnp.float32) - middle) * spacing
        out_y = ((lanes % HALF).astype(jnp.float32) - middle) * spacing
        in_x = ((first + pair % groups * GROUP + r).astype(jnp.float32) - middle) * spacing
        out_sq, in_sq = out_x * out_x + out_y * out_y, in_x * in_x
        energy_ref[...] = EXPONENT * (out_sq - in_sq)
        gauss_ref[...] = jnp.exp((out_sq + in_sq) * -0.25) * (0.5 / EXPONENT)
        for part in range(HALF // rows):
            wy = ((iota((rows, LANES), 0) + part * rows).astype(jnp.float32) - middle) * spacing
            in_y_sq = EXPONENT * wy * wy
            in_y_gauss = jnp.exp(wy * wy * -0.25)
            dy_same = EXPONENT * ((vy - wy) ** 2 + spacing * spacing)
            dy_flip = EXPONENT * ((vy + wy) ** 2 + spacing * spacing)
            for m in range(1 - groups, groups):
                apart = (me * local - first + m * GROUP - r + slot).astype(jnp.float32) * spacing
                dx_sq = EXPONENT * apart * apart
                same_sq, flip_sq = dx_sq + dy_same, dx_sq + dy_flip
                same_inv, flip_inv = lax.rsqrt(same_sq), lax.rsqrt(flip_sq)
                same_inv_sq, flip_inv_sq = same_inv * same_inv, flip_inv * flip_inv
                same_top, flip_top = jnp.log2(same_inv) - same_sq, jnp.log2(flip_inv) - flip_sq
                same_r, flip_r = same_sq * same_inv, flip_sq * flip_inv
                sum_r, gap_r = same_r + flip_r, same_r - flip_r
                for g in range(max(0, m), min(groups, groups + m)):
                    k = g - m
                    at = g * groups + k
                    energy = energy_ref[at : at + 1, :] - in_y_sq
                    energy_sq = energy * energy
                    gauss = gauss_ref[at : at + 1, :] * in_y_gauss
                    same = jnp.exp2(same_top - energy_sq * same_inv_sq)
                    flip = jnp.exp2(flip_top - energy_sq * flip_inv_sq)
                    to = (k * GROUP + slot_order(r)) * HALF + part * rows
                    to = pl.ds(pl.multiple_of(to, rows), rows)
                    cols = slice(g * LANES, (g + 1) * LANES)
                    values = ((same + flip) - gauss * sum_r, (same - flip) - gauss * gap_r)
                    for parity, value in enumerate(values):
                        high = value.astype(jnp.bfloat16)
                        hi_ref[source, parity, to, cols] = high
                        lo_ref[source, parity, to, cols] = (value - high.astype(jnp.float32)).astype(jnp.bfloat16)
        return carry

    lax.fori_loop(0, sources * GROUP, one, 0)


def make_entries(local, sources, ahead_of):
    size = local * HALF
    shape = pltpu.VMEM((sources, 2, size, size), jnp.bfloat16)
    return pl.pallas_call(
        functools.partial(entries_body, local, sources),
        in_specs=[WHOLE] * len(ahead_of),
        out_specs=[WHOLE, WHOLE],
        out_shape=[shape, shape],
        scratch_shapes=[pltpu.VMEM(((local // GROUP) ** 2, LANES), jnp.float32)] * 2,
        compiler_params=room(8),
        cost_estimate=SMALL,
        name="kernel_entries",
    )(*map(in_vmem, ahead_of))


def pack_far(far, ahead, low_half):
    count = far.shape[0] // 2
    if ahead:
        return jnp.where(low_half, pltpu.roll(far[count:], LANES - HALF, 1), far[:count])
    return jnp.where(low_half, far[:count], pltpu.roll(far[count:], HALF, 1))


def unpack_far(packed, ahead):
    shift = HALF if ahead else LANES - HALF
    parts = [packed[:, i : i + LANES] for i in range(0, packed.shape[1], LANES)]
    turned = jnp.concatenate([pltpu.roll(p, shift, 1) for p in parts], axis=1)
    return jnp.concatenate([packed, turned], axis=0)


def outer_columns(field, rows_x, span, upper):
    rows_y = field.shape[0] // rows_x
    half = rows_y // 2
    at = iota((half, span.stop - span.start), 0)
    shift = 1 - half if upper else 0
    nears, fars = [], []
    for first in range(0, rows_x, half):
        near = far = None
        for s in range(half):
            start = (first + s) * rows_y + (half if upper else 0)
            turned = pltpu.roll(field[start : start + half, span], (s + shift) % half, 0)
            near = turned if near is None else jnp.where(at == s, turned, near)
            beside = (s - 1 if upper else s + 1) % half
            far = turned if far is None else jnp.where(at == beside, turned, far)
        nears.append(near)
        fars.append(pltpu.roll(far, 1 if upper else half - 1, 0))
    return jnp.concatenate(nears, axis=0), jnp.concatenate(fars, axis=0)


def write_edges(here_ref, rows_x, field, span, edge_refs):
    one_ref, two_ref, xsend_ref, far_ref = edge_refs
    rows_y = field.shape[0] // rows_x
    to_next = here_ref[3] > 0
    for layer in range(2):
        low_row, high_row = (field[x * rows_y : (x + 1) * rows_y, span] for x in (layer, rows_x - 2 + layer))
        xsend_ref[layer, :, span] = jnp.where(to_next, high_row, low_row)
    odd = here_ref[4] > 0
    low_near, low_far = outer_columns(field, rows_x, span, False)
    high_near, high_far = outer_columns(field, rows_x, span, True)
    one_ref[:rows_x, span] = jnp.where(odd, low_near, high_near)
    two_ref[:rows_x, span] = jnp.where(odd, high_near, low_near)
    far_ref[0, :, span] = jnp.where(odd, low_far, high_far)
    far_ref[1, :, span] = jnp.where(odd, high_far, low_far)
    low_half = iota((rows_x // 2, LANES), 1) % NVX < HALF
    for i in range(0, span.stop - span.start, LANES):
        at = slice(span.start + i, span.start + i + LANES)
        low = pack_far(low_far[:, i : i + LANES], False, low_half)
        high = pack_far(high_far[:, i : i + LANES], True, low_half)
        one_ref[rows_x:, at] = jnp.where(odd, low, high)
        two_ref[rows_x:, at] = jnp.where(odd, high, low)


def edge_shapes(rows_x, rows_y, local_len):
    edge_y = pltpu.VMEM((rows_x + rows_x // 2, local_len), jnp.float32)
    layers_x = pltpu.VMEM((2, rows_y, local_len), jnp.float32)
    return [edge_y, edge_y, layers_x, pltpu.VMEM((2, rows_x, local_len), jnp.float32)]


def stage_body(wide, rows_x, from_ref, field, *rest):
    here_ref = place()
    *edge_refs, sems = rest
    spans = [slice(i, i + wide) for i in range(0, field.shape[1], wide)]
    copies = [pltpu.make_async_copy(from_ref.at[:, s], field.at[:, s], sems.at[i]) for i, s in enumerate(spans)]
    for copy in copies:
        copy.start()
    for copy, span in zip(copies, spans):
        copy.wait()
        write_edges(here_ref, rows_x, field, span, edge_refs)


def stage(rows_x, field):
    cells, local_len = field.shape
    wide = local_len // 4
    return pl.pallas_call(
        functools.partial(stage_body, wide, rows_x),
        in_specs=[pl.BlockSpec(memory_space=pltpu.HBM)],
        out_specs=[WHOLE] * 5,
        out_shape=[pltpu.VMEM(field.shape, jnp.float32)] + edge_shapes(rows_x, cells // rows_x, local_len),
        scratch_shapes=[pltpu.SemaphoreType.DMA((4,))],
        compiler_params=room(4),
        name="stage",
    )(pltpu.with_memory_space_constraint(field, pltpu.HBM))


def beyond(here_ref, rows_x, one_ref, two_ref, cols):
    odd = here_ref[4] > 0
    one, two = one_ref[:, cols], two_ref[:, cols]
    low, high = jnp.where(odd, one, two), jnp.where(odd, two, one)
    return unpack_far(low[rows_x:], True), low[:rows_x], high[:rows_x], unpack_far(high[rows_x:], False)


def minmod(a, b):
    return jnp.maximum(jnp.minimum(a, b), 0.0) + jnp.minimum(jnp.maximum(a, b), 0.0)


def fold_masks(rows):
    lane = iota((rows, LANES), 1)
    slot = lane // HALF
    even = slot % 2 == 0
    turned = jnp.where(even, 2 - slot, slot) * HALF + (HALF - 1) - lane % HALF
    return even, turned


def folded(a, b, even, turned):
    near = jnp.where(even, a, b)
    far = pltpu.roll(jnp.where(even, b, a), HALF, 1)
    lower = jnp.where(even, near, far)
    upper = jnp.take_along_axis(jnp.where(even, far, near), turned, axis=1)
    return lower + upper, lower - upper


def unfolded(lower, upper, even, turned):
    upper = jnp.take_along_axis(upper, turned, axis=1)
    near = jnp.where(even, lower, upper)
    far = pltpu.roll(jnp.where(even, upper, lower), LANES - HALF, 1)
    return jnp.where(even, near, far), jnp.where(even, far, near)


def transport_body(wide, rows_x, whole, field_ref, xhalo_ref, *rest):
    here_ref = place()
    if whole:
        one_halo, two_halo, one_ref, two_ref = rest[:4]
        adv_ref, fold_ref, low_edge, high_edge, low_near, high_near = rest[-6:]
    else:
        adv_ref, fold_ref = rest[-2:]
    cells, local_len = field_ref.shape
    rows_y = cells // rows_x
    has_low = here_ref[2] > 0
    has_high = here_ref[3] > 0
    at_y = iota((rows_y, wide), 0)
    first_y = at_y == 0
    last_y = at_y == rows_y - 1
    even, turned = fold_masks(rows_y)

    def chunk(c, carry):
        cols = pl.ds(pl.multiple_of(c * wide, wide), wide)
        vx, vy = velocity_parts(here_ref[0] * local_len + c * wide + iota((1, wide), 1))
        ax = time_step * vx
        ay = time_step * vy
        bx = 0.5 * jnp.abs(ax) * (1.0 - jnp.abs(ax))
        by = 0.5 * jnp.abs(ay) * (1.0 - jnp.abs(ay))
        ahead_x = ax > 0
        ahead_y = ay > 0

        def face_y(f0, f1, f2):
            return ay * f1 + by * minmod(f1 - f0, f2 - f1)

        if whole:
            low_far, low_near[...], high_near[...], high_far = beyond(here_ref, rows_x, one_halo, two_halo, cols)
            odd = here_ref[4] > 0
            one, two = one_ref[:rows_x, cols], two_ref[:rows_x, cols]
            low_edge[...] = face_y(low_far, low_near[...], jnp.where(odd, one, two))
            high_edge[...] = face_y(jnp.where(odd, two, one), high_near[...], high_far)

        def row(i):
            if i < 0:
                return jnp.where(has_low, xhalo_ref[i + 2, :, cols], 0.0)
            if i >= rows_x:
                return jnp.where(has_high, xhalo_ref[i - rows_x, :, cols], 0.0)
            return field_ref[i * rows_y : (i + 1) * rows_y, cols]

        near = [row(-2), row(-1), row(0)]
        low, high = near[1] - near[0], near[2] - near[1]
        face = [ax * near[1] + bx * minmod(low, high)]
        for i in range(rows_x + 1):
            near = [near[1], near[2], row(i + 1)]
            low, high = high, near[2] - near[1]
            face.append(ax * near[1] + bx * minmod(low, high))
            if i == 0:
                continue
            x = i - 1
            here = near[0]
            row_term = jnp.where(ahead_x, face[x + 1] - face[x], face[x + 2] - face[x + 1])
            if whole:
                below = jnp.where(first_y, low_near[x : x + 1], pltpu.roll(here, 1, 0))
                above = jnp.where(last_y, high_near[x : x + 1], pltpu.roll(here, rows_y - 1, 0))
                mine = face_y(below, here, above)
                mine_below = jnp.where(first_y, low_edge[x : x + 1], pltpu.roll(mine, 1, 0))
                mine_above = jnp.where(last_y, high_edge[x : x + 1], pltpu.roll(mine, rows_y - 1, 0))
                col_term = jnp.where(ahead_y, mine - mine_below, mine_above - mine)
            else:
                rise = here - pltpu.roll(here, 1, 0)
                mine = ay * here + by * minmod(rise, pltpu.roll(rise, rows_y - 1, 0))
                mine = jnp.where(first_y | last_y, 0.0, mine)
                step = mine - pltpu.roll(mine, 1, 0)
                col_term = jnp.where(ahead_y, step, pltpu.roll(step, rows_y - 1, 0))
            moved = here - row_term - col_term
            at = slice(x * rows_y, (x + 1) * rows_y)
            adv_ref[at, cols] = moved
            for part in range(wide // (2 * LANES)):
                first = 2 * part * LANES
                both = folded(moved[:, first : first + LANES], moved[:, first + LANES : first + 2 * LANES], even, turned)
                to = pl.ds(pl.multiple_of(c * (wide // 2) + part * LANES, LANES), LANES)
                fold_ref[0, at, to], fold_ref[1, at, to] = both
        return carry

    lax.fori_loop(0, local_len // wide, chunk, 0)


def columns_body(wide, rows_x, one_ref, two_ref, far_ref, one_halo, two_halo, adv_in, fold_in, *rest):
    here_ref = place()
    adv_ref, fold_ref = rest[-2:]
    cells, local_len = adv_in.shape
    rows_y = cells // rows_x
    half = rows_y // 2
    masks = fold_masks(rows_x)

    def spread(parts, from_ref, to_ref, cols):
        at = iota((half, parts[0].shape[1]), 0)
        even = at % 2 == 0
        for first in range(0, rows_x, half):
            for upper in range(2):
                a, b = (part[first : first + half] for part in parts[2 * upper : 2 * upper + 2])
                b = pltpu.roll(b, 1, 0)
                pairs = jnp.where(even, a, b), jnp.where(even, b, a)
                place = upper * (half - 2)
                here = (at == place) | (at == place + 1)
                done = []
                for s in range(half):
                    start = (first + s) * rows_y + upper * half
                    rows = slice(start, start + half)
                    more = jnp.where(here, pltpu.roll(pairs[s % 2], (place - s) % half, 0), 0.0)
                    done.append((rows, from_ref[rows, cols] + more))
                for rows, value in done:
                    to_ref[rows, cols] = value

    def chunk(c, carry):
        cols = pl.ds(pl.multiple_of(c * wide, wide), wide)
        fold_cols = pl.ds(pl.multiple_of(c * (wide // 2), wide // 2), wide // 2)
        _, vy = velocity_parts(here_ref[0] * local_len + c * wide + iota((1, wide), 1))
        ay = time_step * vy
        by = 0.5 * jnp.abs(ay) * (1.0 - jnp.abs(ay))
        ahead = ay > 0

        def face(f0, f1, f2):
            return ay * f1 + by * minmod(f1 - f0, f2 - f1)

        low_far, low_near, high_near, high_far = beyond(here_ref, rows_x, one_halo, two_halo, cols)
        odd = here_ref[4] > 0
        one, two = one_ref[:rows_x, cols], two_ref[:rows_x, cols]
        low, high = jnp.where(odd, one, two), jnp.where(odd, two, one)
        one, two = far_ref[0, :, cols], far_ref[1, :, cols]
        second, last_but_one = jnp.where(odd, one, two), jnp.where(odd, two, one)
        before = face(low_far, low_near, low)
        first = face(low_near, low, second)
        last = face(last_but_one, high, high_near)
        after = face(high, high_near, high_far)
        parts = [
            jnp.where(ahead, before - first, first),
            jnp.where(ahead, first, 0.0),
            jnp.where(ahead, 0.0, -last),
            jnp.where(ahead, -last, last - after),
        ]
        spread(parts, adv_in, adv_ref, cols)
        both = []
        for part in parts:
            pairs = [folded(part[:, j : j + LANES], part[:, j + LANES : j + 2 * LANES], *masks) for j in range(0, wide, 2 * LANES)]
            both.append([jnp.concatenate(tiles, axis=1) for tiles in zip(*pairs)])
        for parity in range(2):
            spread([pair[parity] for pair in both], fold_in.at[parity], fold_ref.at[parity], fold_cols)
        return carry

    lax.fori_loop(0, local_len // wide, chunk, 0)


def transport(rows_x, field, xhalo, yhalos, entries):
    cells, local_len = field.shape
    wide = 4 * LANES
    return pl.pallas_call(
        functools.partial(transport_body, wide, rows_x, bool(yhalos)),
        in_specs=[WHOLE] * (2 + len(yhalos) + len(entries)),
        out_specs=[WHOLE] * 2,
        out_shape=[pltpu.VMEM(field.shape, jnp.float32), pltpu.VMEM((2, cells, local_len // 2), jnp.float32)],
        scratch_shapes=[pltpu.VMEM((rows_x, wide), jnp.float32)] * (4 if yhalos else 0),
        compiler_params=room(4),
        cost_estimate=SMALL,
        name="transport" if yhalos else "inner_transport",
    )(*map(in_vmem, (field, xhalo, *yhalos, *entries)))


def add_columns(rows_x, one, two, far, one_halo, two_halo, advected, fold, entries):
    wide = 4 * LANES
    return pl.pallas_call(
        functools.partial(columns_body, wide, rows_x),
        in_specs=[WHOLE] * (7 + len(entries)),
        out_specs=[WHOLE] * 2,
        out_shape=[pltpu.VMEM(advected.shape, jnp.float32), pltpu.VMEM(fold.shape, jnp.float32)],
        input_output_aliases={5: 0, 6: 1},
        compiler_params=room(4),
        cost_estimate=SMALL,
        name="add_columns",
    )(*map(in_vmem, (one, two, far, one_halo, two_halo, advected, fold, *entries)))


def split_into(value_ref, high, low):
    for parity in range(2):
        value = value_ref[parity]
        rounded = value.astype(jnp.bfloat16)
        high[parity] = rounded
        low[parity] = (value - rounded.astype(jnp.float32)).astype(jnp.bfloat16)


def product(high, low, hi_ref, lo_ref, source, parity, cols):
    dot = functools.partial(jnp.dot, preferred_element_type=jnp.float32)
    tile = hi_ref[source, parity, :, cols]
    return dot(high[parity], tile) + (dot(low[parity], tile) + dot(high[parity], lo_ref[source, parity, :, cols]))


def own_body(wide, fold_ref, hi_ref, lo_ref, adv_ref, density_ref, type_ref, inflow_ref, out_ref, keep_ref, high, low):
    here_ref = place()
    split_into(fold_ref, high, low)
    for j in range(fold_ref.shape[2] // wide):
        cols = slice(j * wide, (j + 1) * wide)
        for parity in range(2):
            out_ref[parity, :, cols] = product(high, low, hi_ref, lo_ref, 0, parity, cols)
    cells, local_len = adv_ref.shape
    rate = jnp.broadcast_to(collision_rate * density_ref[...], (cells, LANES))
    kind = jnp.broadcast_to(type_ref[...], (cells, LANES))
    wall, inlet = kind == 1, kind == 2
    for first in range(0, local_len, LANES):
        at = slice(first, first + LANES)
        vx, vy = velocity_parts(here_ref[0] * local_len + first + iota((1, LANES), 1))
        nu = 1.0 + (vx * vx + vy * vy) / 8.0
        kept = adv_ref[:, at] * (1.0 - rate * nu)
        keep_ref[:, at] = jnp.where(wall, 0.0, jnp.where(inlet, inflow_ref[:, at], kept))


def own_gain(fold, entries, advected, density, kind, inflow):
    _, cells, size = fold.shape
    return pl.pallas_call(
        functools.partial(own_body, 4 * LANES),
        in_specs=[WHOLE] * 7,
        out_specs=[WHOLE] * 2,
        out_shape=[pltpu.VMEM(fold.shape, jnp.float32), pltpu.VMEM(advected.shape, jnp.float32)],
        scratch_shapes=[pltpu.VMEM(fold.shape, jnp.bfloat16)] * 2,
        compiler_params=room(8),
        cost_estimate=SMALL,
        name="own_gain",
    )(*map(in_vmem, (fold, *entries, advected, density, kind)), inflow)


def collide_body(
    wide, rows_x, last, fold_ref, hi_ref, lo_ref, part_ref, keep_ref, density_ref, type_ref, *rest
):
    here_ref = place()
    if last:
        out_ref, high, low, field, sems = rest
    else:
        field, *edge_refs, high, low = rest
    cells, local_len = keep_ref.shape
    split_into(fold_ref, high, low)
    even_slot, turned = fold_masks(cells)
    gas = (type_ref[...] != 1) & (type_ref[...] != 2)
    gain_rate = jnp.where(gas, collision_rate * ENTRY_SCALE * density_ref[...], 0.0)
    gain_rate = jnp.broadcast_to(gain_rate, (cells, LANES))
    copies = []
    for j in range(local_len // (2 * wide)):
        cols = slice(j * wide, (j + 1) * wide)
        even, odd = (part_ref[p, :, cols] + product(high, low, hi_ref, lo_ref, 1, p, cols) for p in range(2))
        lower = even + odd
        upper = even - odd
        for part in range(wide // LANES):
            group = slice(part * LANES, (part + 1) * LANES)
            for side, gain in enumerate(unfolded(lower[:, group], upper[:, group], even_slot, turned)):
                first = 2 * (j * wide + part * LANES) + side * LANES
                at = slice(first, first + LANES)
                field[:, at] = keep_ref[:, at] + gain_rate * gain
            span = slice(first - LANES, first + LANES)
            if last:
                i = first // (2 * LANES)
                copy = pltpu.make_async_copy(field.at[:, span], out_ref.at[:, span], sems.at[i])
                copy.start()
                copies.append(copy)
            else:
                write_edges(here_ref, rows_x, field, span, edge_refs)
    for copy in copies:
        copy.wait()


def collide(rows_x, fold, entries, part, kept, density, kind, last):
    _, cells, size = fold.shape
    local_len = kept.shape[1]
    wide = 4 * LANES
    halves = [pltpu.VMEM(fold.shape, jnp.bfloat16)] * 2
    if last:
        out_specs = pl.BlockSpec(memory_space=pl.ANY)
        out_shape = jax.ShapeDtypeStruct(kept.shape, jnp.float32)
        scratch = halves + [pltpu.VMEM(kept.shape, jnp.float32), pltpu.SemaphoreType.DMA((size // LANES,))]
    else:
        out_specs = [WHOLE] * 5
        out_shape = [pltpu.VMEM(kept.shape, jnp.float32)] + edge_shapes(rows_x, cells // rows_x, local_len)
        scratch = halves
    return pl.pallas_call(
        functools.partial(collide_body, wide, rows_x, last),
        in_specs=[WHOLE] * 7,
        out_specs=out_specs,
        out_shape=out_shape,
        scratch_shapes=scratch,
        compiler_params=room(12),
        cost_estimate=SMALL,
        name="collide",
    )(in_vmem(fold), in_vmem(entries[0]), in_vmem(entries[1]), in_vmem(part), in_vmem(kept), density, kind)


def swapped(block, axis, first):
    pairs = [(i, i + 1) for i in range(first, lax.axis_size(axis) - 1, 2)]
    return lax.ppermute(block, axis, [pair for i, j in pairs for pair in ((i, j), (j, i))])


def per_device(distribution, density, cell_type, inflow):
    rows_x, rows_y, local_len = distribution.shape
    cells = rows_x * rows_y
    vert = lax.axis_index("vert")
    verts = lax.axis_size("vert")
    at_x = lax.axis_index("gx")
    size_x = lax.axis_size("gx")
    assert size_x == 2 and verts == 2
    column_density = density.reshape(cells, 1)
    column_type = cell_type.reshape(cells, 1)
    row_inflow = inflow.reshape(1, local_len)
    swap = [(0, 1), (1, 0)]
    field, one, two, send_x, far = stage(rows_x, distribution.reshape(cells, local_len))
    entries = None
    for step in range(STEPS):
        last = step == STEPS - 1
        one_halo = swapped(one, "gy", 0)
        two_halo = swapped(two, "gy", 1)
        xhalo = lax.ppermute(send_x, "gx", swap)
        if entries is None:
            entries = make_entries(local_len // NVX, verts, [column_density, column_type])
        if step == 0:
            advected, fold = transport(rows_x, field, xhalo, [one_halo, two_halo, one, two], entries)
        else:
            advected, fold = transport(rows_x, field, xhalo, [], entries)
            advected, fold = add_columns(rows_x, one, two, far, one_halo, two_halo, advected, fold, entries)
        other = lax.ppermute(fold, "vert", swap)
        part, kept = own_gain(fold, entries, advected, column_density, column_type, row_inflow)
        out = collide(rows_x, other, entries, part, kept, column_density, column_type, last)
        if not last:
            field, one, two, send_x, far = out
    return out.reshape(rows_x, rows_y, local_len)


def solution(mesh):
    placed = (P("gx", "gy", "vert"), P("gx", "gy"), P("gx", "gy"), P("vert"))
    return jax.shard_map(
        per_device, mesh=mesh, in_specs=placed, out_specs=P("gx", "gy", "vert"), check_vma=False
    )
```
